32 devices in a mesh: seq: 4 (over x, core), head: 8 (over z, y).
Axes of the slice: x: 2, y: 2, z: 4, core: 2. Of those that a mesh axis runs over, the one named last changes fastest.
Arguments:
- x_rows: bfloat16 [20480, 3072], P('seq', 'head'), may hold values from -16 to 16
- z_rows: bfloat16 [20480, 3072], P('seq', 'head'), may hold values from -6 to 6
- b_rows: bfloat16 [20480, 128], P('seq', 'head'), may hold values from -6 to 6
- c_rows: bfloat16 [20480, 128], P('seq', 'head'), may hold values from -0.5 to 0.5
- step_raw: float32 [20480, 48], P('seq', 'head'), may hold values from -4 to 4
- conv_x: bfloat16 [4, 3072], P(None, 'head'), may hold values from -3 to 3
- conv_b: bfloat16 [4, 128], P(None, 'head'), may hold values from -3 to 3
- conv_c: bfloat16 [4, 128], P(None, 'head'), may hold values from -3 to 3
- decay_rate: float32 [48], P('head'), may hold values from 0 to 1, as said below
- norm_gain: float32 [3072], P('head'), may hold values from 0.5 to 1.5
Outputs:
- normed: bfloat16 [20480, 3072], P('seq', 'head')
The draws below stay inside these ranges and needn't reach their ends.
Inputs may be any that keep to these rules, and one draw needn't show every extreme that they name: `decay_rate`: positive rates.
All inputs are finite; a program needn't handle non-finite values.
Results may differ from the reference program's by a relative error of at most 0.011.
Values may be sent and summed in bfloat16 or wider, within the bound.
No kernel may reach another device: no remote copies, remote signals or barrier semaphores. Data moves between devices by JAX's collectives and lax.ppermute only.
A program may use at most 128 MiB of HBM per device.

```python
import jax
import jax.numpy as jnp
from jax import lax

HEAD_SIZE = 64
STATE = 128
CONV = 4
GROUP = 256
HEADS = 48
TOKENS = 20480


def draw_x_rows(key, part):
    key = jax.random.fold_in(key, 11)
    first = jax.random.fold_in(key, 0)
    columns = HEADS * HEAD_SIZE
    heads = (jnp.arange(columns) // HEAD_SIZE).astype(jnp.float32)
    rising = jnp.exp(jnp.log(3.0) * heads / max(HEADS - 1, 1))
    base = jnp.clip(jax.random.normal(first, (TOKENS, columns), jnp.float32), -4.0, 4.0)
    return (base * rising[None, :]).astype(jnp.bfloat16)


def draw_step_raw(key, part):
    key = jax.random.fold_in(key, 23)
    first, second = jax.random.split(key)
    block = max(TOKENS // 16, 1)
    offsets = jax.random.uniform(second, (TOKENS // block + 1, HEADS), jnp.float32, -1.0, 1.0)
    shift = offsets[jnp.arange(TOKENS) // block]
    noise = jnp.clip(0.7 * jax.random.normal(first, (TOKENS, HEADS), jnp.float32), -2.5, 2.5)
    return noise + shift


def draw_decay_rate(key, part):
    key = jax.random.fold_in(key, 37)
    first, second, third = jax.random.split(key, 3)
    pick = jax.random.uniform(first, (HEADS,), jnp.float32)
    slow = jnp.exp(jax.random.uniform(second, (HEADS,), jnp.float32, 1.5, 3.0)) / TOKENS
    fast = jnp.exp(jax.random.uniform(third, (HEADS,), jnp.float32, -3.69, -3.1))
    share = 0.55
    return jnp.where(pick < share, slow, fast)


def block_scale(key, shape, shards, smallest, top_value):
    loudness = 1.0
    for dim, parts in shards:
        draws = jax.random.uniform(jax.random.fold_in(jax.random.fold_in(key, 6), dim), (parts,), jnp.float32, smallest / len(shards), top_value / len(shards))
        loudness = loudness * jnp.repeat(jnp.exp(draws), shape[dim] // parts).reshape((-1,) + (1,) * (len(shape) - 1 - dim))
    return loudness


def normal_values(key, extent, spread, limit, cuts=(), kind=jnp.bfloat16):
    factor_of = block_scale(key, extent, cuts, -0.22, 0.18) if cuts else 1.0
    values = jax.random.normal(key, extent, jnp.float32) * spread * factor_of
    return jnp.minimum(jnp.maximum(values, -limit), limit).astype(kind)


def setup_inputs(seed: int = 0) -> dict:
    keys = jax.random.split(jax.random.key(seed), 11)
    return {
        "x_rows": draw_x_rows(jax.random.fold_in(keys[10], 71), 0),
        "z_rows": normal_values(keys[1], (TOKENS, HEADS * HEAD_SIZE), 1.0, 6.0, ((0, 4), (1, 8))),
        "b_rows": normal_values(keys[2], (TOKENS, STATE), 1.0, 6.0, ((0, 4), (1, 8))),
        "c_rows": normal_values(keys[3], (TOKENS, STATE), STATE ** -0.5, 0.5, ((0, 4), (1, 8))),
        "step_raw": draw_step_raw(jax.random.fold_in(keys[10], 71), 0),
        "conv_x": normal_values(keys[5], (CONV, HEADS * HEAD_SIZE), CONV ** -0.5, 3.0, ((1, 8),)),
        "conv_b": normal_values(keys[6], (CONV, STATE), CONV ** -0.5, 3.0, ((1, 8),)),
        "conv_c": normal_values(keys[7], (CONV, STATE), CONV ** -0.5, 3.0, ((1, 8),)),
        "decay_rate": draw_decay_rate(jax.random.fold_in(keys[10], 71), 0),
        "norm_gain": jnp.clip(1.0 + 0.1 * jax.random.normal(keys[9], (HEADS * HEAD_SIZE,), jnp.float32), 0.5, 1.5),
    }


def conv_valid(padded, weights, length):
    total = jnp.zeros((length, padded.shape[1]), jnp.float32)
    for k in range(weights.shape[0]):
        total = total + weights[k].astype(jnp.float32)[None, :] * padded[k:k + length].astype(jnp.float32)
    return jax.nn.silu(total).astype(jnp.bfloat16)

def causal_conv(rows, weights):
    width = weights.shape[0]
    padded = jnp.concatenate([jnp.zeros((width - 1, rows.shape[1]), rows.dtype), rows], axis=0)
    return conv_valid(padded, weights, rows.shape[0])

def block_parts(x_block, b_block, c_block, step_block, cum_block):
    scores = jnp.dot(c_block, b_block.T, preferred_element_type=jnp.float32)
    order = jnp.arange(x_block.shape[0])
    causal = order[:, None] >= order[None, :]
    gap = cum_block.T[:, :, None] - cum_block.T[:, None, :]
    gap = jnp.where(causal[None], gap, -jnp.inf)
    mixing = (scores[None] * jnp.exp(gap) * step_block.T[:, None, :]).astype(jnp.bfloat16)
    diag = jnp.einsum('hts,shp->thp', mixing.astype(jnp.float32), x_block.astype(jnp.float32))
    tail = jnp.exp(cum_block[-1][None, :] - cum_block) * step_block
    weighted = (tail[:, :, None] * x_block.astype(jnp.float32)).astype(jnp.bfloat16)
    block_state = jnp.einsum('shp,sn->hpn', weighted.astype(jnp.float32), b_block.astype(jnp.float32))
    return (diag, block_state)

def reference(x_rows, z_rows, b_rows, c_rows, step_raw, conv_x, conv_b, conv_c, decay_rate, norm_gain):
    xs = causal_conv(x_rows, conv_x)
    bs = causal_conv(b_rows, conv_b)
    cs = causal_conv(c_rows, conv_c)
    step = jax.nn.softplus(step_raw)
    log_decay = -step * decay_rate[None, :]
    count = TOKENS // GROUP
    pieces = (xs.reshape(count, GROUP, HEADS, HEAD_SIZE), bs.reshape(count, GROUP, STATE), cs.reshape(count, GROUP, STATE), step.reshape(count, GROUP, HEADS), log_decay.reshape(count, GROUP, HEADS))

    def advance(state, piece):
        x_block, b_block, c_block, step_block, decay_block = piece
        cum = jnp.cumsum(decay_block, axis=0)
        diag, block_state = block_parts(x_block, b_block, c_block, step_block, cum)
        carried = jnp.einsum('hpn,tn->thp', state, c_block.astype(jnp.float32), precision=lax.Precision.HIGHEST) * jnp.exp(cum)[:, :, None]
        new_state = jnp.exp(cum[-1])[:, None, None] * state + block_state
        return (new_state, (diag + carried).reshape(GROUP, HEADS * HEAD_SIZE))
    start = jnp.zeros((HEADS, HEAD_SIZE, STATE), jnp.float32)
    _, outputs = lax.scan(advance, start, pieces)
    y_rows = outputs.reshape(TOKENS, HEADS * HEAD_SIZE)
    gated = y_rows * jax.nn.silu(z_rows.astype(jnp.float32))
    mean_sq = lax.optimization_barrier(jnp.sum(gated * gated, axis=1, keepdims=True)) / (HEADS * HEAD_SIZE)
    return (gated * lax.rsqrt(mean_sq + 1e-05) * norm_gain[None, :]).astype(jnp.bfloat16)
```

```python
import functools
import math

import jax
import jax.numpy as jnp
from jax import lax
from jax.experimental import pallas as pl
from jax.experimental.pallas import tpu as pltpu
from jax.sharding import PartitionSpec as P

SUB = 128
ROWS = 16
TILE = 8 * SUB
LOG2E = math.log2(math.e)
MIB = 1024 * 1024
F32, BF16 = jnp.float32, jnp.bfloat16


def params(mib=16):
    return pltpu.CompilerParams(vmem_limit_bytes=mib * MIB)


def in_hbm(value):
    return pltpu.with_memory_space_constraint(value, pltpu.HBM)


def in_vmem(values):
    return [pltpu.with_memory_space_constraint(value, pltpu.VMEM) for value in values]


IN_VMEM = pl.BlockSpec(memory_space=pltpu.VMEM)
BRIEF = pl.CostEstimate(flops=1000, bytes_accessed=1000, transcendentals=0)
ANYWHERE = pl.BlockSpec(memory_space=pl.ANY)


def silu(value):
    half = 0.5 * value
    return half * jnp.tanh(half) + half


def factors(count):
    inner = max(d for d in range(1, math.isqrt(count) + 1) if count % d == 0)
    return count // inner, inner


def outer_pairs(d):
    outer, inner = factors(lax.axis_size("head"))
    return [(z * inner + y, (z + d) % outer * inner + y) for z in range(outer) for y in range(inner)]


def inner_pairs(e):
    outer, inner = factors(lax.axis_size("head"))
    return [(z * inner + y, z * inner + (y + e) % inner) for z in range(outer) for y in range(inner)]


def along_outer(piece):
    outer, _ = factors(lax.axis_size("head"))
    return [lax.ppermute(piece, "head", outer_pairs(d)) for d in range(1, outer)]


def along_inner(pieces):
    _, inner = factors(lax.axis_size("head"))
    return [lax.ppermute(p, "head", inner_pairs(e)) for e in range(1, inner) for p in pieces]


def tie_kernel(*refs):
    pass


def after(values, *tokens):
    out = pl.pallas_call(
        tie_kernel,
        in_specs=[ANYWHERE] * (len(values) + len(tokens)),
        out_specs=[ANYWHERE] * len(values),
        out_shape=[jax.ShapeDtypeStruct(v.shape, v.dtype) for v in values],
        input_output_aliases={i: i for i in range(len(values))},
        compiler_params=params(1),
        cost_estimate=BRIEF,
        name="tie",
    )(*values, *tokens)
    return list(out)


def pack_kernel(rows, cuts, *refs):
    outs = refs[len(refs) - len(cuts) + 1 :]
    for out_ref, first_token, last_token in zip(outs, cuts[:-1], cuts[1:]):
        row = 0
        for ref, (first, last) in zip(refs, rows):
            out_ref[row : row + last - first] = ref[first:last, first_token:last_token]
            row += last - first


def pack(pieces, rows, *tokens, cuts=None):
    cuts = cuts or [0, pieces[0].shape[1]]
    count = sum(last - first for first, last in rows)
    return pl.pallas_call(
        functools.partial(pack_kernel, rows, cuts),
        in_specs=[IN_VMEM] * len(pieces) + [ANYWHERE] * len(tokens),
        out_specs=[IN_VMEM] * (len(cuts) - 1),
        out_shape=[
            pltpu.VMEM((count, last - first), pieces[0].dtype) for first, last in zip(cuts[:-1], cuts[1:])
        ],
        compiler_params=params(),
        cost_estimate=BRIEF,
        name="pack",
    )(*in_vmem(pieces), *tokens)


def tails_kernel(x_ref, b_ref, c_ref, out_ref, b_out, c_out):
    cols, length = b_ref.shape
    out_ref[...] = jnp.zeros_like(out_ref)
    out_ref[:16] = x_ref[...]
    out_ref[16 : 16 + cols, :SUB] = b_ref[:, length - SUB :]
    out_ref[32 : 32 + cols, :SUB] = c_ref[:, length - SUB :]
    b_out[...] = b_ref[...]
    c_out[...] = c_ref[...]


def tails(x_rows, b_cols, c_cols):
    length, width = x_rows.shape
    cols = b_cols.shape[0]
    whole = pl.BlockSpec((cols, length), lambda i: (0, 0))
    held = pltpu.VMEM((cols, length), BF16)
    return pl.pallas_call(
        tails_kernel,
        grid=(1,),
        in_specs=[pl.BlockSpec((16, width), lambda i: (length // 16 - 1, 0)), whole, whole],
        out_specs=[pl.BlockSpec((48, width), lambda i: (0, 0)), IN_VMEM, IN_VMEM],
        out_shape=[jax.ShapeDtypeStruct((48, width), BF16), held, held],
        compiler_params=params(),
        cost_estimate=BRIEF,
        name="tails",
    )(in_hbm(x_rows), in_hbm(b_cols), in_hbm(c_cols))


def conv_columns(rows, halo, taps):
    wide = jnp.concatenate([halo, rows], axis=1).astype(F32)
    width = taps.shape[1]
    total = None
    for k in range(width):
        lag = width - 1 - k
        moved = pltpu.roll(wide, lag, axis=1) if lag else wide
        term = taps[:, k : k + 1] * moved[:, SUB:]
        total = term if total is None else total + term
    return silu(total).astype(BF16)


def shared_conv_kernel(b_ref, c_ref, halo_ref, tb_ref, tc_ref, bs_ref, cs_ref, again_ref):
    cols = b_ref.shape[0]
    bs_ref[...] = conv_columns(b_ref[...], halo_ref[16 : 16 + cols, :SUB], tb_ref[...])
    cs = conv_columns(c_ref[...], halo_ref[32 : 32 + cols, :SUB], tc_ref[...])
    cs_ref[...], again_ref[...] = cs, cs


def shared_conv(b_cols, c_cols, halo, taps_b, taps_c):
    operands = [b_cols, c_cols, halo, taps_b, taps_c]
    return pl.pallas_call(
        shared_conv_kernel,
        in_specs=[IN_VMEM] * 5,
        out_specs=[IN_VMEM] * 3,
        out_shape=[pltpu.VMEM(b_cols.shape, BF16)] * 3,
        compiler_params=params(),
        cost_estimate=BRIEF,
        name="shared_conv",
    )(*in_vmem(operands))


def parts_of(value, count):
    parts = []
    for _ in range(count):
        part = value.astype(BF16).astype(F32)
        parts.append(part)
        value = value - part
    return jnp.concatenate(parts, axis=0)


def spread_matrix(first, last, count, width, size):
    i = lax.broadcasted_iota(jnp.int32, (count, width), 0)
    j = lax.broadcasted_iota(jnp.int32, (count, width), 1)
    head = jnp.bitwise_and(i, 7) * size
    lanes = jnp.logical_and(j >= head, j < head + size)
    return jnp.logical_and(lanes, jnp.logical_and(i >= first, i < last)).astype(F32).astype(BF16)


def rows_kernel(step_ref, rate_ref, q_ref, column_ref, decay_ref, sp, ld):
    heads, length = step_ref.shape
    width = decay_ref.shape[1]
    subs = length // SUB
    raw = step_ref[...]
    soft = jnp.maximum(raw, 0.0) + jnp.log(1.0 + jnp.exp(-jnp.abs(raw)))
    sp[...] = jnp.ones_like(sp)
    ld[...] = jnp.zeros_like(ld)
    sp[:heads] = soft
    ld[:heads] = soft * (rate_ref[...] * -LOG2E)
    i = lax.broadcasted_iota(jnp.int32, (SUB, SUB), 0)
    j = lax.broadcasted_iota(jnp.int32, (SUB, SUB), 1)
    upper = (i <= j).astype(F32)
    logs = ld[...]
    stacked = jnp.concatenate([logs[:, s * SUB : (s + 1) * SUB] for s in range(subs)], axis=0)
    sums = jnp.dot(stacked, upper, precision=lax.Precision.HIGHEST, preferred_element_type=F32)
    log_step = jnp.log(sp[...]) * LOG2E
    lasts = []
    for s in range(subs):
        at = slice(s * SUB, (s + 1) * SUB)
        cum = sums[s * 8 : (s + 1) * 8]
        q = cum - log_step[:, at]
        q_ref[:, at] = q
        weight = jnp.exp2(cum[:, SUB - 1 :] - q)
        columns = jnp.concatenate([parts_of(weight, 2), parts_of(cum, 3)], axis=0).T
        column_ref[at] = columns.astype(BF16)
        lasts.append(columns[SUB - 1 :])
    whole = jnp.concatenate(lasts, axis=0).astype(BF16)
    to_lanes = spread_matrix(16, 40, 40, width, width // heads)
    decay_ref[...] = jnp.exp2(jnp.dot(whole, to_lanes, preferred_element_type=F32))


def rows_of(steps, rates, width):
    heads, length = steps.shape
    return pl.pallas_call(
        rows_kernel,
        in_specs=[IN_VMEM] * 2,
        out_specs=[IN_VMEM] * 3,
        out_shape=[
            pltpu.VMEM((8, length), F32),
            pltpu.VMEM((length, 40), BF16),
            pltpu.VMEM((length // SUB, width), F32),
        ],
        scratch_shapes=[pltpu.VMEM((8, length), F32), pltpu.VMEM((8, length), F32)],
        compiler_params=params(),
        cost_estimate=BRIEF,
        name="rows",
    )(*in_vmem([steps, rates]))


def head_conv_kernel(first, heads, x_ref, before_ref, halo_ref, taps_ref, column_ref, *refs):
    xs_ref, wt_ref, ext, spread = refs[-4:]
    length, width = x_ref.shape
    taps = taps_ref.shape[0]
    pairs = width // SUB

    @pl.when(pl.program_id(0) == 0)
    def _():
        for p in range(pairs):
            rows = before_ref if first else halo_ref
            ext[p, :8] = rows[8:16, p * SUB : (p + 1) * SUB].astype(F32)

    for p in range(pairs):
        ext[p, 8:] = x_ref[:, p * SUB : (p + 1) * SUB].astype(F32)
    count = column_ref.shape[1]
    spread[...] = jnp.dot(
        column_ref[...],
        spread_matrix(0, 16, count, width, width // heads),
        preferred_element_type=F32,
    )
    for s in range(length // SUB):
        at = slice(s * SUB, (s + 1) * SUB)
        for p in range(pairs):
            cols = slice(p * SUB, (p + 1) * SUB)
            total = None
            for k in range(taps):
                start = 8 - (taps - 1) + k + s * SUB
                term = taps_ref[k : k + 1, cols] * ext[p, start : start + SUB]
                total = term if total is None else total + term
            xs = silu(total).astype(BF16)
            xs_ref[at, cols] = xs
            wt_ref[at, cols] = (spread[at, cols] * xs.astype(F32)).astype(BF16)
    for p in range(pairs):
        ext[p, :8] = ext[p, length : length + 8]


def head_conv(x_rows, halo, taps, columns, heads, first, count, filled=()):
    length, width = x_rows.shape
    wide = pl.BlockSpec((TILE, width), lambda i: (first + i, 0))
    whole = lambda a: pl.BlockSpec(a.shape, lambda i: (0, 0))
    return pl.pallas_call(
        functools.partial(head_conv_kernel, first, heads),
        grid=(count,),
        in_specs=[
            wide,
            pl.BlockSpec((16, width), lambda i: (max(first * TILE // 16 - 1, 0), 0)),
            whole(halo),
            whole(taps),
            pl.BlockSpec((TILE, columns.shape[1]), lambda i: (first + i, 0)),
        ]
        + [ANYWHERE] * len(filled),
        out_specs=[wide, wide],
        out_shape=[jax.ShapeDtypeStruct((length, width), BF16)] * 2,
        scratch_shapes=[
            pltpu.VMEM((width // SUB, TILE + 8, SUB), F32),
            pltpu.VMEM((TILE, width), F32),
        ],
        compiler_params=params(),
        input_output_aliases={5 + i: i for i in range(len(filled))},
        cost_estimate=BRIEF,
        name="head_conv",
    )(in_hbm(x_rows), in_hbm(x_rows), halo, taps, columns, *filled)


def gates_kernel(z_ref, column_ref, q_ref, gate_ref, factor_ref, start_ref, spread):
    length, width = z_ref.shape
    heads = factor_ref.shape[0] // (length // ROWS)
    size = width // heads
    subs, groups = length // SUB, SUB // ROWS
    columns = column_ref[...]
    to_lanes = spread_matrix(16, 40, columns.shape[1], width, size)
    for p in range(width // SUB):
        spread[p] = jnp.dot(
            columns, to_lanes[:, p * SUB : (p + 1) * SUB], preferred_element_type=F32
        )
    for s in range(subs):
        at = slice(s * SUB, (s + 1) * SUB)
        starts = []
        for p in range(width // SUB):
            cols = slice(p * SUB, (p + 1) * SUB)
            cum = spread[p, at].reshape(groups, ROWS // 8, 8, SUB)
            grown = jnp.exp2(cum - cum[:, ROWS // 16 : ROWS // 16 + 1, :1]).reshape(SUB, SUB)
            gate_ref[at, cols] = grown * silu(z_ref[at, cols].astype(F32))
            start = spread[p, pl.ds(s * SUB + ROWS // 2, groups, stride=ROWS)]
            start_ref[p, s * groups : (s + 1) * groups] = jnp.exp2(start)
            starts.append(start)
        for h in range(heads):
            lane = h * size % SUB
            start = jnp.broadcast_to(starts[h * size // SUB][:, lane : lane + 1], (groups, SUB))
            row = (s * heads + h) * groups
            factor_ref[row : row + groups] = jnp.exp2(
                jnp.minimum(start - q_ref[h : h + 1, at], 64.0)
            )


def gates(z_rows, columns, q, heads):
    length, width = z_rows.shape
    wide = pl.BlockSpec((TILE, width), lambda i: (i, 0))
    rows = pl.BlockSpec((8, TILE), lambda i: (0, i))
    return pl.pallas_call(
        gates_kernel,
        grid=(length // TILE,),
        in_specs=[wide, pl.BlockSpec((TILE, columns.shape[1]), lambda i: (i, 0)), rows],
        out_specs=[
            wide,
            pl.BlockSpec((TILE // ROWS * heads, SUB), lambda i: (i, 0)),
            pl.BlockSpec((width // SUB, TILE // ROWS, SUB), lambda i: (0, i, 0)),
        ],
        out_shape=[
            jax.ShapeDtypeStruct((length, width), F32),
            jax.ShapeDtypeStruct((length // ROWS * heads, SUB), F32),
            jax.ShapeDtypeStruct((width // SUB, length // ROWS, SUB), F32),
        ],
        scratch_shapes=[pltpu.VMEM((width // SUB, TILE, SUB), F32)],
        compiler_params=params(),
        cost_estimate=BRIEF,
        name="gates",
    )(z_rows, columns, q)


def columns_of(refs, rows, at):
    return jnp.concatenate([ref[first:last, at] for ref, (first, last) in zip(refs, rows)], axis=0)


def columns_from(refs, rows, begins, start):
    parts = [
        ref[first:last, pl.ds(pl.multiple_of(start - begin, SUB), SUB)]
        for ref, (first, last), begin in zip(refs, rows, begins)
    ]
    return jnp.concatenate(parts, axis=0)


def last_state_kernel(rows, wt_ref, decay_ref, *refs):
    pieces, (out_ref, local_ref, before_ref, state, total) = refs[:-5], refs[-5:]
    size = state.shape[0]
    subs = TILE // SUB
    state[...] = jnp.zeros_like(state)
    total[...] = jnp.ones_like(total)

    def tile(t, _):
        held, grown = state[...], total[:1]
        row = pl.multiple_of(t * subs, subs)
        decays = decay_ref[pl.ds(row, subs)]
        products = []
        for s in range(subs):
            at = pl.ds(pl.multiple_of(t * TILE + s * SUB, SUB), SUB)
            b_cols = columns_of(pieces, rows, at)
            added = jnp.dot(b_cols, wt_ref[at], preferred_element_type=F32)
            local_ref[pl.ds(pl.multiple_of((t * subs + s) * size, size), size)] = held
            products.append(grown)
            held = held * decays[s : s + 1] + added
            grown = grown * decays[s : s + 1]
        before_ref[pl.ds(row, subs)] = jnp.concatenate(products, axis=0)
        state[...] = held
        total[...] = jnp.broadcast_to(grown, total.shape)
        return 0

    lax.fori_loop(0, wt_ref.shape[0] // TILE, tile, 0)
    out_ref[:size] = state[...].astype(BF16)
    out_ref[size:] = jnp.broadcast_to(total[:1], (16, total.shape[1])).astype(BF16)


def last_state(weighted, decays, pieces, rows):
    length, width = weighted.shape
    size = sum(last - first for first, last in rows)
    count = length // SUB
    return pl.pallas_call(
        functools.partial(last_state_kernel, rows),
        in_specs=[IN_VMEM] * (2 + len(pieces)),
        out_specs=[IN_VMEM] * 3,
        out_shape=[
            jax.ShapeDtypeStruct((size + 16, width), BF16),
            pltpu.VMEM((count * size, width), F32),
            pltpu.VMEM((count, width), F32),
        ],
        scratch_shapes=[pltpu.VMEM((size, width), F32), pltpu.VMEM((8, width), F32)],
        compiler_params=params(),
        cost_estimate=BRIEF,
        name="last_state",
    )(*in_vmem([weighted, decays, *pieces]))


def join_kernel(early_ref, late_ref, token_ref, out_ref):
    size = late_ref.shape[0] - 16
    early, late = early_ref[...].astype(F32), late_ref[...].astype(F32)
    decay = late[size : size + 1]
    out_ref[:size] = (early[:size] * decay + late[:size]).astype(BF16)
    out_ref[size:] = (early[size:] * decay).astype(BF16)


def join(early, late, token):
    return pl.pallas_call(
        join_kernel,
        in_specs=[IN_VMEM] * 2 + [ANYWHERE],
        out_specs=IN_VMEM,
        out_shape=jax.ShapeDtypeStruct(late.shape, BF16),
        compiler_params=params(),
        cost_estimate=BRIEF,
        name="join",
    )(*in_vmem([early, late]), token)


def enter_kernel(local_ref, before_ref, *refs):
    earlier, (out_ref, state) = refs[:-2], refs[-2:]
    size = state.shape[0]
    carry = jnp.zeros(state.shape, F32)
    for ref in reversed(earlier):
        carry = carry * ref[size : size + 1].astype(F32) + ref[:size].astype(F32)
    state[...] = carry
    some = 8

    def group(t, _):
        row = pl.multiple_of(t * some, some)
        decays = before_ref[pl.ds(row, some)]
        held = state[...]
        for s in range(some):
            at = pl.ds(pl.multiple_of((t * some + s) * size, size), size)
            out_ref[at] = (local_ref[at] + held * decays[s : s + 1]).astype(BF16)
        return 0

    lax.fori_loop(0, before_ref.shape[0] // some, group, 0)


def enter(local, before, earlier):
    rows, width = local.shape
    size = rows // before.shape[0]
    operands = [local, before, *earlier]
    return pl.pallas_call(
        enter_kernel,
        in_specs=[IN_VMEM] * len(operands),
        out_specs=IN_VMEM,
        out_shape=pltpu.VMEM((rows, width), BF16),
        scratch_shapes=[pltpu.VMEM((size, width), F32)],
        compiler_params=params(),
        cost_estimate=BRIEF,
        name="enter",
    )(*in_vmem(operands))


def scan_kernel(
    span, b_rows, b_picks, c_rows_of, c_picks, c_begins, gate_ref, factor_ref, start_ref, xs_ref, state_ref, *refs
):
    b_refs, c_refs = [refs[i] for i in b_picks], [refs[i] for i in c_picks]
    gated_ref, square_ref, c_rows, scores, carried, squares = refs[-6:]
    length, width = gate_ref.shape
    heads = factor_ref.shape[0] // (length // ROWS)
    groups, subs, pairs = SUB // ROWS, TILE // SUB, width // SUB
    size = state_ref.shape[0] // square_ref.shape[0]
    i = lax.broadcasted_iota(jnp.int32, (SUB, SUB), 0)
    j = lax.broadcasted_iota(jnp.int32, (SUB, SUB), 1)
    causal = i >= j
    low = (j < SUB // 2).astype(F32)
    keep_low, keep_high = low.astype(BF16), (1.0 - low).astype(BF16)

    def rows_times(value, load):
        rows = [value[g * ROWS : (g + 1) * ROWS] * load(g) for g in range(groups)]
        return jnp.concatenate(rows, axis=0)

    def repeated(ref, row):
        return jnp.broadcast_to(ref[pl.ds(row, 1)], (ROWS, SUB))

    local = [slice(s * SUB, (s + 1) * SUB) for s in range(subs)]

    def tile(t, _):
        whole = [pl.ds(pl.multiple_of(t * TILE + s * SUB, SUB), SUB) for s in range(subs)]
        row = pl.multiple_of(t * subs, subs)
        factors = pl.multiple_of(t * (subs * heads * groups), subs * heads * groups)
        starts = pl.multiple_of(t * (subs * groups), subs * groups)

        def turn(s):
            c_rows[local[s]] = columns_from(c_refs, c_rows_of, c_begins, t * TILE + s * SUB).T

        def products(s):
            b_cols = columns_of(b_refs, b_rows, whole[s])
            held = pl.ds(pl.multiple_of((t * subs + s) * size, size), size)
            both = jnp.dot(
                c_rows[local[s]],
                jnp.concatenate([b_cols, state_ref[held]], axis=1),
                preferred_element_type=F32,
            )
            scores[local[s]] = jnp.where(causal, both[:, :SUB], 0.0)
            carried[local[s]] = both[:, SUB:]

        turn(0)
        turn(1)
        products(0)
        for s, at in enumerate(whole):
            if s + 2 < subs:
                turn(s + 2)
            if s + 1 < subs:
                products(s + 1)
            total = None
            score = scores[local[s]]
            for p in range(pairs):
                cols = slice(p * SUB, (p + 1) * SUB)
                mixing = []
                for h in (2 * p, 2 * p + 1):
                    base = factors + (s * heads + h) * groups
                    mixing.append(rows_times(score, lambda g: repeated(factor_ref, base + g)).astype(BF16))
                xs = xs_ref[at, cols]
                mixed = jnp.dot(
                    jnp.concatenate(mixing, axis=1),
                    jnp.concatenate([xs * keep_low, xs * keep_high], axis=0),
                    preferred_element_type=F32,
                )
                base = starts + s * groups
                before = rows_times(carried[local[s], cols], lambda g: repeated(start_ref.at[p], base + g))
                gated = gate_ref[at, cols] * (mixed + before)
                gated_ref[at, cols] = gated.astype(BF16)
                square = gated * gated
                total = square if total is None else total + square
            squares[local[s]] = total.astype(BF16)
        sums = lax.dot_general(
            jnp.ones((8, SUB), BF16), squares[...], (((1,), (1,)), ((), ())), preferred_element_type=F32
        )
        square_ref[pl.ds(row, subs)] = jnp.concatenate([sums[:1, at] for at in local], axis=0)
        return 0

    lax.fori_loop(*span, tile, 0)


def scan(span, gate, factor, start, xs, states, b_pieces, b_rows, c_pieces, c_rows, c_begins, filled=()):
    length, width = xs.shape
    size = sum(last - first for first, last in b_rows)
    pieces = []
    for piece in b_pieces + c_pieces:
        if not any(piece is other for other in pieces):
            pieces.append(piece)
    picks = lambda some: [next(i for i, q in enumerate(pieces) if q is p) for p in some]
    operands = [gate, factor, start, xs, states, *pieces, *filled]
    first = len(operands) - len(filled)
    return pl.pallas_call(
        functools.partial(
            scan_kernel, span, b_rows, picks(b_pieces), c_rows, picks(c_pieces), c_begins
        ),
        in_specs=[IN_VMEM] * len(operands),
        out_specs=[IN_VMEM, IN_VMEM],
        out_shape=[pltpu.VMEM((length, width), BF16), pltpu.VMEM((length // SUB, SUB), F32)],
        scratch_shapes=[
            pltpu.VMEM((TILE, size), BF16),
            pltpu.VMEM((TILE, SUB), F32),
            pltpu.VMEM((TILE, width), F32),
            pltpu.VMEM((TILE, SUB), BF16),
        ],
        input_output_aliases={first + i: i for i in range(len(filled))},
        compiler_params=params(),
        cost_estimate=BRIEF,
        name="scan",
    )(*in_vmem(operands))


def norm_kernel(channels, gated_ref, gain_ref, *refs):
    squares, (out_ref, rows, sems) = refs[:-3], refs[-3:]
    total = squares[0][...]
    for ref in squares[1:]:
        total = total + ref[...]
    scale = lax.rsqrt(total * (1.0 / channels) + 1e-05).T
    gain = gain_ref[...]
    step = TILE // 2
    copies = []
    for t in range(gated_ref.shape[0] // step):
        for s in range(t * step // SUB, (t + 1) * step // SUB):
            at = slice(s * SUB, (s + 1) * SUB)
            rows[at] = (gated_ref[at].astype(F32) * scale[:, s : s + 1] * gain).astype(BF16)
        at = slice(t * step, (t + 1) * step)
        copies.append(pltpu.make_async_copy(rows.at[at], out_ref.at[at], sems.at[t]))
        copies[-1].start()
    for copy in copies:
        copy.wait()


def norm(channels, gated, gain, squares):
    length, width = gated.shape
    operands = [gated, gain, *squares]
    return pl.pallas_call(
        functools.partial(norm_kernel, channels),
        in_specs=[IN_VMEM] * len(operands),
        out_specs=ANYWHERE,
        out_shape=pltpu.HBM((length, width), BF16),
        scratch_shapes=[
            pltpu.VMEM((length, width), BF16),
            pltpu.SemaphoreType.DMA((2 * length // TILE,)),
        ],
        compiler_params=params(),
        cost_estimate=BRIEF,
        name="norm",
    )(*in_vmem(operands))


def body(x_rows, z_rows, b_rows, c_rows, step_raw, conv_x, conv_b, conv_c, decay_rate, norm_gain):
    length, width = x_rows.shape
    local_heads = decay_rate.shape[0]
    seq, heads = lax.axis_size("seq"), lax.axis_size("head")
    b_cols, c_cols = b_rows.T, c_rows.T
    ahead = lambda d: [(s, s + d) for s in range(seq - d)]
    ends, b_cols, c_cols = tails(x_rows, b_cols, c_cols)
    halo = lax.ppermute(ends, "seq", ahead(1))
    bs, cs, cs_sent = shared_conv(b_cols, c_cols, halo, conv_b.T.astype(F32), conv_c.T.astype(F32))
    cols = bs.shape[0]
    outer, _ = factors(heads)
    tiles = x_rows.shape[0] // TILE
    q, columns, decays = rows_of(step_raw.T, decay_rate[:, None], width)
    conv = functools.partial(head_conv, x_rows, halo, conv_x.astype(F32), columns, local_heads)
    if cols % 16 or factors(heads) != (4, 2):
        b_pieces, c_pieces = [
            [jnp.concatenate(near + along_inner(near), axis=0)]
            for near in ([own] + along_outer(own) for own in (bs, cs))
        ]
        b_rows = c_rows = [(0, b_pieces[0].shape[0])]
        xs, weighted = conv(0, tiles)
        mine, local, before = last_state(weighted, decays, b_pieces, b_rows)
        gate, factor, start = gates(z_rows, columns, q, local_heads)
        token, tail, runs = mine, [], [((0, tiles), None, None)]
    else:
        one, two = (0, cols), (0, 2 * cols)
        b_outer, own = along_outer(bs), along_inner([bs])
        xs, weighted = conv(0, tiles)
        (b_packed,) = pack(b_outer, [one] * 3, xs, *own)
        b_passed = along_inner([b_packed])
        cs_sent, columns = after([cs_sent, columns], b_packed)
        c_outer = along_outer(cs_sent)
        gate, factor, start = gates(z_rows, columns, q, local_heads)
        (c_first,) = pack([cs, c_outer[0]], [one] * 2, start)
        c_passed = along_inner([c_first])
        (decays,) = after([decays], c_first)
        b_pieces = [bs, *own, *b_outer, *b_passed]
        b_rows = [one] * 5 + [(0, 3 * cols)]
        mine, local, before = last_state(weighted, decays, b_pieces, b_rows)
        cut = -(-tiles // 2) * TILE
        c_rest = pack(c_outer[1:], [one] * 2, mine, cuts=[0, cut, length])
        c_ends = along_inner(c_rest)
        c_pieces = [cs, *c_passed, *c_outer, *c_passed]
        c_rows = [one] * 5 + [(cols, 2 * cols)]
        token, tail = c_rest[0], [two]
        runs = [((0, cut // TILE), c_ends[0], 0), ((cut // TILE, tiles), c_ends[1], cut)]
    earlier, reach, ends = [], 1, mine
    while True:
        earlier.append(lax.ppermute(ends, "seq", ahead(reach)))
        reach *= 2
        if reach >= seq:
            break
        ends = join(earlier[-1], ends, token)
    states = enter(local, before, earlier)
    filled = ()
    for span, piece, begin in runs:
        filled = scan(
            span, gate, factor, start, xs, states, b_pieces, b_rows,
            c_pieces + [piece] * len(tail), c_rows + tail, [0] * len(c_pieces) + [begin], filled,
        )
    gated, square = filled
    square = square + sum(along_outer(square))
    squares = [square] + along_inner([square])
    return norm(heads * width, gated, norm_gain[None, :], squares)


def solution(mesh):
    placed = (
        P("seq", "head"),
        P("seq", "head"),
        P("seq", "head"),
        P("seq", "head"),
        P("seq", "head"),
        P(None, "head"),
        P(None, "head"),
        P(None, "head"),
        P("head"),
        P("head"),
    )
    return jax.shard_map(
        body, mesh=mesh, in_specs=placed, out_specs=P("seq", "head"), check_vma=False
    )
```

```python
import functools
import math

import jax
import jax.numpy as jnp
from jax import lax
from jax.experimental import pallas as pl
from jax.experimental.pallas import tpu as pltpu
from jax.sharding import PartitionSpec as P

SUB = 128
ROWS = 16
TILE = 8 * SUB
LOG2E = math.log2(math.e)
MIB = 1024 * 1024
F32, BF16 = jnp.float32, jnp.bfloat16


def params(mib=16):
    return pltpu.CompilerParams(vmem_limit_bytes=mib * MIB)


def in_hbm(value):
    return pltpu.with_memory_space_constraint(value, pltpu.HBM)


def in_vmem(values):
    return [pltpu.with_memory_space_constraint(value, pltpu.VMEM) for value in values]


IN_VMEM = pl.BlockSpec(memory_space=pltpu.VMEM)
BRIEF = pl.CostEstimate(flops=1000, bytes_accessed=1000, transcendentals=0)
ANYWHERE = pl.BlockSpec(memory_space=pl.ANY)


def silu(value):
    half = 0.5 * value
    return half * jnp.tanh(half) + half


def factors(count):
    inner = max(d for d in range(1, math.isqrt(count) + 1) if count % d == 0)
    return count // inner, inner


def outer_pairs(d):
    outer, inner = factors(lax.axis_size("head"))
    return [(z * inner + y, (z + d) % outer * inner + y) for z in range(outer) for y in range(inner)]


def inner_pairs(e):
    outer, inner = factors(lax.axis_size("head"))
    return [(z * inner + y, z * inner + (y + e) % inner) for z in range(outer) for y in range(inner)]


def along_outer(piece):
    outer, _ = factors(lax.axis_size("head"))
    return [lax.ppermute(piece, "head", outer_pairs(d)) for d in range(1, outer)]


def along_inner(pieces):
    _, inner = factors(lax.axis_size("head"))
    return [lax.ppermute(p, "head", inner_pairs(e)) for e in range(1, inner) for p in pieces]


def tie_kernel(*refs):
    pass


def after(values, *tokens):
    out = pl.pallas_call(
        tie_kernel,
        in_specs=[ANYWHERE] * (len(values) + len(tokens)),
        out_specs=[ANYWHERE] * len(values),
        out_shape=[jax.ShapeDtypeStruct(v.shape, v.dtype) for v in values],
        input_output_aliases={i: i for i in range(len(values))},
        compiler_params=params(1),
        cost_estimate=BRIEF,
        name="tie",
    )(*values, *tokens)
    return list(out)


def pack_kernel(rows, cuts, *refs):
    outs = refs[len(refs) - len(cuts) + 1 :]
    for out_ref, first_token, last_token in zip(outs, cuts[:-1], cuts[1:]):
        row = 0
        for ref, (first, last) in zip(refs, rows):
            out_ref[row : row + last - first] = ref[first:last, first_token:last_token]
            row += last - first


def pack(pieces, rows, *tokens, cuts=None):
    cuts = cuts or [0, pieces[0].shape[1]]
    count = sum(last - first for first, last in rows)
    return pl.pallas_call(
        functools.partial(pack_kernel, rows, cuts),
        in_specs=[IN_VMEM] * len(pieces) + [ANYWHERE] * len(tokens),
        out_specs=[IN_VMEM] * (len(cuts) - 1),
        out_shape=[
            pltpu.VMEM((count, last - first), pieces[0].dtype) for first, last in zip(cuts[:-1], cuts[1:])
        ],
        compiler_params=params(),
        cost_estimate=BRIEF,
        name="pack",
    )(*in_vmem(pieces), *tokens)


def tails_kernel(x_ref, b_ref, c_ref, out_ref, b_out, c_out):
    cols, length = b_ref.shape
    out_ref[...] = jnp.zeros_like(out_ref)
    out_ref[:16] = x_ref[...]
    out_ref[16 : 16 + cols, :SUB] = b_ref[:, length - SUB :]
    out_ref[32 : 32 + cols, :SUB] = c_ref[:, length - SUB :]
    b_out[...] = b_ref[...]
    c_out[...] = c_ref[...]


def tails(x_rows, b_cols, c_cols):
    length, width = x_rows.shape
    cols = b_cols.shape[0]
    whole = pl.BlockSpec((cols, length), lambda i: (0, 0))
    held = pltpu.VMEM((cols, length), BF16)
    return pl.pallas_call(
        tails_kernel,
        grid=(1,),
        in_specs=[pl.BlockSpec((16, width), lambda i: (length // 16 - 1, 0)), whole, whole],
        out_specs=[pl.BlockSpec((48, width), lambda i: (0, 0)), IN_VMEM, IN_VMEM],
        out_shape=[jax.ShapeDtypeStruct((48, width), BF16), held, held],
        compiler_params=params(),
        cost_estimate=BRIEF,
        name="tails",
    )(in_hbm(x_rows), in_hbm(b_cols), in_hbm(c_cols))


def conv_columns(rows, halo, taps):
    wide = jnp.concatenate([halo, rows], axis=1).astype(F32)
    width = taps.shape[1]
    total = None
    for k in range(width):
        lag = width - 1 - k
        moved = pltpu.roll(wide, lag, axis=1) if lag else wide
        term = taps[:, k : k + 1] * moved[:, SUB:]
        total = term if total is None else total + term
    return silu(total).astype(BF16)


def shared_conv_kernel(b_ref, c_ref, halo_ref, tb_ref, tc_ref, bs_ref, cs_ref, again_ref):
    cols = b_ref.shape[0]
    bs_ref[...] = conv_columns(b_ref[...], halo_ref[16 : 16 + cols, :SUB], tb_ref[...])
    cs = conv_columns(c_ref[...], halo_ref[32 : 32 + cols, :SUB], tc_ref[...])
    cs_ref[...], again_ref[...] = cs, cs


def shared_conv(b_cols, c_cols, halo, taps_b, taps_c):
    operands = [b_cols, c_cols, halo, taps_b, taps_c]
    return pl.pallas_call(
        shared_conv_kernel,
        in_specs=[IN_VMEM] * 5,
        out_specs=[IN_VMEM] * 3,
        out_shape=[pltpu.VMEM(b_cols.shape, BF16)] * 3,
        compiler_params=params(),
        cost_estimate=BRIEF,
        name="shared_conv",
    )(*in_vmem(operands))


def parts_of(value, count):
    parts = []
    for _ in range(count):
        part = value.astype(BF16).astype(F32)
        parts.append(part)
        value = value - part
    return jnp.concatenate(parts, axis=0)


def spread_matrix(first, last, count, width, size):
    i = lax.broadcasted_iota(jnp.int32, (count, width), 0)
    j = lax.broadcasted_iota(jnp.int32, (count, width), 1)
    head = jnp.bitwise_and(i, 7) * size
    lanes = jnp.logical_and(j >= head, j < head + size)
    return jnp.logical_and(lanes, jnp.logical_and(i >= first, i < last)).astype(F32).astype(BF16)


def rows_kernel(step_ref, rate_ref, q_ref, column_ref, decay_ref, sp, ld):
    heads, length = step_ref.shape
    width = decay_ref.shape[1]
    subs = length // SUB
    raw = step_ref[...]
    soft = jnp.maximum(raw, 0.0) + jnp.log(1.0 + jnp.exp(-jnp.abs(raw)))
    sp[...] = jnp.ones_like(sp)
    ld[...] = jnp.zeros_like(ld)
    sp[:heads] = soft
    ld[:heads] = soft * (rate_ref[...] * -LOG2E)
    i = lax.broadcasted_iota(jnp.int32, (SUB, SUB), 0)
    j = lax.broadcasted_iota(jnp.int32, (SUB, SUB), 1)
    upper = (i <= j).astype(F32)
    logs = ld[...]
    stacked = jnp.concatenate([logs[:, s * SUB : (s + 1) * SUB] for s in range(subs)], axis=0)
    sums = jnp.dot(stacked, upper, precision=lax.Precision.HIGHEST, preferred_element_type=F32)
    log_step = jnp.log(sp[...]) * LOG2E
    lasts = []
    for s in range(subs):
        at = slice(s * SUB, (s + 1) * SUB)
        cum = sums[s * 8 : (s + 1) * 8]
        q = cum - log_step[:, at]
        q_ref[:, at] = q
        weight = jnp.exp2(cum[:, SUB - 1 :] - q)
        columns = jnp.concatenate([parts_of(weight, 2), parts_of(cum, 3)], axis=0).T
        column_ref[at] = columns.astype(BF16)
        lasts.append(columns[SUB - 1 :])
    whole = jnp.concatenate(lasts, axis=0).astype(BF16)
    to_lanes = spread_matrix(16, 40, 40, width, width // heads)
    decay_ref[...] = jnp.exp2(jnp.dot(whole, to_lanes, preferred_element_type=F32))


def rows_of(steps, rates, width):
    heads, length = steps.shape
    return pl.pallas_call(
        rows_kernel,
        in_specs=[IN_VMEM] * 2,
        out_specs=[IN_VMEM] * 3,
        out_shape=[
            pltpu.VMEM((8, length), F32),
            pltpu.VMEM((length, 40), BF16),
            pltpu.VMEM((length // SUB, width), F32),
        ],
        scratch_shapes=[pltpu.VMEM((8, length), F32), pltpu.VMEM((8, length), F32)],
        compiler_params=params(),
        cost_estimate=BRIEF,
        name="rows",
    )(*in_vmem([steps, rates]))


def head_conv_kernel(first, heads, x_ref, before_ref, halo_ref, taps_ref, column_ref, *refs):
    xs_ref, wt_ref, ext, spread = refs[-4:]
    length, width = x_ref.shape
    taps = taps_ref.shape[0]
    pairs = width // SUB

    @pl.when(pl.program_id(0) == 0)
    def _():
        for p in range(pairs):
            rows = before_ref if first else halo_ref
            ext[p, :8] = rows[8:16, p * SUB : (p + 1) * SUB].astype(F32)

    for p in range(pairs):
        ext[p, 8:] = x_ref[:, p * SUB : (p + 1) * SUB].astype(F32)
    count = column_ref.shape[1]
    spread[...] = jnp.dot(
        column_ref[...],
        spread_matrix(0, 16, count, width, width // heads),
        preferred_element_type=F32,
    )
    for s in range(length // SUB):
        at = slice(s * SUB, (s + 1) * SUB)
        for p in range(pairs):
            cols = slice(p * SUB, (p + 1) * SUB)
            total = None
            for k in range(taps):
                start = 8 - (taps - 1) + k + s * SUB
                term = taps_ref[k : k + 1, cols] * ext[p, start : start + SUB]
                total = term if total is None else total + term
            xs = silu(total).astype(BF16)
            xs_ref[at, cols] = xs
            wt_ref[at, cols] = (spread[at, cols] * xs.astype(F32)).astype(BF16)
    for p in range(pairs):
        ext[p, :8] = ext[p, length : length + 8]


def head_conv(x_rows, halo, taps, columns, heads, first, count, filled=()):
    length, width = x_rows.shape
    wide = pl.BlockSpec((TILE, width), lambda i: (first + i, 0))
    whole = lambda a: pl.BlockSpec(a.shape, lambda i: (0, 0))
    return pl.pallas_call(
        functools.partial(head_conv_kernel, first, heads),
        grid=(count,),
        in_specs=[
            wide,
            pl.BlockSpec((16, width), lambda i: (max(first * TILE // 16 - 1, 0), 0)),
            whole(halo),
            whole(taps),
            pl.BlockSpec((TILE, columns.shape[1]), lambda i: (first + i, 0)),
        ]
        + [ANYWHERE] * len(filled),
        out_specs=[wide, wide],
        out_shape=[jax.ShapeDtypeStruct((length, width), BF16)] * 2,
        scratch_shapes=[
            pltpu.VMEM((width // SUB, TILE + 8, SUB), F32),
            pltpu.VMEM((TILE, width), F32),
        ],
        compiler_params=params(),
        input_output_aliases={5 + i: i for i in range(len(filled))},
        cost_estimate=BRIEF,
        name="head_conv",
    )(in_hbm(x_rows), in_hbm(x_rows), halo, taps, columns, *filled)


def gates_kernel(z_ref, column_ref, q_ref, gate_ref, factor_ref, start_ref, spread):
    length, width = z_ref.shape
    heads = factor_ref.shape[0] // (length // ROWS)
    size = width // heads
    subs, groups = length // SUB, SUB // ROWS
    columns = column_ref[...]
    to_lanes = spread_matrix(16, 40, columns.shape[1], width, size)
    for p in range(width // SUB):
        spread[p] = jnp.dot(
            columns, to_lanes[:, p * SUB : (p + 1) * SUB], preferred_element_type=F32
        )
    for s in range(subs):
        at = slice(s * SUB, (s + 1) * SUB)
        starts = []
        for p in range(width // SUB):
            cols = slice(p * SUB, (p + 1) * SUB)
            cum = spread[p, at].reshape(groups, ROWS // 8, 8, SUB)
            grown = jnp.exp2(cum - cum[:, ROWS // 16 : ROWS // 16 + 1, :1]).reshape(SUB, SUB)
            gate_ref[at, cols] = grown * silu(z_ref[at, cols].astype(F32))
            start = spread[p, pl.ds(s * SUB + ROWS // 2, groups, stride=ROWS)]
            start_ref[p, s * groups : (s + 1) * groups] = jnp.exp2(start)
            starts.append(start)
        for h in range(heads):
            lane = h * size % SUB
            start = jnp.broadcast_to(starts[h * size // SUB][:, lane : lane + 1], (groups, SUB))
            row = (s * heads + h) * groups
            factor_ref[row : row + groups] = jnp.exp2(
                jnp.minimum(start - q_ref[h : h + 1, at], 64.0)
            )


def gates(z_rows, columns, q, heads):
    length, width = z_rows.shape
    wide = pl.BlockSpec((TILE, width), lambda i: (i, 0))
    rows = pl.BlockSpec((8, TILE), lambda i: (0, i))
    return pl.pallas_call(
        gates_kernel,
        grid=(length // TILE,),
        in_specs=[wide, pl.BlockSpec((TILE, columns.shape[1]), lambda i: (i, 0)), rows],
        out_specs=[
            wide,
            pl.BlockSpec((TILE // ROWS * heads, SUB), lambda i: (i, 0)),
            pl.BlockSpec((width // SUB, TILE // ROWS, SUB), lambda i: (0, i, 0)),
        ],
        out_shape=[
            jax.ShapeDtypeStruct((length, width), F32),
            jax.ShapeDtypeStruct((length // ROWS * heads, SUB), F32),
            jax.ShapeDtypeStruct((width // SUB, length // ROWS, SUB), F32),
        ],
        scratch_shapes=[pltpu.VMEM((width // SUB, TILE, SUB), F32)],
        compiler_params=params(),
        cost_estimate=BRIEF,
        name="gates",
    )(z_rows, columns, q)


def columns_of(refs, rows, at):
    return jnp.concatenate([ref[first:last, at] for ref, (first, last) in zip(refs, rows)], axis=0)


def columns_from(refs, rows, begins, start):
    parts = [
        ref[first:last, pl.ds(pl.multiple_of(start - begin, SUB), SUB)]
        for ref, (first, last), begin in zip(refs, rows, begins)
    ]
    return jnp.concatenate(parts, axis=0)


def last_state_kernel(rows, wt_ref, decay_ref, *refs):
    pieces, (out_ref, local_ref, before_ref, state, total) = refs[:-5], refs[-5:]
    size = state.shape[0]
    subs = TILE // SUB
    state[...] = jnp.zeros_like(state)
    total[...] = jnp.ones_like(total)

    def tile(t, _):
        held, grown = state[...], total[:1]
        row = pl.multiple_of(t * subs, subs)
        decays = decay_ref[pl.ds(row, subs)]
        products = []
        for s in range(subs):
            at = pl.ds(pl.multiple_of(t * TILE + s * SUB, SUB), SUB)
            b_cols = columns_of(pieces, rows, at)
            added = jnp.dot(b_cols, wt_ref[at], preferred_element_type=F32)
            local_ref[pl.ds(pl.multiple_of((t * subs + s) * size, size), size)] = held
            products.append(grown)
            held = held * decays[s : s + 1] + added
            grown = grown * decays[s : s + 1]
        before_ref[pl.ds(row, subs)] = jnp.concatenate(products, axis=0)
        state[...] = held
        total[...] = jnp.broadcast_to(grown, total.shape)
        return 0

    lax.fori_loop(0, wt_ref.shape[0] // TILE, tile, 0)
    out_ref[:size] = state[...].astype(BF16)
    out_ref[size:] = jnp.broadcast_to(total[:1], (16, total.shape[1])).astype(BF16)


def last_state(weighted, decays, pieces, rows):
    length, width = weighted.shape
    size = sum(last - first for first, last in rows)
    count = length // SUB
    return pl.pallas_call(
        functools.partial(last_state_kernel, rows),
        in_specs=[IN_VMEM] * (2 + len(pieces)),
        out_specs=[IN_VMEM] * 3,
        out_shape=[
            jax.ShapeDtypeStruct((size + 16, width), BF16),
            pltpu.VMEM((count * size, width), F32),
            pltpu.VMEM((count, width), F32),
        ],
        scratch_shapes=[pltpu.VMEM((size, width), F32), pltpu.VMEM((8, width), F32)],
        compiler_params=params(),
        cost_estimate=BRIEF,
        name="last_state",
    )(*in_vmem([weighted, decays, *pieces]))


def join_kernel(bit, mine_ref, other_ref, token_ref, out_ref):
    size = mine_ref.shape[0] - 16
    upper = jnp.bitwise_and(lax.axis_index("seq"), bit) != 0
    mine, other = mine_ref[...].astype(F32), other_ref[...].astype(F32)
    early, late = jnp.where(upper, other, mine), jnp.where(upper, mine, other)
    decay = late[size : size + 1]
    out_ref[:size] = (early[:size] * decay + late[:size]).astype(BF16)
    out_ref[size:] = (early[size:] * decay).astype(BF16)


def join(bit, mine, other, token):
    return pl.pallas_call(
        functools.partial(join_kernel, bit),
        in_specs=[IN_VMEM, IN_VMEM, ANYWHERE],
        out_specs=IN_VMEM,
        out_shape=jax.ShapeDtypeStruct(mine.shape, BF16),
        compiler_params=params(),
        cost_estimate=BRIEF,
        name="join",
    )(*in_vmem([mine, other]), token)


def enter_kernel(local_ref, before_ref, *refs):
    others, out_ref, state = refs[:-2], refs[-2], refs[-1]
    size = state.shape[0]
    carry = jnp.zeros(state.shape, F32)
    for k in reversed(range(len(others))):
        longer = carry * others[k][size : size + 1].astype(F32) + others[k][:size].astype(F32)
        carry = jnp.where(jnp.bitwise_and(lax.axis_index("seq"), 1 << k) != 0, longer, carry)
    state[...] = carry
    some = 8

    def group(t, _):
        row = pl.multiple_of(t * some, some)
        decays = before_ref[pl.ds(row, some)]
        held = state[...]
        for s in range(some):
            at = pl.ds(pl.multiple_of((t * some + s) * size, size), size)
            out_ref[at] = (local_ref[at] + held * decays[s : s + 1]).astype(BF16)
        return 0

    lax.fori_loop(0, before_ref.shape[0] // some, group, 0)


def enter(local, before, others):
    rows, width = local.shape
    size = rows // before.shape[0]
    operands = [local, before, *others]
    return pl.pallas_call(
        enter_kernel,
        in_specs=[IN_VMEM] * len(operands),
        out_specs=IN_VMEM,
        out_shape=pltpu.VMEM((rows, width), BF16),
        scratch_shapes=[pltpu.VMEM((size, width), F32)],
        compiler_params=params(),
        cost_estimate=BRIEF,
        name="enter",
    )(*in_vmem(operands))


def scan_kernel(
    span, b_rows, b_picks, c_rows_of, c_picks, c_begins, gate_ref, factor_ref, start_ref, xs_ref, state_ref, *refs
):
    b_refs, c_refs = [refs[i] for i in b_picks], [refs[i] for i in c_picks]
    gated_ref, square_ref, c_rows, scores, carried, squares = refs[-6:]
    length, width = gate_ref.shape
    heads = factor_ref.shape[0] // (length // ROWS)
    groups, subs, pairs = SUB // ROWS, TILE // SUB, width // SUB
    size = state_ref.shape[0] // square_ref.shape[0]
    i = lax.broadcasted_iota(jnp.int32, (SUB, SUB), 0)
    j = lax.broadcasted_iota(jnp.int32, (SUB, SUB), 1)
    causal = i >= j
    low = (j < SUB // 2).astype(F32)
    keep_low, keep_high = low.astype(BF16), (1.0 - low).astype(BF16)

    def rows_times(value, load):
        rows = [value[g * ROWS : (g + 1) * ROWS] * load(g) for g in range(groups)]
        return jnp.concatenate(rows, axis=0)

    def repeated(ref, row):
        return jnp.broadcast_to(ref[pl.ds(row, 1)], (ROWS, SUB))

    local = [slice(s * SUB, (s + 1) * SUB) for s in range(subs)]

    def tile(t, _):
        whole = [pl.ds(pl.multiple_of(t * TILE + s * SUB, SUB), SUB) for s in range(subs)]
        row = pl.multiple_of(t * subs, subs)
        factors = pl.multiple_of(t * (subs * heads * groups), subs * heads * groups)
        starts = pl.multiple_of(t * (subs * groups), subs * groups)

        def turn(s):
            c_rows[local[s]] = columns_from(c_refs, c_rows_of, c_begins, t * TILE + s * SUB).T

        def products(s):
            b_cols = columns_of(b_refs, b_rows, whole[s])
            held = pl.ds(pl.multiple_of((t * subs + s) * size, size), size)
            both = jnp.dot(
                c_rows[local[s]],
                jnp.concatenate([b_cols, state_ref[held]], axis=1),
                preferred_element_type=F32,
            )
            scores[local[s]] = jnp.where(causal, both[:, :SUB], 0.0)
            carried[local[s]] = both[:, SUB:]

        turn(0)
        turn(1)
        products(0)
        for s, at in enumerate(whole):
            if s + 2 < subs:
                turn(s + 2)
            if s + 1 < subs:
                products(s + 1)
            total = None
            score = scores[local[s]]
            for p in range(pairs):
                cols = slice(p * SUB, (p + 1) * SUB)
                mixing = []
                for h in (2 * p, 2 * p + 1):
                    base = factors + (s * heads + h) * groups
                    mixing.append(rows_times(score, lambda g: repeated(factor_ref, base + g)).astype(BF16))
                xs = xs_ref[at, cols]
                mixed = jnp.dot(
                    jnp.concatenate(mixing, axis=1),
                    jnp.concatenate([xs * keep_low, xs * keep_high], axis=0),
                    preferred_element_type=F32,
                )
                base = starts + s * groups
                before = rows_times(carried[local[s], cols], lambda g: repeated(start_ref.at[p], base + g))
                gated = gate_ref[at, cols] * (mixed + before)
                gated_ref[at, cols] = gated.astype(BF16)
                square = gated * gated
                total = square if total is None else total + square
            squares[local[s]] = total.astype(BF16)
        sums = lax.dot_general(
            jnp.ones((8, SUB), BF16), squares[...], (((1,), (1,)), ((), ())), preferred_element_type=F32
        )
        square_ref[pl.ds(row, subs)] = jnp.concatenate([sums[:1, at] for at in local], axis=0)
        return 0

    lax.fori_loop(*span, tile, 0)


def scan(span, gate, factor, start, xs, states, b_pieces, b_rows, c_pieces, c_rows, c_begins, filled=()):
    length, width = xs.shape
    size = sum(last - first for first, last in b_rows)
    pieces = []
    for piece in b_pieces + c_pieces:
        if not any(piece is other for other in pieces):
            pieces.append(piece)
    picks = lambda some: [next(i for i, q in enumerate(pieces) if q is p) for p in some]
    operands = [gate, factor, start, xs, states, *pieces, *filled]
    first = len(operands) - len(filled)
    return pl.pallas_call(
        functools.partial(
            scan_kernel, span, b_rows, picks(b_pieces), c_rows, picks(c_pieces), c_begins
        ),
        in_specs=[IN_VMEM] * len(operands),
        out_specs=[IN_VMEM, IN_VMEM],
        out_shape=[pltpu.VMEM((length, width), BF16), pltpu.VMEM((length // SUB, SUB), F32)],
        scratch_shapes=[
            pltpu.VMEM((TILE, size), BF16),
            pltpu.VMEM((TILE, SUB), F32),
            pltpu.VMEM((TILE, width), F32),
            pltpu.VMEM((TILE, SUB), BF16),
        ],
        input_output_aliases={first + i: i for i in range(len(filled))},
        compiler_params=params(),
        cost_estimate=BRIEF,
        name="scan",
    )(*in_vmem(operands))


def norm_kernel(channels, gated_ref, gain_ref, *refs):
    squares, (out_ref, rows, sems) = refs[:-3], refs[-3:]
    total = squares[0][...]
    for ref in squares[1:]:
        total = total + ref[...]
    scale = lax.rsqrt(total * (1.0 / channels) + 1e-05).T
    gain = gain_ref[...]
    step = TILE // 2
    copies = []
    for t in range(gated_ref.shape[0] // step):
        for s in range(t * step // SUB, (t + 1) * step // SUB):
            at = slice(s * SUB, (s + 1) * SUB)
            rows[at] = (gated_ref[at].astype(F32) * scale[:, s : s + 1] * gain).astype(BF16)
        at = slice(t * step, (t + 1) * step)
        copies.append(pltpu.make_async_copy(rows.at[at], out_ref.at[at], sems.at[t]))
        copies[-1].start()
    for copy in copies:
        copy.wait()


def norm(channels, gated, gain, squares):
    length, width = gated.shape
    operands = [gated, gain, *squares]
    return pl.pallas_call(
        functools.partial(norm_kernel, channels),
        in_specs=[IN_VMEM] * len(operands),
        out_specs=ANYWHERE,
        out_shape=pltpu.HBM((length, width), BF16),
        scratch_shapes=[
            pltpu.VMEM((length, width), BF16),
            pltpu.SemaphoreType.DMA((2 * length // TILE,)),
        ],
        compiler_params=params(),
        cost_estimate=BRIEF,
        name="norm",
    )(*in_vmem(operands))


def body(x_rows, z_rows, b_rows, c_rows, step_raw, conv_x, conv_b, conv_c, decay_rate, norm_gain):
    length, width = x_rows.shape
    local_heads = decay_rate.shape[0]
    seq, heads = lax.axis_size("seq"), lax.axis_size("head")
    b_cols, c_cols = b_rows.T, c_rows.T
    ends, b_cols, c_cols = tails(x_rows, b_cols, c_cols)
    halo = lax.ppermute(ends, "seq", [(i, i + 1) for i in range(seq - 1)])
    bs, cs, cs_sent = shared_conv(b_cols, c_cols, halo, conv_b.T.astype(F32), conv_c.T.astype(F32))
    cols = bs.shape[0]
    outer, _ = factors(heads)
    tiles = x_rows.shape[0] // TILE
    q, columns, decays = rows_of(step_raw.T, decay_rate[:, None], width)
    conv = functools.partial(head_conv, x_rows, halo, conv_x.astype(F32), columns, local_heads)
    if cols % 16 or factors(heads) != (4, 2):
        b_pieces, c_pieces = [
            [jnp.concatenate(near + along_inner(near), axis=0)]
            for near in ([own] + along_outer(own) for own in (bs, cs))
        ]
        b_rows = c_rows = [(0, b_pieces[0].shape[0])]
        xs, weighted = conv(0, tiles)
        mine, local, before = last_state(weighted, decays, b_pieces, b_rows)
        gate, factor, start = gates(z_rows, columns, q, local_heads)
        token, tail, runs = mine, [], [((0, tiles), None, None)]
    else:
        one, two = (0, cols), (0, 2 * cols)
        b_outer, own = along_outer(bs), along_inner([bs])
        xs, weighted = conv(0, tiles)
        (b_packed,) = pack(b_outer, [one] * 3, xs, *own)
        b_passed = along_inner([b_packed])
        cs_sent, columns = after([cs_sent, columns], b_packed)
        c_outer = along_outer(cs_sent)
        gate, factor, start = gates(z_rows, columns, q, local_heads)
        (c_first,) = pack([cs, c_outer[0]], [one] * 2, start)
        c_passed = along_inner([c_first])
        (decays,) = after([decays], c_first)
        b_pieces = [bs, *own, *b_outer, *b_passed]
        b_rows = [one] * 5 + [(0, 3 * cols)]
        mine, local, before = last_state(weighted, decays, b_pieces, b_rows)
        cut = -(-tiles // 2) * TILE
        c_rest = pack(c_outer[1:], [one] * 2, mine, cuts=[0, cut, length])
        c_ends = along_inner(c_rest)
        c_pieces = [cs, *c_passed, *c_outer, *c_passed]
        c_rows = [one] * 5 + [(cols, 2 * cols)]
        token, tail = c_rest[0], [two]
        runs = [((0, cut // TILE), c_ends[0], 0), ((cut // TILE, tiles), c_ends[1], cut)]
    others, bit = [], 1
    while bit < seq:
        last = 2 * bit == seq
        pairs = [(i, i ^ bit) for i in range(seq) if not (last and i & bit)]
        others.append(lax.ppermute(mine, "seq", pairs))
        if not last:
            mine = join(bit, mine, others[-1], token)
        bit *= 2
    states = enter(local, before, others)
    filled = ()
    for span, piece, begin in runs:
        filled = scan(
            span, gate, factor, start, xs, states, b_pieces, b_rows,
            c_pieces + [piece] * len(tail), c_rows + tail, [0] * len(c_pieces) + [begin], filled,
        )
    gated, square = filled
    square = square + sum(along_outer(square))
    squares = [square] + along_inner([square])
    return norm(heads * width, gated, norm_gain[None, :], squares)


def solution(mesh):
    placed = (
        P("seq", "head"),
        P("seq", "head"),
        P("seq", "head"),
        P("seq", "head"),
        P("seq", "head"),
        P(None, "head"),
        P(None, "head"),
        P(None, "head"),
        P("head"),
        P("head"),
    )
    return jax.shard_map(
        body, mesh=mesh, in_specs=placed, out_specs=P("seq", "head"), check_vma=False
    )
```

```python
import functools
import math

import jax
import jax.numpy as jnp
from jax import lax
from jax.experimental import pallas as pl
from jax.experimental.pallas import tpu as pltpu
from jax.sharding import PartitionSpec as P

SUB = 128
ROWS = 16
TILE = 8 * SUB
LOG2E = math.log2(math.e)
MIB = 1024 * 1024
F32, BF16 = jnp.float32, jnp.bfloat16


def params(mib=16):
    return pltpu.CompilerParams(vmem_limit_bytes=mib * MIB)


def in_hbm(value):
    return pltpu.with_memory_space_constraint(value, pltpu.HBM)


def in_vmem(values):
    return [pltpu.with_memory_space_constraint(value, pltpu.VMEM) for value in values]


IN_VMEM = pl.BlockSpec(memory_space=pltpu.VMEM)
BRIEF = pl.CostEstimate(flops=1000, bytes_accessed=1000, transcendentals=0)
ANYWHERE = pl.BlockSpec(memory_space=pl.ANY)


def silu(value):
    half = 0.5 * value
    return half * jnp.tanh(half) + half


def factors(count):
    inner = max(d for d in range(1, math.isqrt(count) + 1) if count % d == 0)
    return count // inner, inner


def outer_pairs(d):
    outer, inner = factors(lax.axis_size("head"))
    return [(z * inner + y, (z + d) % outer * inner + y) for z in range(outer) for y in range(inner)]


def inner_pairs(e):
    outer, inner = factors(lax.axis_size("head"))
    return [(z * inner + y, z * inner + (y + e) % inner) for z in range(outer) for y in range(inner)]


def along_outer(piece):
    outer, _ = factors(lax.axis_size("head"))
    return [lax.ppermute(piece, "head", outer_pairs(d)) for d in range(1, outer)]


def along_inner(pieces):
    _, inner = factors(lax.axis_size("head"))
    return [lax.ppermute(p, "head", inner_pairs(e)) for e in range(1, inner) for p in pieces]


def tie_kernel(*refs):
    pass


def after(values, *tokens):
    out = pl.pallas_call(
        tie_kernel,
        in_specs=[ANYWHERE] * (len(values) + len(tokens)),
        out_specs=[ANYWHERE] * len(values),
        out_shape=[jax.ShapeDtypeStruct(v.shape, v.dtype) for v in values],
        input_output_aliases={i: i for i in range(len(values))},
        compiler_params=params(1),
        cost_estimate=BRIEF,
        name="tie",
    )(*values, *tokens)
    return list(out)


def pack_kernel(rows, cuts, *refs):
    outs = refs[len(refs) - len(cuts) + 1 :]
    for out_ref, first_token, last_token in zip(outs, cuts[:-1], cuts[1:]):
        row = 0
        for ref, (first, last) in zip(refs, rows):
            out_ref[row : row + last - first] = ref[first:last, first_token:last_token]
            row += last - first


def pack(pieces, rows, *tokens, cuts=None):
    cuts = cuts or [0, pieces[0].shape[1]]
    count = sum(last - first for first, last in rows)
    return pl.pallas_call(
        functools.partial(pack_kernel, rows, cuts),
        in_specs=[IN_VMEM] * len(pieces) + [ANYWHERE] * len(tokens),
        out_specs=[IN_VMEM] * (len(cuts) - 1),
        out_shape=[
            pltpu.VMEM((count, last - first), pieces[0].dtype) for first, last in zip(cuts[:-1], cuts[1:])
        ],
        compiler_params=params(),
        cost_estimate=BRIEF,
        name="pack",
    )(*in_vmem(pieces), *tokens)


def tails_kernel(x_ref, b_ref, c_ref, out_ref, b_out, c_out):
    cols, length = b_ref.shape
    out_ref[...] = jnp.zeros_like(out_ref)
    out_ref[:16] = x_ref[...]
    out_ref[16 : 16 + cols, :SUB] = b_ref[:, length - SUB :]
    out_ref[32 : 32 + cols, :SUB] = c_ref[:, length - SUB :]
    b_out[...] = b_ref[...]
    c_out[...] = c_ref[...]


def tails(x_rows, b_cols, c_cols):
    length, width = x_rows.shape
    cols = b_cols.shape[0]
    whole = pl.BlockSpec((cols, length), lambda i: (0, 0))
    held = pltpu.VMEM((cols, length), BF16)
    return pl.pallas_call(
        tails_kernel,
        grid=(1,),
        in_specs=[pl.BlockSpec((16, width), lambda i: (length // 16 - 1, 0)), whole, whole],
        out_specs=[pl.BlockSpec((48, width), lambda i: (0, 0)), IN_VMEM, IN_VMEM],
        out_shape=[jax.ShapeDtypeStruct((48, width), BF16), held, held],
        compiler_params=params(),
        cost_estimate=BRIEF,
        name="tails",
    )(in_hbm(x_rows), in_hbm(b_cols), in_hbm(c_cols))


def conv_columns(rows, halo, taps):
    wide = jnp.concatenate([halo, rows], axis=1).astype(F32)
    width = taps.shape[1]
    total = None
    for k in range(width):
        lag = width - 1 - k
        moved = pltpu.roll(wide, lag, axis=1) if lag else wide
        term = taps[:, k : k + 1] * moved[:, SUB:]
        total = term if total is None else total + term
    return silu(total).astype(BF16)


def shared_conv_kernel(b_ref, c_ref, halo_ref, tb_ref, tc_ref, bs_ref, cs_ref, again_ref):
    cols = b_ref.shape[0]
    bs_ref[...] = conv_columns(b_ref[...], halo_ref[16 : 16 + cols, :SUB], tb_ref[...])
    cs = conv_columns(c_ref[...], halo_ref[32 : 32 + cols, :SUB], tc_ref[...])
    cs_ref[...], again_ref[...] = cs, cs


def shared_conv(b_cols, c_cols, halo, taps_b, taps_c):
    operands = [b_cols, c_cols, halo, taps_b, taps_c]
    return pl.pallas_call(
        shared_conv_kernel,
        in_specs=[IN_VMEM] * 5,
        out_specs=[IN_VMEM] * 3,
        out_shape=[pltpu.VMEM(b_cols.shape, BF16)] * 3,
        compiler_params=params(),
        cost_estimate=BRIEF,
        name="shared_conv",
    )(*in_vmem(operands))


def parts_of(value, count):
    parts = []
    for _ in range(count):
        part = value.astype(BF16).astype(F32)
        parts.append(part)
        value = value - part
    return jnp.concatenate(parts, axis=0)


def spread_matrix(first, last, count, width, size):
    i = lax.broadcasted_iota(jnp.int32, (count, width), 0)
    j = lax.broadcasted_iota(jnp.int32, (count, width), 1)
    head = jnp.bitwise_and(i, 7) * size
    lanes = jnp.logical_and(j >= head, j < head + size)
    return jnp.logical_and(lanes, jnp.logical_and(i >= first, i < last)).astype(F32).astype(BF16)


def rows_kernel(step_ref, rate_ref, q_ref, column_ref, decay_ref, sp, ld):
    heads, length = step_ref.shape
    width = decay_ref.shape[1]
    subs = length // SUB
    raw = step_ref[...]
    soft = jnp.maximum(raw, 0.0) + jnp.log(1.0 + jnp.exp(-jnp.abs(raw)))
    sp[...] = jnp.ones_like(sp)
    ld[...] = jnp.zeros_like(ld)
    sp[:heads] = soft
    ld[:heads] = soft * (rate_ref[...] * -LOG2E)
    i = lax.broadcasted_iota(jnp.int32, (SUB, SUB), 0)
    j = lax.broadcasted_iota(jnp.int32, (SUB, SUB), 1)
    upper = (i <= j).astype(F32)
    logs = ld[...]
    stacked = jnp.concatenate([logs[:, s * SUB : (s + 1) * SUB] for s in range(subs)], axis=0)
    sums = jnp.dot(stacked, upper, precision=lax.Precision.HIGHEST, preferred_element_type=F32)
    log_step = jnp.log(sp[...]) * LOG2E
    lasts = []
    for s in range(subs):
        at = slice(s * SUB, (s + 1) * SUB)
        cum = sums[s * 8 : (s + 1) * 8]
        q = cum - log_step[:, at]
        q_ref[:, at] = q
        weight = jnp.exp2(cum[:, SUB - 1 :] - q)
        columns = jnp.concatenate([parts_of(weight, 2), parts_of(cum, 3)], axis=0).T
        column_ref[at] = columns.astype(BF16)
        lasts.append(columns[SUB - 1 :])
    whole = jnp.concatenate(lasts, axis=0).astype(BF16)
    to_lanes = spread_matrix(16, 40, 40, width, width // heads)
    decay_ref[...] = jnp.exp2(jnp.dot(whole, to_lanes, preferred_element_type=F32))


def rows_of(steps, rates, width):
    heads, length = steps.shape
    return pl.pallas_call(
        rows_kernel,
        in_specs=[IN_VMEM] * 2,
        out_specs=[IN_VMEM] * 3,
        out_shape=[
            pltpu.VMEM((8, length), F32),
            pltpu.VMEM((length, 40), BF16),
            pltpu.VMEM((length // SUB, width), F32),
        ],
        scratch_shapes=[pltpu.VMEM((8, length), F32), pltpu.VMEM((8, length), F32)],
        compiler_params=params(),
        cost_estimate=BRIEF,
        name="rows",
    )(*in_vmem([steps, rates]))


def head_conv_kernel(first, heads, x_ref, before_ref, halo_ref, taps_ref, column_ref, *refs):
    xs_ref, wt_ref, ext, spread = refs[-4:]
    length, width = x_ref.shape
    taps = taps_ref.shape[0]
    pairs = width // SUB

    @pl.when(pl.program_id(0) == 0)
    def _():
        for p in range(pairs):
            rows = before_ref if first else halo_ref
            ext[p, :8] = rows[8:16, p * SUB : (p + 1) * SUB].astype(F32)

    for p in range(pairs):
        ext[p, 8:] = x_ref[:, p * SUB : (p + 1) * SUB].astype(F32)
    count = column_ref.shape[1]
    spread[...] = jnp.dot(
        column_ref[...],
        spread_matrix(0, 16, count, width, width // heads),
        preferred_element_type=F32,
    )
    for s in range(length // SUB):
        at = slice(s * SUB, (s + 1) * SUB)
        for p in range(pairs):
            cols = slice(p * SUB, (p + 1) * SUB)
            total = None
            for k in range(taps):
                start = 8 - (taps - 1) + k + s * SUB
                term = taps_ref[k : k + 1, cols] * ext[p, start : start + SUB]
                total = term if total is None else total + term
            xs = silu(total).astype(BF16)
            xs_ref[at, cols] = xs
            wt_ref[at, cols] = (spread[at, cols] * xs.astype(F32)).astype(BF16)
    for p in range(pairs):
        ext[p, :8] = ext[p, length : length + 8]


def head_conv(x_rows, halo, taps, columns, heads, first, count, filled=()):
    length, width = x_rows.shape
    wide = pl.BlockSpec((TILE, width), lambda i: (first + i, 0))
    whole = lambda a: pl.BlockSpec(a.shape, lambda i: (0, 0))
    return pl.pallas_call(
        functools.partial(head_conv_kernel, first, heads),
        grid=(count,),
        in_specs=[
            wide,
            pl.BlockSpec((16, width), lambda i: (max(first * TILE // 16 - 1, 0), 0)),
            whole(halo),
            whole(taps),
            pl.BlockSpec((TILE, columns.shape[1]), lambda i: (first + i, 0)),
        ]
        + [ANYWHERE] * len(filled),
        out_specs=[wide, wide],
        out_shape=[jax.ShapeDtypeStruct((length, width), BF16)] * 2,
        scratch_shapes=[
            pltpu.VMEM((width // SUB, TILE + 8, SUB), F32),
            pltpu.VMEM((TILE, width), F32),
        ],
        compiler_params=params(),
        input_output_aliases={5 + i: i for i in range(len(filled))},
        cost_estimate=BRIEF,
        name="head_conv",
    )(in_hbm(x_rows), in_hbm(x_rows), halo, taps, columns, *filled)


def gates_kernel(z_ref, column_ref, q_ref, gate_ref, factor_ref, start_ref, spread):
    length, width = z_ref.shape
    heads = factor_ref.shape[0] // (length // ROWS)
    size = width // heads
    subs, groups = length // SUB, SUB // ROWS
    columns = column_ref[...]
    to_lanes = spread_matrix(16, 40, columns.shape[1], width, size)
    for p in range(width // SUB):
        spread[p] = jnp.dot(
            columns, to_lanes[:, p * SUB : (p + 1) * SUB], preferred_element_type=F32
        )
    for s in range(subs):
        at = slice(s * SUB, (s + 1) * SUB)
        starts = []
        for p in range(width // SUB):
            cols = slice(p * SUB, (p + 1) * SUB)
            cum = spread[p, at].reshape(groups, ROWS // 8, 8, SUB)
            grown = jnp.exp2(cum - cum[:, ROWS // 16 : ROWS // 16 + 1, :1]).reshape(SUB, SUB)
            gate_ref[at, cols] = grown * silu(z_ref[at, cols].astype(F32))
            start = spread[p, pl.ds(s * SUB + ROWS // 2, groups, stride=ROWS)]
            start_ref[p, s * groups : (s + 1) * groups] = jnp.exp2(start)
            starts.append(start)
        for h in range(heads):
            lane = h * size % SUB
            start = jnp.broadcast_to(starts[h * size // SUB][:, lane : lane + 1], (groups, SUB))
            row = (s * heads + h) * groups
            factor_ref[row : row + groups] = jnp.exp2(
                jnp.minimum(start - q_ref[h : h + 1, at], 64.0)
            )


def gates(z_rows, columns, q, heads):
    length, width = z_rows.shape
    wide = pl.BlockSpec((TILE, width), lambda i: (i, 0))
    rows = pl.BlockSpec((8, TILE), lambda i: (0, i))
    return pl.pallas_call(
        gates_kernel,
        grid=(length // TILE,),
        in_specs=[wide, pl.BlockSpec((TILE, columns.shape[1]), lambda i: (i, 0)), rows],
        out_specs=[
            wide,
            pl.BlockSpec((TILE // ROWS * heads, SUB), lambda i: (i, 0)),
            pl.BlockSpec((width // SUB, TILE // ROWS, SUB), lambda i: (0, i, 0)),
        ],
        out_shape=[
            jax.ShapeDtypeStruct((length, width), F32),
            jax.ShapeDtypeStruct((length // ROWS * heads, SUB), F32),
            jax.ShapeDtypeStruct((width // SUB, length // ROWS, SUB), F32),
        ],
        scratch_shapes=[pltpu.VMEM((width // SUB, TILE, SUB), F32)],
        compiler_params=params(),
        cost_estimate=BRIEF,
        name="gates",
    )(z_rows, columns, q)


def columns_of(refs, rows, at):
    return jnp.concatenate([ref[first:last, at] for ref, (first, last) in zip(refs, rows)], axis=0)


def columns_from(refs, rows, begins, start):
    parts = [
        ref[first:last, pl.ds(pl.multiple_of(start - begin, SUB), SUB)]
        for ref, (first, last), begin in zip(refs, rows, begins)
    ]
    return jnp.concatenate(parts, axis=0)


def last_state_kernel(rows, wt_ref, decay_ref, *refs):
    pieces, (out_ref, local_ref, before_ref, state, total) = refs[:-5], refs[-5:]
    size = state.shape[0]
    subs = TILE // SUB
    state[...] = jnp.zeros_like(state)
    total[...] = jnp.ones_like(total)

    def tile(t, _):
        held, grown = state[...], total[:1]
        row = pl.multiple_of(t * subs, subs)
        decays = decay_ref[pl.ds(row, subs)]
        products = []
        for s in range(subs):
            at = pl.ds(pl.multiple_of(t * TILE + s * SUB, SUB), SUB)
            b_cols = columns_of(pieces, rows, at)
            added = jnp.dot(b_cols, wt_ref[at], preferred_element_type=F32)
            local_ref[pl.ds(pl.multiple_of((t * subs + s) * size, size), size)] = held
            products.append(grown)
            held = held * decays[s : s + 1] + added
            grown = grown * decays[s : s + 1]
        before_ref[pl.ds(row, subs)] = jnp.concatenate(products, axis=0)
        state[...] = held
        total[...] = jnp.broadcast_to(grown, total.shape)
        return 0

    lax.fori_loop(0, wt_ref.shape[0] // TILE, tile, 0)
    out_ref[:size] = state[...].astype(BF16)
    out_ref[size:] = jnp.broadcast_to(total[:1], (16, total.shape[1])).astype(BF16)


def last_state(weighted, decays, pieces, rows):
    length, width = weighted.shape
    size = sum(last - first for first, last in rows)
    count = length // SUB
    return pl.pallas_call(
        functools.partial(last_state_kernel, rows),
        in_specs=[IN_VMEM] * (2 + len(pieces)),
        out_specs=[IN_VMEM] * 3,
        out_shape=[
            jax.ShapeDtypeStruct((size + 16, width), BF16),
            pltpu.VMEM((count * size, width), F32),
            pltpu.VMEM((count, width), F32),
        ],
        scratch_shapes=[pltpu.VMEM((size, width), F32), pltpu.VMEM((8, width), F32)],
        compiler_params=params(),
        cost_estimate=BRIEF,
        name="last_state",
    )(*in_vmem([weighted, decays, *pieces]))


def join_kernel(bit, mine_ref, other_ref, token_ref, out_ref):
    size = mine_ref.shape[0] - 16
    upper = jnp.bitwise_and(lax.axis_index("seq"), bit) != 0
    mine, other = mine_ref[...].astype(F32), other_ref[...].astype(F32)
    early, late = jnp.where(upper, other, mine), jnp.where(upper, mine, other)
    decay = late[size : size + 1]
    out_ref[:size] = (early[:size] * decay + late[:size]).astype(BF16)
    out_ref[size:] = (early[size:] * decay).astype(BF16)


def join(bit, mine, other, token):
    return pl.pallas_call(
        functools.partial(join_kernel, bit),
        in_specs=[IN_VMEM, IN_VMEM, ANYWHERE],
        out_specs=IN_VMEM,
        out_shape=jax.ShapeDtypeStruct(mine.shape, BF16),
        compiler_params=params(),
        cost_estimate=BRIEF,
        name="join",
    )(*in_vmem([mine, other]), token)


def scan_kernel(
    span, count, b_rows, b_picks, c_rows_of, c_picks, c_begins, gate_ref, factor_ref, start_ref, xs_ref,
    local_ref, before_ref, *refs
):
    others, refs = refs[:count], refs[count:]
    b_refs, c_refs = [refs[i] for i in b_picks], [refs[i] for i in c_picks]
    gated_ref, square_ref, carry, c_rows, scores, carried, squares = refs[-7:]
    length, width = gate_ref.shape
    heads = factor_ref.shape[0] // (length // ROWS)
    groups, subs, pairs = SUB // ROWS, TILE // SUB, width // SUB
    size = carry.shape[0]
    entering = jnp.zeros(carry.shape, F32)
    for k in reversed(range(count)):
        end = others[k][...].astype(F32)
        longer = entering * end[size : size + 1] + end[:size]
        entering = jnp.where(jnp.bitwise_and(lax.axis_index("seq"), 1 << k) != 0, longer, entering)
    carry[...] = entering
    i = lax.broadcasted_iota(jnp.int32, (SUB, SUB), 0)
    j = lax.broadcasted_iota(jnp.int32, (SUB, SUB), 1)
    causal = i >= j
    low = (j < SUB // 2).astype(F32)
    keep_low, keep_high = low.astype(BF16), (1.0 - low).astype(BF16)

    def rows_times(value, load):
        rows = [value[g * ROWS : (g + 1) * ROWS] * load(g) for g in range(groups)]
        return jnp.concatenate(rows, axis=0)

    def repeated(ref, row):
        return jnp.broadcast_to(ref[pl.ds(row, 1)], (ROWS, SUB))

    local = [slice(s * SUB, (s + 1) * SUB) for s in range(subs)]

    def tile(t, _):
        whole = [pl.ds(pl.multiple_of(t * TILE + s * SUB, SUB), SUB) for s in range(subs)]
        row = pl.multiple_of(t * subs, subs)
        factors = pl.multiple_of(t * (subs * heads * groups), subs * heads * groups)
        starts = pl.multiple_of(t * (subs * groups), subs * groups)

        decays = before_ref[pl.ds(row, subs)]

        def turn(s):
            c_rows[local[s]] = columns_from(c_refs, c_rows_of, c_begins, t * TILE + s * SUB).T

        def products(s):
            b_cols = columns_of(b_refs, b_rows, whole[s])
            held = pl.ds(pl.multiple_of((t * subs + s) * size, size), size)
            state = local_ref[held] + carry[...] * decays[s : s + 1]
            both = jnp.dot(
                c_rows[local[s]],
                jnp.concatenate([b_cols, state.astype(BF16)], axis=1),
                preferred_element_type=F32,
            )
            scores[local[s]] = jnp.where(causal, both[:, :SUB], 0.0)
            carried[local[s]] = both[:, SUB:]

        turn(0)
        turn(1)
        products(0)
        for s, at in enumerate(whole):
            if s + 2 < subs:
                turn(s + 2)
            if s + 1 < subs:
                products(s + 1)
            total = None
            score = scores[local[s]]
            for p in range(pairs):
                cols = slice(p * SUB, (p + 1) * SUB)
                mixing = []
                for h in (2 * p, 2 * p + 1):
                    base = factors + (s * heads + h) * groups
                    mixing.append(rows_times(score, lambda g: repeated(factor_ref, base + g)).astype(BF16))
                xs = xs_ref[at, cols]
                mixed = jnp.dot(
                    jnp.concatenate(mixing, axis=1),
                    jnp.concatenate([xs * keep_low, xs * keep_high], axis=0),
                    preferred_element_type=F32,
                )
                base = starts + s * groups
                before = rows_times(carried[local[s], cols], lambda g: repeated(start_ref.at[p], base + g))
                gated = gate_ref[at, cols] * (mixed + before)
                gated_ref[at, cols] = gated.astype(BF16)
                square = gated * gated
                total = square if total is None else total + square
            squares[local[s]] = total.astype(BF16)
        sums = lax.dot_general(
            jnp.ones((8, SUB), BF16), squares[...], (((1,), (1,)), ((), ())), preferred_element_type=F32
        )
        square_ref[pl.ds(row, subs)] = jnp.concatenate([sums[:1, at] for at in local], axis=0)
        return 0

    lax.fori_loop(*span, tile, 0)


def scan(span, gate, factor, start, xs, local, before, others, b_pieces, b_rows, c_pieces, c_rows, c_begins, filled=()):
    length, width = xs.shape
    size = sum(last - first for first, last in b_rows)
    pieces = []
    for piece in b_pieces + c_pieces:
        if not any(piece is other for other in pieces):
            pieces.append(piece)
    picks = lambda some: [next(i for i, q in enumerate(pieces) if q is p) for p in some]
    operands = [gate, factor, start, xs, local, before, *others, *pieces, *filled]
    first = len(operands) - len(filled)
    return pl.pallas_call(
        functools.partial(
            scan_kernel, span, len(others), b_rows, picks(b_pieces), c_rows, picks(c_pieces), c_begins
        ),
        in_specs=[IN_VMEM] * len(operands),
        out_specs=[IN_VMEM, IN_VMEM],
        out_shape=[pltpu.VMEM((length, width), BF16), pltpu.VMEM((length // SUB, SUB), F32)],
        scratch_shapes=[
            pltpu.VMEM((size, width), F32),
            pltpu.VMEM((TILE, size), BF16),
            pltpu.VMEM((TILE, SUB), F32),
            pltpu.VMEM((TILE, width), F32),
            pltpu.VMEM((TILE, SUB), BF16),
        ],
        input_output_aliases={first + i: i for i in range(len(filled))},
        compiler_params=params(),
        cost_estimate=BRIEF,
        name="scan",
    )(*in_vmem(operands))


def norm_kernel(channels, gated_ref, gain_ref, *refs):
    squares, (out_ref, rows, sems) = refs[:-3], refs[-3:]
    total = squares[0][...]
    for ref in squares[1:]:
        total = total + ref[...]
    scale = lax.rsqrt(total * (1.0 / channels) + 1e-05).T
    gain = gain_ref[...]
    step = TILE // 2
    copies = []
    for t in range(gated_ref.shape[0] // step):
        for s in range(t * step // SUB, (t + 1) * step // SUB):
            at = slice(s * SUB, (s + 1) * SUB)
            rows[at] = (gated_ref[at].astype(F32) * scale[:, s : s + 1] * gain).astype(BF16)
        at = slice(t * step, (t + 1) * step)
        copies.append(pltpu.make_async_copy(rows.at[at], out_ref.at[at], sems.at[t]))
        copies[-1].start()
    for copy in copies:
        copy.wait()


def norm(channels, gated, gain, squares):
    length, width = gated.shape
    operands = [gated, gain, *squares]
    return pl.pallas_call(
        functools.partial(norm_kernel, channels),
        in_specs=[IN_VMEM] * len(operands),
        out_specs=ANYWHERE,
        out_shape=pltpu.HBM((length, width), BF16),
        scratch_shapes=[
            pltpu.VMEM((length, width), BF16),
            pltpu.SemaphoreType.DMA((2 * length // TILE,)),
        ],
        compiler_params=params(),
        cost_estimate=BRIEF,
        name="norm",
    )(*in_vmem(operands))


def body(x_rows, z_rows, b_rows, c_rows, step_raw, conv_x, conv_b, conv_c, decay_rate, norm_gain):
    length, width = x_rows.shape
    local_heads = decay_rate.shape[0]
    seq, heads = lax.axis_size("seq"), lax.axis_size("head")
    b_cols, c_cols = b_rows.T, c_rows.T
    ends, b_cols, c_cols = tails(x_rows, b_cols, c_cols)
    halo = lax.ppermute(ends, "seq", [(i, i + 1) for i in range(seq - 1)])
    bs, cs, cs_sent = shared_conv(b_cols, c_cols, halo, conv_b.T.astype(F32), conv_c.T.astype(F32))
    cols = bs.shape[0]
    outer, _ = factors(heads)
    tiles = x_rows.shape[0] // TILE
    q, columns, decays = rows_of(step_raw.T, decay_rate[:, None], width)
    conv = functools.partial(head_conv, x_rows, halo, conv_x.astype(F32), columns, local_heads)
    if cols % 16 or factors(heads) != (4, 2):
        b_pieces, c_pieces = [
            [jnp.concatenate(near + along_inner(near), axis=0)]
            for near in ([own] + along_outer(own) for own in (bs, cs))
        ]
        b_rows = c_rows = [(0, b_pieces[0].shape[0])]
        xs, weighted = conv(0, tiles)
        mine, local, before = last_state(weighted, decays, b_pieces, b_rows)
        gate, factor, start = gates(z_rows, columns, q, local_heads)
        token, tail, runs = mine, [], [((0, tiles), None, None)]
    else:
        one, two = (0, cols), (0, 2 * cols)
        b_outer, own = along_outer(bs), along_inner([bs])
        xs, weighted = conv(0, tiles)
        (b_packed,) = pack(b_outer, [one] * 3, xs, *own)
        b_passed = along_inner([b_packed])
        cs_sent, columns = after([cs_sent, columns], b_packed)
        c_outer = along_outer(cs_sent)
        gate, factor, start = gates(z_rows, columns, q, local_heads)
        (c_first,) = pack([cs, c_outer[0]], [one] * 2, start)
        c_passed = along_inner([c_first])
        (decays,) = after([decays], c_first)
        b_pieces = [bs, *own, *b_outer, *b_passed]
        b_rows = [one] * 5 + [(0, 3 * cols)]
        mine, local, before = last_state(weighted, decays, b_pieces, b_rows)
        cut = -(-tiles // 2) * TILE
        c_rest = pack(c_outer[1:], [one] * 2, mine, cuts=[0, cut, length])
        c_ends = along_inner(c_rest)
        c_pieces = [cs, *c_passed, *c_outer, *c_passed]
        c_rows = [one] * 5 + [(cols, 2 * cols)]
        token, tail = c_rest[0], [two]
        runs = [((0, cut // TILE), c_ends[0], 0), ((cut // TILE, tiles), c_ends[1], cut)]
    others, bit = [], 1
    while bit < seq:
        last = 2 * bit == seq
        pairs = [(i, i ^ bit) for i in range(seq) if not (last and i & bit)]
        others.append(lax.ppermute(mine, "seq", pairs))
        if not last:
            mine = join(bit, mine, others[-1], token)
        bit *= 2
    filled = ()
    for span, piece, begin in runs:
        filled = scan(
            span, gate, factor, start, xs, local, before, others, b_pieces, b_rows,
            c_pieces + [piece] * len(tail), c_rows + tail, [0] * len(c_pieces) + [begin], filled,
        )
    gated, square = filled
    square = square + sum(along_outer(square))
    squares = [square] + along_inner([square])
    return norm(heads * width, gated, norm_gain[None, :], squares)


def solution(mesh):
    placed = (
        P("seq", "head"),
        P("seq", "head"),
        P("seq", "head"),
        P("seq", "head"),
        P("seq", "head"),
        P(None, "head"),
        P(None, "head"),
        P(None, "head"),
        P("head"),
        P("head"),
    )
    return jax.shard_map(
        body, mesh=mesh, in_specs=placed, out_specs=P("seq", "head"), check_vma=False
    )
```

```python
import functools
import math

import jax
import jax.numpy as jnp
from jax import lax
from jax.experimental import pallas as pl
from jax.experimental.pallas import tpu as pltpu
from jax.sharding import PartitionSpec as P

SUB = 128
ROWS = 16
TILE = 8 * SUB
LOG2E = math.log2(math.e)
MIB = 1024 * 1024
F32, BF16 = jnp.float32, jnp.bfloat16


def params(mib=16):
    return pltpu.CompilerParams(vmem_limit_bytes=mib * MIB)


def in_hbm(value):
    return pltpu.with_memory_space_constraint(value, pltpu.HBM)


def in_vmem(values):
    return [pltpu.with_memory_space_constraint(value, pltpu.VMEM) for value in values]


IN_VMEM = pl.BlockSpec(memory_space=pltpu.VMEM)
BRIEF = pl.CostEstimate(flops=1000, bytes_accessed=1000, transcendentals=0)
ANYWHERE = pl.BlockSpec(memory_space=pl.ANY)


def silu(value):
    half = 0.5 * value
    return half * jnp.tanh(half) + half


def factors(count):
    inner = max(d for d in range(1, math.isqrt(count) + 1) if count % d == 0)
    return count // inner, inner


def outer_pairs(d):
    outer, inner = factors(lax.axis_size("head"))
    return [(z * inner + y, (z + d) % outer * inner + y) for z in range(outer) for y in range(inner)]


def inner_pairs(e):
    outer, inner = factors(lax.axis_size("head"))
    return [(z * inner + y, z * inner + (y + e) % inner) for z in range(outer) for y in range(inner)]


def along_outer(piece):
    outer, _ = factors(lax.axis_size("head"))
    return [lax.ppermute(piece, "head", outer_pairs(d)) for d in range(1, outer)]


def along_inner(pieces):
    _, inner = factors(lax.axis_size("head"))
    return [lax.ppermute(p, "head", inner_pairs(e)) for e in range(1, inner) for p in pieces]


def tie_kernel(*refs):
    pass


def after(values, *tokens):
    out = pl.pallas_call(
        tie_kernel,
        in_specs=[ANYWHERE] * (len(values) + len(tokens)),
        out_specs=[ANYWHERE] * len(values),
        out_shape=[jax.ShapeDtypeStruct(v.shape, v.dtype) for v in values],
        input_output_aliases={i: i for i in range(len(values))},
        compiler_params=params(1),
        cost_estimate=BRIEF,
        name="tie",
    )(*values, *tokens)
    return list(out)


def pack_kernel(rows, cuts, *refs):
    outs = refs[len(refs) - len(cuts) + 1 :]
    for out_ref, first_token, last_token in zip(outs, cuts[:-1], cuts[1:]):
        row = 0
        for ref, (first, last) in zip(refs, rows):
            out_ref[row : row + last - first] = ref[first:last, first_token:last_token]
            row += last - first


def pack(pieces, rows, *tokens, cuts=None):
    cuts = cuts or [0, pieces[0].shape[1]]
    count = sum(last - first for first, last in rows)
    return pl.pallas_call(
        functools.partial(pack_kernel, rows, cuts),
        in_specs=[IN_VMEM] * len(pieces) + [ANYWHERE] * len(tokens),
        out_specs=[IN_VMEM] * (len(cuts) - 1),
        out_shape=[
            pltpu.VMEM((count, last - first), pieces[0].dtype) for first, last in zip(cuts[:-1], cuts[1:])
        ],
        compiler_params=params(),
        cost_estimate=BRIEF,
        name="pack",
    )(*in_vmem(pieces), *tokens)


def tails_kernel(x_ref, b_ref, c_ref, out_ref, b_out, c_out):
    cols, length = b_ref.shape
    out_ref[...] = jnp.zeros_like(out_ref)
    out_ref[:16] = x_ref[...]
    out_ref[16 : 16 + cols, :SUB] = b_ref[:, length - SUB :]
    out_ref[32 : 32 + cols, :SUB] = c_ref[:, length - SUB :]
    b_out[...] = b_ref[...]
    c_out[...] = c_ref[...]


def tails(x_rows, b_cols, c_cols):
    length, width = x_rows.shape
    cols = b_cols.shape[0]
    whole = pl.BlockSpec((cols, length), lambda i: (0, 0))
    held = pltpu.VMEM((cols, length), BF16)
    return pl.pallas_call(
        tails_kernel,
        grid=(1,),
        in_specs=[pl.BlockSpec((16, width), lambda i: (length // 16 - 1, 0)), whole, whole],
        out_specs=[pl.BlockSpec((48, width), lambda i: (0, 0)), IN_VMEM, IN_VMEM],
        out_shape=[jax.ShapeDtypeStruct((48, width), BF16), held, held],
        compiler_params=params(),
        cost_estimate=BRIEF,
        name="tails",
    )(in_hbm(x_rows), in_hbm(b_cols), in_hbm(c_cols))


def conv_columns(rows, halo, taps):
    wide = jnp.concatenate([halo, rows], axis=1).astype(F32)
    width = taps.shape[1]
    total = None
    for k in range(width):
        lag = width - 1 - k
        moved = pltpu.roll(wide, lag, axis=1) if lag else wide
        term = taps[:, k : k + 1] * moved[:, SUB:]
        total = term if total is None else total + term
    return silu(total).astype(BF16)


def shared_conv_kernel(b_ref, c_ref, halo_ref, tb_ref, tc_ref, bs_ref, cs_ref, again_ref):
    cols = b_ref.shape[0]
    bs_ref[...] = conv_columns(b_ref[...], halo_ref[16 : 16 + cols, :SUB], tb_ref[...])
    cs = conv_columns(c_ref[...], halo_ref[32 : 32 + cols, :SUB], tc_ref[...])
    cs_ref[...], again_ref[...] = cs, cs


def shared_conv(b_cols, c_cols, halo, taps_b, taps_c):
    operands = [b_cols, c_cols, halo, taps_b, taps_c]
    return pl.pallas_call(
        shared_conv_kernel,
        in_specs=[IN_VMEM] * 5,
        out_specs=[IN_VMEM] * 3,
        out_shape=[pltpu.VMEM(b_cols.shape, BF16)] * 3,
        compiler_params=params(),
        cost_estimate=BRIEF,
        name="shared_conv",
    )(*in_vmem(operands))


def parts_of(value, count):
    parts = []
    for _ in range(count):
        part = value.astype(BF16).astype(F32)
        parts.append(part)
        value = value - part
    return jnp.concatenate(parts, axis=0)


def spread_matrix(first, last, count, width, size):
    i = lax.broadcasted_iota(jnp.int32, (count, width), 0)
    j = lax.broadcasted_iota(jnp.int32, (count, width), 1)
    head = jnp.bitwise_and(i, 7) * size
    lanes = jnp.logical_and(j >= head, j < head + size)
    return jnp.logical_and(lanes, jnp.logical_and(i >= first, i < last)).astype(F32).astype(BF16)


def rows_kernel(step_ref, rate_ref, q_ref, column_ref, decay_ref, sp, ld):
    heads, length = step_ref.shape
    width = decay_ref.shape[1]
    subs = length // SUB
    raw = step_ref[...]
    soft = jnp.maximum(raw, 0.0) + jnp.log(1.0 + jnp.exp(-jnp.abs(raw)))
    sp[...] = jnp.ones_like(sp)
    ld[...] = jnp.zeros_like(ld)
    sp[:heads] = soft
    ld[:heads] = soft * (rate_ref[...] * -LOG2E)
    i = lax.broadcasted_iota(jnp.int32, (SUB, SUB), 0)
    j = lax.broadcasted_iota(jnp.int32, (SUB, SUB), 1)
    upper = (i <= j).astype(F32)
    logs = ld[...]
    stacked = jnp.concatenate([logs[:, s * SUB : (s + 1) * SUB] for s in range(subs)], axis=0)
    sums = jnp.dot(stacked, upper, precision=lax.Precision.HIGHEST, preferred_element_type=F32)
    log_step = jnp.log(sp[...]) * LOG2E
    lasts = []
    for s in range(subs):
        at = slice(s * SUB, (s + 1) * SUB)
        cum = sums[s * 8 : (s + 1) * 8]
        q = cum - log_step[:, at]
        q_ref[:, at] = q
        weight = jnp.exp2(cum[:, SUB - 1 :] - q)
        columns = jnp.concatenate([parts_of(weight, 2), parts_of(cum, 3)], axis=0).T
        column_ref[at] = columns.astype(BF16)
        lasts.append(columns[SUB - 1 :])
    whole = jnp.concatenate(lasts, axis=0).astype(BF16)
    to_lanes = spread_matrix(16, 40, 40, width, width // heads)
    decay_ref[...] = jnp.exp2(jnp.dot(whole, to_lanes, preferred_element_type=F32))


def rows_of(steps, rates, width):
    heads, length = steps.shape
    return pl.pallas_call(
        rows_kernel,
        in_specs=[IN_VMEM] * 2,
        out_specs=[IN_VMEM] * 3,
        out_shape=[
            pltpu.VMEM((8, length), F32),
            pltpu.VMEM((length, 40), BF16),
            pltpu.VMEM((length // SUB, width), F32),
        ],
        scratch_shapes=[pltpu.VMEM((8, length), F32), pltpu.VMEM((8, length), F32)],
        compiler_params=params(),
        cost_estimate=BRIEF,
        name="rows",
    )(*in_vmem([steps, rates]))


def head_conv_kernel(first, heads, x_ref, before_ref, halo_ref, taps_ref, column_ref, *refs):
    xs_ref, wt_ref, ext, spread = refs[-4:]
    length, width = x_ref.shape
    taps = taps_ref.shape[0]
    pairs = width // SUB

    @pl.when(pl.program_id(0) == 0)
    def _():
        for p in range(pairs):
            rows = before_ref if first else halo_ref
            ext[p, :8] = rows[8:16, p * SUB : (p + 1) * SUB].astype(F32)

    for p in range(pairs):
        ext[p, 8:] = x_ref[:, p * SUB : (p + 1) * SUB].astype(F32)
    count = column_ref.shape[1]
    spread[...] = jnp.dot(
        column_ref[...],
        spread_matrix(0, 16, count, width, width // heads),
        preferred_element_type=F32,
    )
    for s in range(length // SUB):
        at = slice(s * SUB, (s + 1) * SUB)
        for p in range(pairs):
            cols = slice(p * SUB, (p + 1) * SUB)
            total = None
            for k in range(taps):
                start = 8 - (taps - 1) + k + s * SUB
                term = taps_ref[k : k + 1, cols] * ext[p, start : start + SUB]
                total = term if total is None else total + term
            xs = silu(total).astype(BF16)
            xs_ref[at, cols] = xs
            wt_ref[at, cols] = (spread[at, cols] * xs.astype(F32)).astype(BF16)
    for p in range(pairs):
        ext[p, :8] = ext[p, length : length + 8]


def head_conv(x_rows, halo, taps, columns, heads, first, count, filled=()):
    length, width = x_rows.shape
    wide = pl.BlockSpec((TILE, width), lambda i: (first + i, 0))
    whole = lambda a: pl.BlockSpec(a.shape, lambda i: (0, 0))
    return pl.pallas_call(
        functools.partial(head_conv_kernel, first, heads),
        grid=(count,),
        in_specs=[
            wide,
            pl.BlockSpec((16, width), lambda i: (max(first * TILE // 16 - 1, 0), 0)),
            whole(halo),
            whole(taps),
            pl.BlockSpec((TILE, columns.shape[1]), lambda i: (first + i, 0)),
        ]
        + [ANYWHERE] * len(filled),
        out_specs=[wide, wide],
        out_shape=[jax.ShapeDtypeStruct((length, width), BF16)] * 2,
        scratch_shapes=[
            pltpu.VMEM((width // SUB, TILE + 8, SUB), F32),
            pltpu.VMEM((TILE, width), F32),
        ],
        compiler_params=params(),
        input_output_aliases={5 + i: i for i in range(len(filled))},
        cost_estimate=BRIEF,
        name="head_conv",
    )(in_hbm(x_rows), in_hbm(x_rows), halo, taps, columns, *filled)


def gates_kernel(z_ref, column_ref, q_ref, gate_ref, factor_ref, start_ref, spread):
    length, width = z_ref.shape
    heads = factor_ref.shape[0] // (length // ROWS)
    size = width // heads
    subs, groups = length // SUB, SUB // ROWS
    columns = column_ref[...]
    to_lanes = spread_matrix(16, 40, columns.shape[1], width, size)
    for p in range(width // SUB):
        spread[p] = jnp.dot(
            columns, to_lanes[:, p * SUB : (p + 1) * SUB], preferred_element_type=F32
        )
    for s in range(subs):
        at = slice(s * SUB, (s + 1) * SUB)
        starts = []
        for p in range(width // SUB):
            cols = slice(p * SUB, (p + 1) * SUB)
            cum = spread[p, at].reshape(groups, ROWS // 8, 8, SUB)
            grown = jnp.exp2(cum - cum[:, ROWS // 16 : ROWS // 16 + 1, :1]).reshape(SUB, SUB)
            gate_ref[at, cols] = grown * silu(z_ref[at, cols].astype(F32))
            start = spread[p, pl.ds(s * SUB + ROWS // 2, groups, stride=ROWS)]
            start_ref[p, s * groups : (s + 1) * groups] = jnp.exp2(start)
            starts.append(start)
        for h in range(heads):
            lane = h * size % SUB
            start = jnp.broadcast_to(starts[h * size // SUB][:, lane : lane + 1], (groups, SUB))
            row = (s * heads + h) * groups
            factor_ref[row : row + groups] = jnp.exp2(
                jnp.minimum(start - q_ref[h : h + 1, at], 64.0)
            )


def gates(z_rows, columns, q, heads):
    length, width = z_rows.shape
    wide = pl.BlockSpec((TILE, width), lambda i: (i, 0))
    rows = pl.BlockSpec((8, TILE), lambda i: (0, i))
    return pl.pallas_call(
        gates_kernel,
        grid=(length // TILE,),
        in_specs=[wide, pl.BlockSpec((TILE, columns.shape[1]), lambda i: (i, 0)), rows],
        out_specs=[
            wide,
            pl.BlockSpec((TILE // ROWS * heads, SUB), lambda i: (i, 0)),
            pl.BlockSpec((width // SUB, TILE // ROWS, SUB), lambda i: (0, i, 0)),
        ],
        out_shape=[
            jax.ShapeDtypeStruct((length, width), F32),
            jax.ShapeDtypeStruct((length // ROWS * heads, SUB), F32),
            jax.ShapeDtypeStruct((width // SUB, length // ROWS, SUB), F32),
        ],
        scratch_shapes=[pltpu.VMEM((width // SUB, TILE, SUB), F32)],
        compiler_params=params(),
        cost_estimate=BRIEF,
        name="gates",
    )(z_rows, columns, q)


def columns_of(refs, rows, at):
    return jnp.concatenate([ref[first:last, at] for ref, (first, last) in zip(refs, rows)], axis=0)


def columns_from(refs, rows, begins, start):
    parts = [
        ref[first:last, pl.ds(pl.multiple_of(start - begin, SUB), SUB)]
        for ref, (first, last), begin in zip(refs, rows, begins)
    ]
    return jnp.concatenate(parts, axis=0)


def last_state_kernel(rows, wt_ref, decay_ref, *refs):
    pieces, (out_ref, local_ref, before_ref, state, total) = refs[:-5], refs[-5:]
    size = state.shape[0]
    subs = TILE // SUB
    state[...] = jnp.zeros_like(state)
    total[...] = jnp.ones_like(total)

    def tile(t, _):
        held, grown = state[...], total[:1]
        row = pl.multiple_of(t * subs, subs)
        decays = decay_ref[pl.ds(row, subs)]
        products = []
        for s in range(subs):
            at = pl.ds(pl.multiple_of(t * TILE + s * SUB, SUB), SUB)
            b_cols = columns_of(pieces, rows, at)
            added = jnp.dot(b_cols, wt_ref[at], preferred_element_type=F32)
            local_ref[pl.ds(pl.multiple_of((t * subs + s) * size, size), size)] = held
            products.append(grown)
            held = held * decays[s : s + 1] + added
            grown = grown * decays[s : s + 1]
        before_ref[pl.ds(row, subs)] = jnp.concatenate(products, axis=0)
        state[...] = held
        total[...] = jnp.broadcast_to(grown, total.shape)
        return 0

    lax.fori_loop(0, wt_ref.shape[0] // TILE, tile, 0)
    out_ref[:size] = state[...].astype(BF16)
    out_ref[size:] = jnp.broadcast_to(total[:1], (16, total.shape[1])).astype(BF16)


def last_state(weighted, decays, pieces, rows):
    length, width = weighted.shape
    size = sum(last - first for first, last in rows)
    count = length // SUB
    return pl.pallas_call(
        functools.partial(last_state_kernel, rows),
        in_specs=[IN_VMEM] * (2 + len(pieces)),
        out_specs=[IN_VMEM] * 3,
        out_shape=[
            jax.ShapeDtypeStruct((size + 16, width), BF16),
            pltpu.VMEM((count * size, width), F32),
            pltpu.VMEM((count, width), F32),
        ],
        scratch_shapes=[pltpu.VMEM((size, width), F32), pltpu.VMEM((8, width), F32)],
        compiler_params=params(),
        cost_estimate=BRIEF,
        name="last_state",
    )(*in_vmem([weighted, decays, *pieces]))


def join_kernel(bit, mine_ref, other_ref, token_ref, out_ref):
    size = mine_ref.shape[0] - 16
    upper = jnp.bitwise_and(lax.axis_index("seq"), bit) != 0
    mine, other = mine_ref[...].astype(F32), other_ref[...].astype(F32)
    early, late = jnp.where(upper, other, mine), jnp.where(upper, mine, other)
    decay = late[size : size + 1]
    out_ref[:size] = (early[:size] * decay + late[:size]).astype(BF16)
    out_ref[size:] = (early[size:] * decay).astype(BF16)


def join(bit, mine, other, token):
    return pl.pallas_call(
        functools.partial(join_kernel, bit),
        in_specs=[IN_VMEM, IN_VMEM, ANYWHERE],
        out_specs=IN_VMEM,
        out_shape=jax.ShapeDtypeStruct(mine.shape, BF16),
        compiler_params=params(),
        cost_estimate=BRIEF,
        name="join",
    )(*in_vmem([mine, other]), token)


def scan_kernel(
    span, count, b_rows, b_picks, c_rows_of, c_picks, c_begins, gate_ref, factor_ref, start_ref, xs_ref,
    local_ref, before_ref, *refs
):
    others, refs = refs[:count], refs[count:]
    b_refs, c_refs = [refs[i] for i in b_picks], [refs[i] for i in c_picks]
    gated_ref, square_ref, carry, c_rows, scores, carried, squares = refs[-7:]
    length, width = gate_ref.shape
    heads = factor_ref.shape[0] // (length // ROWS)
    groups, subs, pairs = SUB // ROWS, TILE // SUB, width // SUB
    size = carry.shape[0]
    entering = jnp.zeros(carry.shape, F32)
    for k in reversed(range(count)):
        end = others[k][...].astype(F32)
        longer = entering * end[size : size + 1] + end[:size]
        entering = jnp.where(jnp.bitwise_and(lax.axis_index("seq"), 1 << k) != 0, longer, entering)
    carry[...] = entering
    i = lax.broadcasted_iota(jnp.int32, (SUB, SUB), 0)
    j = lax.broadcasted_iota(jnp.int32, (SUB, SUB), 1)
    causal = i >= j
    low = (j < SUB // 2).astype(F32)
    keep_low, keep_high = low.astype(BF16), (1.0 - low).astype(BF16)

    def rows_times(value, load):
        rows = [value[g * ROWS : (g + 1) * ROWS] * load(g) for g in range(groups)]
        return jnp.concatenate(rows, axis=0)

    def repeated(ref, row):
        return jnp.broadcast_to(ref[pl.ds(row, 1)], (ROWS, SUB))

    local = [slice(s * SUB, (s + 1) * SUB) for s in range(subs)]

    def tile(t, _):
        whole = [pl.ds(pl.multiple_of(t * TILE + s * SUB, SUB), SUB) for s in range(subs)]
        row = pl.multiple_of(t * subs, subs)
        factors = pl.multiple_of(t * (subs * heads * groups), subs * heads * groups)
        starts = pl.multiple_of(t * (subs * groups), subs * groups)

        decays = before_ref[pl.ds(row, subs)]

        def turn(s):
            c_rows[local[s]] = columns_from(c_refs, c_rows_of, c_begins, t * TILE + s * SUB).T

        def products(s):
            b_cols = columns_of(b_refs, b_rows, whole[s])
            held = pl.ds(pl.multiple_of((t * subs + s) * size, size), size)
            state = local_ref[held] + carry[...] * decays[s : s + 1]
            both = jnp.dot(
                c_rows[local[s]],
                jnp.concatenate([b_cols, state.astype(BF16)], axis=1),
                preferred_element_type=F32,
            )
            scores[local[s]] = jnp.where(causal, both[:, :SUB], 0.0)
            carried[local[s]] = both[:, SUB:]

        turn(0)
        turn(1)
        products(0)
        for s, at in enumerate(whole):
            if s + 2 < subs:
                turn(s + 2)
            if s + 1 < subs:
                products(s + 1)
            total = None
            score = scores[local[s]]
            for p in range(pairs):
                cols = slice(p * SUB, (p + 1) * SUB)
                mixing = []
                for h in (2 * p, 2 * p + 1):
                    base = factors + (s * heads + h) * groups
                    mixing.append(rows_times(score, lambda g: repeated(factor_ref, base + g)).astype(BF16))
                xs = xs_ref[at, cols]
                mixed = jnp.dot(
                    jnp.concatenate(mixing, axis=1),
                    jnp.concatenate([xs * keep_low, xs * keep_high], axis=0),
                    preferred_element_type=F32,
                )
                base = starts + s * groups
                before = rows_times(carried[local[s], cols], lambda g: repeated(start_ref.at[p], base + g))
                gated = gate_ref[at, cols] * (mixed + before)
                gated_ref[at, cols] = gated.astype(BF16)
                square = gated * gated
                total = square if total is None else total + square
            squares[local[s]] = total.astype(BF16)
        sums = lax.dot_general(
            jnp.ones((8, SUB), BF16), squares[...], (((1,), (1,)), ((), ())), preferred_element_type=F32
        )
        square_ref[pl.ds(row, subs)] = jnp.concatenate([sums[:1, at] for at in local], axis=0)
        return 0

    lax.fori_loop(*span, tile, 0)


def scan(span, gate, factor, start, xs, local, before, others, b_pieces, b_rows, c_pieces, c_rows, c_begins, filled=()):
    length, width = xs.shape
    size = sum(last - first for first, last in b_rows)
    pieces = []
    for piece in b_pieces + c_pieces:
        if not any(piece is other for other in pieces):
            pieces.append(piece)
    picks = lambda some: [next(i for i, q in enumerate(pieces) if q is p) for p in some]
    operands = [gate, factor, start, xs, local, before, *others, *pieces, *filled]
    first = len(operands) - len(filled)
    return pl.pallas_call(
        functools.partial(
            scan_kernel, span, len(others), b_rows, picks(b_pieces), c_rows, picks(c_pieces), c_begins
        ),
        in_specs=[IN_VMEM] * len(operands),
        out_specs=[IN_VMEM, IN_VMEM],
        out_shape=[pltpu.VMEM((length, width), BF16), pltpu.VMEM((length // SUB, SUB), F32)],
        scratch_shapes=[
            pltpu.VMEM((size, width), F32),
            pltpu.VMEM((TILE, size), BF16),
            pltpu.VMEM((TILE, SUB), F32),
            pltpu.VMEM((TILE, width), F32),
            pltpu.VMEM((TILE, SUB), BF16),
        ],
        input_output_aliases={first + i: i for i in range(len(filled))},
        compiler_params=params(),
        cost_estimate=BRIEF,
        name="scan",
    )(*in_vmem(operands))


def norm_kernel(channels, gated_ref, gain_ref, *refs):
    squares, (out_ref, rows, sems) = refs[:-3], refs[-3:]
    total = squares[0][...]
    for ref in squares[1:]:
        total = total + ref[...]
    scale = lax.rsqrt(total * (1.0 / channels) + 1e-05).T
    gain = gain_ref[...]
    step = TILE // 2
    copies = []
    for t in range(gated_ref.shape[0] // step):
        for s in range(t * step // SUB, (t + 1) * step // SUB):
            at = slice(s * SUB, (s + 1) * SUB)
            rows[at] = (gated_ref[at].astype(F32) * scale[:, s : s + 1] * gain).astype(BF16)
        at = slice(t * step, (t + 1) * step)
        copies.append(pltpu.make_async_copy(rows.at[at], out_ref.at[at], sems.at[t]))
        copies[-1].start()
    for copy in copies:
        copy.wait()


def norm(channels, gated, gain, squares):
    length, width = gated.shape
    operands = [gated, gain, *squares]
    return pl.pallas_call(
        functools.partial(norm_kernel, channels),
        in_specs=[IN_VMEM] * len(operands),
        out_specs=ANYWHERE,
        out_shape=pltpu.HBM((length, width), BF16),
        scratch_shapes=[
            pltpu.VMEM((length, width), BF16),
            pltpu.SemaphoreType.DMA((2 * length // TILE,)),
        ],
        compiler_params=params(),
        cost_estimate=BRIEF,
        name="norm",
    )(*in_vmem(operands))


def body(x_rows, z_rows, b_rows, c_rows, step_raw, conv_x, conv_b, conv_c, decay_rate, norm_gain):
    length, width = x_rows.shape
    local_heads = decay_rate.shape[0]
    seq, heads = lax.axis_size("seq"), lax.axis_size("head")
    b_cols, c_cols = b_rows.T, c_rows.T
    ends, b_cols, c_cols = tails(x_rows, b_cols, c_cols)
    halo = lax.ppermute(ends, "seq", [(i, i + 1) for i in range(seq - 1)])
    bs, cs, cs_sent = shared_conv(b_cols, c_cols, halo, conv_b.T.astype(F32), conv_c.T.astype(F32))
    cols = bs.shape[0]
    outer, _ = factors(heads)
    tiles = x_rows.shape[0] // TILE
    q, columns, decays = rows_of(step_raw.T, decay_rate[:, None], width)
    conv = functools.partial(head_conv, x_rows, halo, conv_x.astype(F32), columns, local_heads)
    if cols % 16 or factors(heads) != (4, 2):
        b_pieces, c_pieces = [
            [jnp.concatenate(near + along_inner(near), axis=0)]
            for near in ([own] + along_outer(own) for own in (bs, cs))
        ]
        b_rows = c_rows = [(0, b_pieces[0].shape[0])]
        xs, weighted = conv(0, tiles)
        mine, local, before = last_state(weighted, decays, b_pieces, b_rows)
        gate, factor, start = gates(z_rows, columns, q, local_heads)
        token, tail, runs = mine, [], [((0, tiles), None, None)]
    else:
        one, two = (0, cols), (0, 2 * cols)
        b_outer, own, c_own = along_outer(bs), along_inner([bs]), along_inner([cs])
        xs, weighted = conv(0, tiles)
        (b_packed,) = pack(b_outer, [one] * 3, xs, *own, *c_own)
        b_passed = along_inner([b_packed])
        cs_sent, columns = after([cs_sent, columns], b_packed)
        c_outer = along_outer(cs_sent)
        gate, factor, start = gates(z_rows, columns, q, local_heads)
        c_outer[:1] = after(c_outer[:1], start)
        c_passed = c_own + along_inner(c_outer[:1])
        (decays,) = after([decays], c_outer[0])
        b_pieces = [bs, *own, *b_outer, *b_passed]
        b_rows = [one] * 5 + [(0, 3 * cols)]
        mine, local, before = last_state(weighted, decays, b_pieces, b_rows)
        cut = -(-tiles // 2) * TILE
        c_rest = pack(c_outer[1:], [one] * 2, mine, c_passed[1], cuts=[0, cut, length])
        c_ends = along_inner(c_rest)
        c_pieces = [cs, *c_own, *c_outer, c_passed[1]]
        c_rows = [one] * 6
        token, tail = c_rest[0], [two]
        runs = [((0, cut // TILE), c_ends[0], 0), ((cut // TILE, tiles), c_ends[1], cut)]
    others, bit = [], 1
    while bit < seq:
        last = 2 * bit == seq
        pairs = [(i, i ^ bit) for i in range(seq) if not (last and i & bit)]
        others.append(lax.ppermute(mine, "seq", pairs))
        if not last:
            mine = join(bit, mine, others[-1], token)
        bit *= 2
    filled = ()
    for span, piece, begin in runs:
        filled = scan(
            span, gate, factor, start, xs, local, before, others, b_pieces, b_rows,
            c_pieces + [piece] * len(tail), c_rows + tail, [0] * len(c_pieces) + [begin], filled,
        )
    gated, square = filled
    square = square + sum(along_outer(square))
    squares = [square] + along_inner([square])
    return norm(heads * width, gated, norm_gain[None, :], squares)


def solution(mesh):
    placed = (
        P("seq", "head"),
        P("seq", "head"),
        P("seq", "head"),
        P("seq", "head"),
        P("seq", "head"),
        P(None, "head"),
        P(None, "head"),
        P(None, "head"),
        P("head"),
        P("head"),
    )
    return jax.shard_map(
        body, mesh=mesh, in_specs=placed, out_specs=P("seq", "head"), check_vma=False
    )
```

```python
import functools
import math

import jax
import jax.numpy as jnp
from jax import lax
from jax.experimental import pallas as pl
from jax.experimental.pallas import tpu as pltpu
from jax.sharding import PartitionSpec as P

SUB = 128
ROWS = 16
TILE = 8 * SUB
LOG2E = math.log2(math.e)
MIB = 1024 * 1024
F32, BF16 = jnp.float32, jnp.bfloat16


def params(mib=16):
    return pltpu.CompilerParams(vmem_limit_bytes=mib * MIB)


def in_hbm(value):
    return pltpu.with_memory_space_constraint(value, pltpu.HBM)


def in_vmem(values):
    return [pltpu.with_memory_space_constraint(value, pltpu.VMEM) for value in values]


IN_VMEM = pl.BlockSpec(memory_space=pltpu.VMEM)
BRIEF = pl.CostEstimate(flops=1000, bytes_accessed=1000, transcendentals=0)
ANYWHERE = pl.BlockSpec(memory_space=pl.ANY)


def silu(value):
    half = 0.5 * value
    return half * jnp.tanh(half) + half


def factors(count):
    inner = max(d for d in range(1, math.isqrt(count) + 1) if count % d == 0)
    return count // inner, inner


def outer_pairs(d):
    outer, inner = factors(lax.axis_size("head"))
    return [(z * inner + y, (z + d) % outer * inner + y) for z in range(outer) for y in range(inner)]


def inner_pairs(e):
    outer, inner = factors(lax.axis_size("head"))
    return [(z * inner + y, z * inner + (y + e) % inner) for z in range(outer) for y in range(inner)]


def along_outer(piece):
    outer, _ = factors(lax.axis_size("head"))
    return [lax.ppermute(piece, "head", outer_pairs(d)) for d in range(1, outer)]


def along_inner(pieces):
    _, inner = factors(lax.axis_size("head"))
    return [lax.ppermute(p, "head", inner_pairs(e)) for e in range(1, inner) for p in pieces]


def tie_kernel(*refs):
    pass


def after(values, *tokens):
    out = pl.pallas_call(
        tie_kernel,
        in_specs=[ANYWHERE] * (len(values) + len(tokens)),
        out_specs=[ANYWHERE] * len(values),
        out_shape=[jax.ShapeDtypeStruct(v.shape, v.dtype) for v in values],
        input_output_aliases={i: i for i in range(len(values))},
        compiler_params=params(1),
        cost_estimate=BRIEF,
        name="tie",
    )(*values, *tokens)
    return list(out)


def pack_kernel(rows, cuts, *refs):
    outs = refs[len(refs) - len(cuts) + 1 :]
    for out_ref, first_token, last_token in zip(outs, cuts[:-1], cuts[1:]):
        row = 0
        for ref, (first, last) in zip(refs, rows):
            out_ref[row : row + last - first] = ref[first:last, first_token:last_token]
            row += last - first


def pack(pieces, rows, *tokens, cuts=None):
    cuts = cuts or [0, pieces[0].shape[1]]
    count = sum(last - first for first, last in rows)
    return pl.pallas_call(
        functools.partial(pack_kernel, rows, cuts),
        in_specs=[IN_VMEM] * len(pieces) + [ANYWHERE] * len(tokens),
        out_specs=[IN_VMEM] * (len(cuts) - 1),
        out_shape=[
            pltpu.VMEM((count, last - first), pieces[0].dtype) for first, last in zip(cuts[:-1], cuts[1:])
        ],
        compiler_params=params(),
        cost_estimate=BRIEF,
        name="pack",
    )(*in_vmem(pieces), *tokens)


def tails_kernel(x_ref, b_ref, c_ref, out_ref, b_out, c_out):
    cols, length = b_ref.shape
    out_ref[...] = jnp.zeros_like(out_ref)
    out_ref[:16] = x_ref[...]
    out_ref[16 : 16 + cols, :SUB] = b_ref[:, length - SUB :]
    out_ref[32 : 32 + cols, :SUB] = c_ref[:, length - SUB :]
    b_out[...] = b_ref[...]
    c_out[...] = c_ref[...]


def tails(x_rows, b_cols, c_cols):
    length, width = x_rows.shape
    cols = b_cols.shape[0]
    whole = pl.BlockSpec((cols, length), lambda i: (0, 0))
    held = pltpu.VMEM((cols, length), BF16)
    return pl.pallas_call(
        tails_kernel,
        grid=(1,),
        in_specs=[pl.BlockSpec((16, width), lambda i: (length // 16 - 1, 0)), whole, whole],
        out_specs=[pl.BlockSpec((48, width), lambda i: (0, 0)), IN_VMEM, IN_VMEM],
        out_shape=[jax.ShapeDtypeStruct((48, width), BF16), held, held],
        compiler_params=params(),
        cost_estimate=BRIEF,
        name="tails",
    )(in_hbm(x_rows), in_hbm(b_cols), in_hbm(c_cols))


def conv_columns(rows, halo, taps):
    wide = jnp.concatenate([halo, rows], axis=1).astype(F32)
    width = taps.shape[1]
    total = None
    for k in range(width):
        lag = width - 1 - k
        moved = pltpu.roll(wide, lag, axis=1) if lag else wide
        term = taps[:, k : k + 1] * moved[:, SUB:]
        total = term if total is None else total + term
    return silu(total).astype(BF16)


def shared_conv_kernel(b_ref, c_ref, halo_ref, tb_ref, tc_ref, bs_ref, cs_ref, again_ref):
    cols = b_ref.shape[0]
    bs_ref[...] = conv_columns(b_ref[...], halo_ref[16 : 16 + cols, :SUB], tb_ref[...])
    cs = conv_columns(c_ref[...], halo_ref[32 : 32 + cols, :SUB], tc_ref[...])
    cs_ref[...], again_ref[...] = cs, cs


def shared_conv(b_cols, c_cols, halo, taps_b, taps_c):
    operands = [b_cols, c_cols, halo, taps_b, taps_c]
    return pl.pallas_call(
        shared_conv_kernel,
        in_specs=[IN_VMEM] * 5,
        out_specs=[IN_VMEM] * 3,
        out_shape=[pltpu.VMEM(b_cols.shape, BF16)] * 3,
        compiler_params=params(),
        cost_estimate=BRIEF,
        name="shared_conv",
    )(*in_vmem(operands))


def parts_of(value, count):
    parts = []
    for _ in range(count):
        part = value.astype(BF16).astype(F32)
        parts.append(part)
        value = value - part
    return jnp.concatenate(parts, axis=0)


def spread_matrix(first, last, count, width, size):
    i = lax.broadcasted_iota(jnp.int32, (count, width), 0)
    j = lax.broadcasted_iota(jnp.int32, (count, width), 1)
    head = jnp.bitwise_and(i, 7) * size
    lanes = jnp.logical_and(j >= head, j < head + size)
    return jnp.logical_and(lanes, jnp.logical_and(i >= first, i < last)).astype(F32).astype(BF16)


def rows_kernel(step_ref, rate_ref, q_ref, column_ref, decay_ref, sp, ld):
    heads, length = step_ref.shape
    width = decay_ref.shape[1]
    subs = length // SUB
    raw = step_ref[...]
    soft = jnp.maximum(raw, 0.0) + jnp.log(1.0 + jnp.exp(-jnp.abs(raw)))
    sp[...] = jnp.ones_like(sp)
    ld[...] = jnp.zeros_like(ld)
    sp[:heads] = soft
    ld[:heads] = soft * (rate_ref[...] * -LOG2E)
    i = lax.broadcasted_iota(jnp.int32, (SUB, SUB), 0)
    j = lax.broadcasted_iota(jnp.int32, (SUB, SUB), 1)
    upper = (i <= j).astype(F32)
    logs = ld[...]
    stacked = jnp.concatenate([logs[:, s * SUB : (s + 1) * SUB] for s in range(subs)], axis=0)
    sums = jnp.dot(stacked, upper, precision=lax.Precision.HIGHEST, preferred_element_type=F32)
    log_step = jnp.log(sp[...]) * LOG2E
    lasts = []
    for s in range(subs):
        at = slice(s * SUB, (s + 1) * SUB)
        cum = sums[s * 8 : (s + 1) * 8]
        q = cum - log_step[:, at]
        q_ref[:, at] = q
        weight = jnp.exp2(cum[:, SUB - 1 :] - q)
        columns = jnp.concatenate([parts_of(weight, 2), parts_of(cum, 3)], axis=0).T
        column_ref[at] = columns.astype(BF16)
        lasts.append(columns[SUB - 1 :])
    whole = jnp.concatenate(lasts, axis=0).astype(BF16)
    to_lanes = spread_matrix(16, 40, 40, width, width // heads)
    decay_ref[...] = jnp.exp2(jnp.dot(whole, to_lanes, preferred_element_type=F32))


def rows_of(steps, rates, width):
    heads, length = steps.shape
    return pl.pallas_call(
        rows_kernel,
        in_specs=[IN_VMEM] * 2,
        out_specs=[IN_VMEM] * 3,
        out_shape=[
            pltpu.VMEM((8, length), F32),
            pltpu.VMEM((length, 40), BF16),
            pltpu.VMEM((length // SUB, width), F32),
        ],
        scratch_shapes=[pltpu.VMEM((8, length), F32), pltpu.VMEM((8, length), F32)],
        compiler_params=params(),
        cost_estimate=BRIEF,
        name="rows",
    )(*in_vmem([steps, rates]))


def head_conv_kernel(first, heads, x_ref, before_ref, halo_ref, taps_ref, column_ref, *refs):
    xs_ref, wt_ref, ext, spread = refs[-4:]
    length, width = x_ref.shape
    taps = taps_ref.shape[0]
    pairs = width // SUB

    @pl.when(pl.program_id(0) == 0)
    def _():
        for p in range(pairs):
            rows = before_ref if first else halo_ref
            ext[p, :8] = rows[8:16, p * SUB : (p + 1) * SUB].astype(F32)

    for p in range(pairs):
        ext[p, 8:] = x_ref[:, p * SUB : (p + 1) * SUB].astype(F32)
    count = column_ref.shape[1]
    spread[...] = jnp.dot(
        column_ref[...],
        spread_matrix(0, 16, count, width, width // heads),
        preferred_element_type=F32,
    )
    for s in range(length // SUB):
        at = slice(s * SUB, (s + 1) * SUB)
        for p in range(pairs):
            cols = slice(p * SUB, (p + 1) * SUB)
            total = None
            for k in range(taps):
                start = 8 - (taps - 1) + k + s * SUB
                term = taps_ref[k : k + 1, cols] * ext[p, start : start + SUB]
                total = term if total is None else total + term
            xs = silu(total).astype(BF16)
            xs_ref[at, cols] = xs
            wt_ref[at, cols] = (spread[at, cols] * xs.astype(F32)).astype(BF16)
    for p in range(pairs):
        ext[p, :8] = ext[p, length : length + 8]


def head_conv(x_rows, halo, taps, columns, heads, first, count, filled=()):
    length, width = x_rows.shape
    wide = pl.BlockSpec((TILE, width), lambda i: (first + i, 0))
    whole = lambda a: pl.BlockSpec(a.shape, lambda i: (0, 0))
    return pl.pallas_call(
        functools.partial(head_conv_kernel, first, heads),
        grid=(count,),
        in_specs=[
            wide,
            pl.BlockSpec((16, width), lambda i: (max(first * TILE // 16 - 1, 0), 0)),
            whole(halo),
            whole(taps),
            pl.BlockSpec((TILE, columns.shape[1]), lambda i: (first + i, 0)),
        ]
        + [ANYWHERE] * len(filled),
        out_specs=[wide, wide],
        out_shape=[jax.ShapeDtypeStruct((length, width), BF16)] * 2,
        scratch_shapes=[
            pltpu.VMEM((width // SUB, TILE + 8, SUB), F32),
            pltpu.VMEM((TILE, width), F32),
        ],
        compiler_params=params(),
        input_output_aliases={5 + i: i for i in range(len(filled))},
        cost_estimate=BRIEF,
        name="head_conv",
    )(in_hbm(x_rows), in_hbm(x_rows), halo, taps, columns, *filled)


def gates_kernel(z_ref, column_ref, q_ref, gate_ref, factor_ref, start_ref, spread):
    length, width = z_ref.shape
    heads = factor_ref.shape[0] // (length // ROWS)
    size = width // heads
    subs, groups = length // SUB, SUB // ROWS
    columns = column_ref[...]
    to_lanes = spread_matrix(16, 40, columns.shape[1], width, size)
    for p in range(width // SUB):
        spread[p] = jnp.dot(
            columns, to_lanes[:, p * SUB : (p + 1) * SUB], preferred_element_type=F32
        )
    for s in range(subs):
        at = slice(s * SUB, (s + 1) * SUB)
        starts = []
        for p in range(width // SUB):
            cols = slice(p * SUB, (p + 1) * SUB)
            cum = spread[p, at].reshape(groups, ROWS // 8, 8, SUB)
            grown = jnp.exp2(cum - cum[:, ROWS // 16 : ROWS // 16 + 1, :1]).reshape(SUB, SUB)
            gate_ref[at, cols] = grown * silu(z_ref[at, cols].astype(F32))
            start = spread[p, pl.ds(s * SUB + ROWS // 2, groups, stride=ROWS)]
            start_ref[p, s * groups : (s + 1) * groups] = jnp.exp2(start)
            starts.append(start)
        for h in range(heads):
            lane = h * size % SUB
            start = jnp.broadcast_to(starts[h * size // SUB][:, lane : lane + 1], (groups, SUB))
            row = (s * heads + h) * groups
            factor_ref[row : row + groups] = jnp.exp2(
                jnp.minimum(start - q_ref[h : h + 1, at], 64.0)
            )


def gates(z_rows, columns, q, heads):
    length, width = z_rows.shape
    wide = pl.BlockSpec((TILE, width), lambda i: (i, 0))
    rows = pl.BlockSpec((8, TILE), lambda i: (0, i))
    return pl.pallas_call(
        gates_kernel,
        grid=(length // TILE,),
        in_specs=[wide, pl.BlockSpec((TILE, columns.shape[1]), lambda i: (i, 0)), rows],
        out_specs=[
            wide,
            pl.BlockSpec((TILE // ROWS * heads, SUB), lambda i: (i, 0)),
            pl.BlockSpec((width // SUB, TILE // ROWS, SUB), lambda i: (0, i, 0)),
        ],
        out_shape=[
            jax.ShapeDtypeStruct((length, width), F32),
            jax.ShapeDtypeStruct((length // ROWS * heads, SUB), F32),
            jax.ShapeDtypeStruct((width // SUB, length // ROWS, SUB), F32),
        ],
        scratch_shapes=[pltpu.VMEM((width // SUB, TILE, SUB), F32)],
        compiler_params=params(),
        cost_estimate=BRIEF,
        name="gates",
    )(z_rows, columns, q)


def columns_of(refs, rows, at):
    return jnp.concatenate([ref[first:last, at] for ref, (first, last) in zip(refs, rows)], axis=0)


def columns_from(refs, rows, begins, start):
    parts = [
        ref[first:last, pl.ds(pl.multiple_of(start - begin, SUB), SUB)]
        for ref, (first, last), begin in zip(refs, rows, begins)
    ]
    return jnp.concatenate(parts, axis=0)


def last_state_kernel(rows, wt_ref, decay_ref, *refs):
    pieces, (out_ref, local_ref, before_ref, state, total) = refs[:-5], refs[-5:]
    size = state.shape[0]
    subs = TILE // SUB
    state[...] = jnp.zeros_like(state)
    total[...] = jnp.ones_like(total)

    def tile(t, _):
        held, grown = state[...], total[:1]
        row = pl.multiple_of(t * subs, subs)
        decays = decay_ref[pl.ds(row, subs)]
        products = []
        for s in range(subs):
            at = pl.ds(pl.multiple_of(t * TILE + s * SUB, SUB), SUB)
            b_cols = columns_of(pieces, rows, at)
            added = jnp.dot(b_cols, wt_ref[at], preferred_element_type=F32)
            local_ref[pl.ds(pl.multiple_of((t * subs + s) * size, size), size)] = held
            products.append(grown)
            held = held * decays[s : s + 1] + added
            grown = grown * decays[s : s + 1]
        before_ref[pl.ds(row, subs)] = jnp.concatenate(products, axis=0)
        state[...] = held
        total[...] = jnp.broadcast_to(grown, total.shape)
        return 0

    lax.fori_loop(0, wt_ref.shape[0] // TILE, tile, 0)
    out_ref[:size] = state[...].astype(BF16)
    out_ref[size:] = jnp.broadcast_to(total[:1], (16, total.shape[1])).astype(BF16)


def last_state(weighted, decays, pieces, rows):
    length, width = weighted.shape
    size = sum(last - first for first, last in rows)
    count = length // SUB
    return pl.pallas_call(
        functools.partial(last_state_kernel, rows),
        in_specs=[IN_VMEM] * (2 + len(pieces)),
        out_specs=[IN_VMEM] * 3,
        out_shape=[
            jax.ShapeDtypeStruct((size + 16, width), BF16),
            pltpu.VMEM((count * size, width), F32),
            pltpu.VMEM((count, width), F32),
        ],
        scratch_shapes=[pltpu.VMEM((size, width), F32), pltpu.VMEM((8, width), F32)],
        compiler_params=params(),
        cost_estimate=BRIEF,
        name="last_state",
    )(*in_vmem([weighted, decays, *pieces]))


def join_kernel(bit, mine_ref, other_ref, token_ref, out_ref):
    size = mine_ref.shape[0] - 16
    upper = jnp.bitwise_and(lax.axis_index("seq"), bit) != 0
    mine, other = mine_ref[...].astype(F32), other_ref[...].astype(F32)
    early, late = jnp.where(upper, other, mine), jnp.where(upper, mine, other)
    decay = late[size : size + 1]
    out_ref[:size] = (early[:size] * decay + late[:size]).astype(BF16)
    out_ref[size:] = (early[size:] * decay).astype(BF16)


def join(bit, mine, other, token):
    return pl.pallas_call(
        functools.partial(join_kernel, bit),
        in_specs=[IN_VMEM, IN_VMEM, ANYWHERE],
        out_specs=IN_VMEM,
        out_shape=jax.ShapeDtypeStruct(mine.shape, BF16),
        compiler_params=params(),
        cost_estimate=BRIEF,
        name="join",
    )(*in_vmem([mine, other]), token)


def scan_kernel(
    span, count, b_rows, b_picks, c_rows_of, c_picks, c_begins, gate_ref, factor_ref, start_ref, xs_ref,
    local_ref, before_ref, *refs
):
    others, refs = refs[:count], refs[count:]
    b_refs, c_refs = [refs[i] for i in b_picks], [refs[i] for i in c_picks]
    gated_ref, square_ref, carry, c_rows, scores, carried, squares = refs[-7:]
    length, width = gate_ref.shape
    heads = factor_ref.shape[0] // (length // ROWS)
    groups, subs, pairs = SUB // ROWS, TILE // SUB, width // SUB
    size = carry.shape[0]
    entering = jnp.zeros(carry.shape, F32)
    for k in reversed(range(count)):
        end = others[k][...].astype(F32)
        longer = entering * end[size : size + 1] + end[:size]
        entering = jnp.where(jnp.bitwise_and(lax.axis_index("seq"), 1 << k) != 0, longer, entering)
    carry[...] = entering
    i = lax.broadcasted_iota(jnp.int32, (SUB, SUB), 0)
    j = lax.broadcasted_iota(jnp.int32, (SUB, SUB), 1)
    causal = i >= j
    low = (j < SUB // 2).astype(F32)
    keep_low, keep_high = low.astype(BF16), (1.0 - low).astype(BF16)

    def rows_times(value, load):
        rows = [value[g * ROWS : (g + 1) * ROWS] * load(g) for g in range(groups)]
        return jnp.concatenate(rows, axis=0)

    def repeated(ref, row):
        return jnp.broadcast_to(ref[pl.ds(row, 1)], (ROWS, SUB))

    local = [slice(s * SUB, (s + 1) * SUB) for s in range(subs)]

    def tile(t, _):
        whole = [pl.ds(pl.multiple_of(t * TILE + s * SUB, SUB), SUB) for s in range(subs)]
        row = pl.multiple_of(t * subs, subs)
        factors = pl.multiple_of(t * (subs * heads * groups), subs * heads * groups)
        starts = pl.multiple_of(t * (subs * groups), subs * groups)

        decays = before_ref[pl.ds(row, subs)]

        def turn(s):
            c_rows[local[s]] = columns_from(c_refs, c_rows_of, c_begins, t * TILE + s * SUB).T

        def products(s):
            b_cols = columns_of(b_refs, b_rows, whole[s])
            held = pl.ds(pl.multiple_of((t * subs + s) * size, size), size)
            state = local_ref[held] + carry[...] * decays[s : s + 1]
            both = jnp.dot(
                c_rows[local[s]],
                jnp.concatenate([b_cols, state.astype(BF16)], axis=1),
                preferred_element_type=F32,
            )
            scores[local[s]] = jnp.where(causal, both[:, :SUB], 0.0)
            carried[local[s]] = both[:, SUB:]

        turn(0)
        turn(1)
        products(0)
        for s, at in enumerate(whole):
            if s + 2 < subs:
                turn(s + 2)
            if s + 1 < subs:
                products(s + 1)
            total = None
            score = scores[local[s]]
            for p in range(pairs):
                cols = slice(p * SUB, (p + 1) * SUB)
                mixing = []
                for h in (2 * p, 2 * p + 1):
                    base = factors + (s * heads + h) * groups
                    mixing.append(rows_times(score, lambda g: repeated(factor_ref, base + g)).astype(BF16))
                xs = xs_ref[at, cols]
                mixed = jnp.dot(
                    jnp.concatenate(mixing, axis=1),
                    jnp.concatenate([xs * keep_low, xs * keep_high], axis=0),
                    preferred_element_type=F32,
                )
                base = starts + s * groups
                before = rows_times(carried[local[s], cols], lambda g: repeated(start_ref.at[p], base + g))
                gated = gate_ref[at, cols] * (mixed + before)
                gated_ref[at, cols] = gated.astype(BF16)
                square = gated * gated
                total = square if total is None else total + square
            squares[local[s]] = total.astype(BF16)
        sums = lax.dot_general(
            jnp.ones((8, SUB), BF16), squares[...], (((1,), (1,)), ((), ())), preferred_element_type=F32
        )
        square_ref[pl.ds(row, subs)] = jnp.concatenate([sums[:1, at] for at in local], axis=0)
        return 0

    lax.fori_loop(*span, tile, 0)


def scan(span, gate, factor, start, xs, local, before, others, b_pieces, b_rows, c_pieces, c_rows, c_begins, filled=()):
    length, width = xs.shape
    size = sum(last - first for first, last in b_rows)
    pieces = []
    for piece in b_pieces + c_pieces:
        if not any(piece is other for other in pieces):
            pieces.append(piece)
    picks = lambda some: [next(i for i, q in enumerate(pieces) if q is p) for p in some]
    operands = [gate, factor, start, xs, local, before, *others, *pieces, *filled]
    first = len(operands) - len(filled)
    return pl.pallas_call(
        functools.partial(
            scan_kernel, span, len(others), b_rows, picks(b_pieces), c_rows, picks(c_pieces), c_begins
        ),
        in_specs=[IN_VMEM] * len(operands),
        out_specs=[IN_VMEM, IN_VMEM],
        out_shape=[pltpu.VMEM((length, width), BF16), pltpu.VMEM((length // SUB, SUB), F32)],
        scratch_shapes=[
            pltpu.VMEM((size, width), F32),
            pltpu.VMEM((TILE, size), BF16),
            pltpu.VMEM((TILE, SUB), F32),
            pltpu.VMEM((TILE, width), F32),
            pltpu.VMEM((TILE, SUB), BF16),
        ],
        input_output_aliases={first + i: i for i in range(len(filled))},
        compiler_params=params(),
        cost_estimate=BRIEF,
        name="scan",
    )(*in_vmem(operands))


def norm_kernel(channels, gated_ref, gain_ref, *refs):
    squares, (out_ref, rows, sems) = refs[:-3], refs[-3:]
    total = squares[0][...]
    for ref in squares[1:]:
        total = total + ref[...]
    scale = lax.rsqrt(total * (1.0 / channels) + 1e-05).T
    gain = gain_ref[...]
    step = TILE // 2
    copies = []
    for t in range(gated_ref.shape[0] // step):
        for s in range(t * step // SUB, (t + 1) * step // SUB):
            at = slice(s * SUB, (s + 1) * SUB)
            rows[at] = (gated_ref[at].astype(F32) * scale[:, s : s + 1] * gain).astype(BF16)
        at = slice(t * step, (t + 1) * step)
        copies.append(pltpu.make_async_copy(rows.at[at], out_ref.at[at], sems.at[t]))
        copies[-1].start()
    for copy in copies:
        copy.wait()


def norm(channels, gated, gain, squares):
    length, width = gated.shape
    operands = [gated, gain, *squares]
    return pl.pallas_call(
        functools.partial(norm_kernel, channels),
        in_specs=[IN_VMEM] * len(operands),
        out_specs=ANYWHERE,
        out_shape=pltpu.HBM((length, width), BF16),
        scratch_shapes=[
            pltpu.VMEM((length, width), BF16),
            pltpu.SemaphoreType.DMA((2 * length // TILE,)),
        ],
        compiler_params=params(),
        cost_estimate=BRIEF,
        name="norm",
    )(*in_vmem(operands))


def body(x_rows, z_rows, b_rows, c_rows, step_raw, conv_x, conv_b, conv_c, decay_rate, norm_gain):
    length, width = x_rows.shape
    local_heads = decay_rate.shape[0]
    seq, heads = lax.axis_size("seq"), lax.axis_size("head")
    b_cols, c_cols = b_rows.T, c_rows.T
    ends, b_cols, c_cols = tails(x_rows, b_cols, c_cols)
    halo = lax.ppermute(ends, "seq", [(i, i + 1) for i in range(seq - 1)])
    bs, cs, cs_sent = shared_conv(b_cols, c_cols, halo, conv_b.T.astype(F32), conv_c.T.astype(F32))
    cols = bs.shape[0]
    outer, _ = factors(heads)
    tiles = x_rows.shape[0] // TILE
    q, columns, decays = rows_of(step_raw.T, decay_rate[:, None], width)
    conv = functools.partial(head_conv, x_rows, halo, conv_x.astype(F32), columns, local_heads)
    if cols % 16 or factors(heads) != (4, 2):
        b_pieces, c_pieces = [
            [jnp.concatenate(near + along_inner(near), axis=0)]
            for near in ([own] + along_outer(own) for own in (bs, cs))
        ]
        b_rows = c_rows = [(0, b_pieces[0].shape[0])]
        xs, weighted = conv(0, tiles)
        mine, local, before = last_state(weighted, decays, b_pieces, b_rows)
        gate, factor, start = gates(z_rows, columns, q, local_heads)
        token, tail, runs = mine, [], [((0, tiles), None, None)]
    else:
        one = (0, cols)
        b_outer, own, c_own = along_outer(bs), along_inner([bs]), along_inner([cs])
        xs, weighted = conv(0, tiles)
        (b_packed,) = pack(b_outer, [one] * 3, xs, *own, *c_own)
        b_passed = along_inner([b_packed])
        cs_sent, columns = after([cs_sent, columns], b_packed)
        c_outer = along_outer(cs_sent)
        gate, factor, start = gates(z_rows, columns, q, local_heads)
        c_outer[:1] = after(c_outer[:1], start)
        c_passed = c_own + along_inner(c_outer[:1])
        (decays,) = after([decays], c_outer[0])
        b_pieces = [bs, *own, *b_outer, *b_passed]
        b_rows = [one] * 5 + [(0, 3 * cols)]
        mine, local, before = last_state(weighted, decays, b_pieces, b_rows)
        cut = -(-tiles // 2) * TILE
        c_rest = pack(c_outer[:0:-1], [one] * 2, mine, c_passed[1], cuts=[0, cut, length])
        c_ends = along_inner(c_rest)
        c_pieces = [cs, *c_own, *c_outer, c_passed[1]]
        c_rows = [one] * 6
        token, tail = c_rest[0], [(cols, 2 * cols), one]
        runs = [((0, cut // TILE), c_ends[0], 0), ((cut // TILE, tiles), c_ends[1], cut)]
    others, bit = [], 1
    while bit < seq:
        last = 2 * bit == seq
        pairs = [(i, i ^ bit) for i in range(seq) if not (last and i & bit)]
        others.append(lax.ppermute(mine, "seq", pairs))
        if not last:
            mine = join(bit, mine, others[-1], token)
        bit *= 2
    filled = ()
    for span, piece, begin in runs:
        filled = scan(
            span, gate, factor, start, xs, local, before, others, b_pieces, b_rows,
            c_pieces + [piece] * len(tail), c_rows + tail, [0] * len(c_pieces) + [begin] * len(tail), filled,
        )
    gated, square = filled
    square = square + sum(along_outer(square))
    squares = [square] + along_inner([square])
    return norm(heads * width, gated, norm_gain[None, :], squares)


def solution(mesh):
    placed = (
        P("seq", "head"),
        P("seq", "head"),
        P("seq", "head"),
        P("seq", "head"),
        P("seq", "head"),
        P(None, "head"),
        P(None, "head"),
        P(None, "head"),
        P("head"),
        P("head"),
    )
    return jax.shard_map(
        body, mesh=mesh, in_specs=placed, out_specs=P("seq", "head"), check_vma=False
    )
```

```python
import functools
import math

import jax
import jax.numpy as jnp
from jax import lax
from jax.experimental import pallas as pl
from jax.experimental.pallas import tpu as pltpu
from jax.sharding import PartitionSpec as P

SUB = 128
ROWS = 16
TILE = 8 * SUB
LOG2E = math.log2(math.e)
MIB = 1024 * 1024
F32, BF16 = jnp.float32, jnp.bfloat16


def params(mib=16):
    return pltpu.CompilerParams(vmem_limit_bytes=mib * MIB)


def in_hbm(value):
    return pltpu.with_memory_space_constraint(value, pltpu.HBM)


def in_vmem(values):
    return [pltpu.with_memory_space_constraint(value, pltpu.VMEM) for value in values]


IN_VMEM = pl.BlockSpec(memory_space=pltpu.VMEM)
BRIEF = pl.CostEstimate(flops=1000, bytes_accessed=1000, transcendentals=0)
ANYWHERE = pl.BlockSpec(memory_space=pl.ANY)


def silu(value):
    half = 0.5 * value
    return half * jnp.tanh(half) + half


def factors(count):
    inner = max(d for d in range(1, math.isqrt(count) + 1) if count % d == 0)
    return count // inner, inner


def outer_pairs(d):
    outer, inner = factors(lax.axis_size("head"))
    return [(z * inner + y, (z + d) % outer * inner + y) for z in range(outer) for y in range(inner)]


def inner_pairs(e):
    outer, inner = factors(lax.axis_size("head"))
    return [(z * inner + y, z * inner + (y + e) % inner) for z in range(outer) for y in range(inner)]


def along_outer(piece):
    outer, _ = factors(lax.axis_size("head"))
    return [lax.ppermute(piece, "head", outer_pairs(d)) for d in range(1, outer)]


def along_inner(pieces):
    _, inner = factors(lax.axis_size("head"))
    return [lax.ppermute(p, "head", inner_pairs(e)) for e in range(1, inner) for p in pieces]


def tie_kernel(*refs):
    pass


def after(values, *tokens):
    out = pl.pallas_call(
        tie_kernel,
        in_specs=[ANYWHERE] * (len(values) + len(tokens)),
        out_specs=[ANYWHERE] * len(values),
        out_shape=[jax.ShapeDtypeStruct(v.shape, v.dtype) for v in values],
        input_output_aliases={i: i for i in range(len(values))},
        compiler_params=params(1),
        cost_estimate=BRIEF,
        name="tie",
    )(*values, *tokens)
    return list(out)


def pack_kernel(rows, cuts, *refs):
    outs = refs[len(refs) - len(cuts) + 1 :]
    for out_ref, first_token, last_token in zip(outs, cuts[:-1], cuts[1:]):
        row = 0
        for ref, (first, last) in zip(refs, rows):
            out_ref[row : row + last - first] = ref[first:last, first_token:last_token]
            row += last - first


def pack(pieces, rows, *tokens, cuts=None):
    cuts = cuts or [0, pieces[0].shape[1]]
    count = sum(last - first for first, last in rows)
    return pl.pallas_call(
        functools.partial(pack_kernel, rows, cuts),
        in_specs=[IN_VMEM] * len(pieces) + [ANYWHERE] * len(tokens),
        out_specs=[IN_VMEM] * (len(cuts) - 1),
        out_shape=[
            pltpu.VMEM((count, last - first), pieces[0].dtype) for first, last in zip(cuts[:-1], cuts[1:])
        ],
        compiler_params=params(),
        cost_estimate=BRIEF,
        name="pack",
    )(*in_vmem(pieces), *tokens)


def tails_kernel(x_ref, b_ref, c_ref, out_ref, b_out, c_out):
    cols, length = b_ref.shape
    out_ref[...] = jnp.zeros_like(out_ref)
    out_ref[:16] = x_ref[...]
    out_ref[16 : 16 + cols, :SUB] = b_ref[:, length - SUB :]
    out_ref[32 : 32 + cols, :SUB] = c_ref[:, length - SUB :]
    b_out[...] = b_ref[...]
    c_out[...] = c_ref[...]


def tails(x_rows, b_cols, c_cols):
    length, width = x_rows.shape
    cols = b_cols.shape[0]
    whole = pl.BlockSpec((cols, length), lambda i: (0, 0))
    held = pltpu.VMEM((cols, length), BF16)
    return pl.pallas_call(
        tails_kernel,
        grid=(1,),
        in_specs=[pl.BlockSpec((16, width), lambda i: (length // 16 - 1, 0)), whole, whole],
        out_specs=[pl.BlockSpec((48, width), lambda i: (0, 0)), IN_VMEM, IN_VMEM],
        out_shape=[jax.ShapeDtypeStruct((48, width), BF16), held, held],
        compiler_params=params(),
        cost_estimate=BRIEF,
        name="tails",
    )(in_hbm(x_rows), in_hbm(b_cols), in_hbm(c_cols))


def conv_columns(rows, halo, taps):
    wide = jnp.concatenate([halo, rows], axis=1).astype(F32)
    width = taps.shape[1]
    total = None
    for k in range(width):
        lag = width - 1 - k
        moved = pltpu.roll(wide, lag, axis=1) if lag else wide
        term = taps[:, k : k + 1] * moved[:, SUB:]
        total = term if total is None else total + term
    return silu(total).astype(BF16)


def shared_conv_kernel(b_ref, c_ref, halo_ref, tb_ref, tc_ref, bs_ref, cs_ref, again_ref):
    cols = b_ref.shape[0]
    bs_ref[...] = conv_columns(b_ref[...], halo_ref[16 : 16 + cols, :SUB], tb_ref[...])
    cs = conv_columns(c_ref[...], halo_ref[32 : 32 + cols, :SUB], tc_ref[...])
    cs_ref[...], again_ref[...] = cs, cs


def shared_conv(b_cols, c_cols, halo, taps_b, taps_c):
    operands = [b_cols, c_cols, halo, taps_b, taps_c]
    return pl.pallas_call(
        shared_conv_kernel,
        in_specs=[IN_VMEM] * 5,
        out_specs=[IN_VMEM] * 3,
        out_shape=[pltpu.VMEM(b_cols.shape, BF16)] * 3,
        compiler_params=params(),
        cost_estimate=BRIEF,
        name="shared_conv",
    )(*in_vmem(operands))


def parts_of(value, count):
    parts = []
    for _ in range(count):
        part = value.astype(BF16).astype(F32)
        parts.append(part)
        value = value - part
    return jnp.concatenate(parts, axis=0)


def spread_matrix(first, last, count, width, size):
    i = lax.broadcasted_iota(jnp.int32, (count, width), 0)
    j = lax.broadcasted_iota(jnp.int32, (count, width), 1)
    head = jnp.bitwise_and(i, 7) * size
    lanes = jnp.logical_and(j >= head, j < head + size)
    return jnp.logical_and(lanes, jnp.logical_and(i >= first, i < last)).astype(F32).astype(BF16)


def rows_kernel(step_ref, rate_ref, q_ref, column_ref, decay_ref, sp, ld):
    heads, length = step_ref.shape
    width = decay_ref.shape[1]
    subs = length // SUB
    raw = step_ref[...]
    soft = jnp.maximum(raw, 0.0) + jnp.log(1.0 + jnp.exp(-jnp.abs(raw)))
    sp[...] = jnp.ones_like(sp)
    ld[...] = jnp.zeros_like(ld)
    sp[:heads] = soft
    ld[:heads] = soft * (rate_ref[...] * -LOG2E)
    i = lax.broadcasted_iota(jnp.int32, (SUB, SUB), 0)
    j = lax.broadcasted_iota(jnp.int32, (SUB, SUB), 1)
    upper = (i <= j).astype(F32)
    logs = ld[...]
    stacked = jnp.concatenate([logs[:, s * SUB : (s + 1) * SUB] for s in range(subs)], axis=0)
    sums = jnp.dot(stacked, upper, precision=lax.Precision.HIGHEST, preferred_element_type=F32)
    log_step = jnp.log(sp[...]) * LOG2E
    lasts = []
    for s in range(subs):
        at = slice(s * SUB, (s + 1) * SUB)
        cum = sums[s * 8 : (s + 1) * 8]
        q = cum - log_step[:, at]
        q_ref[:, at] = q
        weight = jnp.exp2(cum[:, SUB - 1 :] - q)
        columns = jnp.concatenate([parts_of(weight, 2), parts_of(cum, 3)], axis=0).T
        column_ref[at] = columns.astype(BF16)
        lasts.append(columns[SUB - 1 :])
    whole = jnp.concatenate(lasts, axis=0).astype(BF16)
    to_lanes = spread_matrix(16, 40, 40, width, width // heads)
    decay_ref[...] = jnp.exp2(jnp.dot(whole, to_lanes, preferred_element_type=F32))


def rows_of(steps, rates, width):
    heads, length = steps.shape
    return pl.pallas_call(
        rows_kernel,
        in_specs=[IN_VMEM] * 2,
        out_specs=[IN_VMEM] * 3,
        out_shape=[
            pltpu.VMEM((8, length), F32),
            pltpu.VMEM((length, 40), BF16),
            pltpu.VMEM((length // SUB, width), F32),
        ],
        scratch_shapes=[pltpu.VMEM((8, length), F32), pltpu.VMEM((8, length), F32)],
        compiler_params=params(),
        cost_estimate=BRIEF,
        name="rows",
    )(*in_vmem([steps, rates]))


def head_conv_kernel(first, heads, x_ref, before_ref, halo_ref, taps_ref, column_ref, *refs):
    xs_ref, wt_ref, ext, spread = refs[-4:]
    length, width = x_ref.shape
    taps = taps_ref.shape[0]
    pairs = width // SUB

    @pl.when(pl.program_id(0) == 0)
    def _():
        for p in range(pairs):
            rows = before_ref if first else halo_ref
            ext[p, :8] = rows[8:16, p * SUB : (p + 1) * SUB].astype(F32)

    for p in range(pairs):
        ext[p, 8:] = x_ref[:, p * SUB : (p + 1) * SUB].astype(F32)
    count = column_ref.shape[1]
    spread[...] = jnp.dot(
        column_ref[...],
        spread_matrix(0, 16, count, width, width // heads),
        preferred_element_type=F32,
    )
    for s in range(length // SUB):
        at = slice(s * SUB, (s + 1) * SUB)
        for p in range(pairs):
            cols = slice(p * SUB, (p + 1) * SUB)
            total = None
            for k in range(taps):
                start = 8 - (taps - 1) + k + s * SUB
                term = taps_ref[k : k + 1, cols] * ext[p, start : start + SUB]
                total = term if total is None else total + term
            xs = silu(total).astype(BF16)
            xs_ref[at, cols] = xs
            wt_ref[at, cols] = (spread[at, cols] * xs.astype(F32)).astype(BF16)
    for p in range(pairs):
        ext[p, :8] = ext[p, length : length + 8]


def head_conv(x_rows, halo, taps, columns, heads, first, count, filled=()):
    length, width = x_rows.shape
    wide = pl.BlockSpec((TILE, width), lambda i: (first + i, 0))
    whole = lambda a: pl.BlockSpec(a.shape, lambda i: (0, 0))
    return pl.pallas_call(
        functools.partial(head_conv_kernel, first, heads),
        grid=(count,),
        in_specs=[
            wide,
            pl.BlockSpec((16, width), lambda i: (max(first * TILE // 16 - 1, 0), 0)),
            whole(halo),
            whole(taps),
            pl.BlockSpec((TILE, columns.shape[1]), lambda i: (first + i, 0)),
        ]
        + [ANYWHERE] * len(filled),
        out_specs=[wide, wide],
        out_shape=[jax.ShapeDtypeStruct((length, width), BF16)] * 2,
        scratch_shapes=[
            pltpu.VMEM((width // SUB, TILE + 8, SUB), F32),
            pltpu.VMEM((TILE, width), F32),
        ],
        compiler_params=params(),
        input_output_aliases={5 + i: i for i in range(len(filled))},
        cost_estimate=BRIEF,
        name="head_conv",
    )(in_hbm(x_rows), in_hbm(x_rows), halo, taps, columns, *filled)


def gates_kernel(z_ref, column_ref, q_ref, gate_ref, factor_ref, start_ref, spread):
    length, width = z_ref.shape
    heads = factor_ref.shape[0] // (length // ROWS)
    size = width // heads
    subs, groups = length // SUB, SUB // ROWS
    columns = column_ref[...]
    to_lanes = spread_matrix(16, 40, columns.shape[1], width, size)
    for p in range(width // SUB):
        spread[p] = jnp.dot(
            columns, to_lanes[:, p * SUB : (p + 1) * SUB], preferred_element_type=F32
        )
    for s in range(subs):
        at = slice(s * SUB, (s + 1) * SUB)
        starts = []
        for p in range(width // SUB):
            cols = slice(p * SUB, (p + 1) * SUB)
            cum = spread[p, at].reshape(groups, ROWS // 8, 8, SUB)
            grown = jnp.exp2(cum - cum[:, ROWS // 16 : ROWS // 16 + 1, :1]).reshape(SUB, SUB)
            gate_ref[at, cols] = grown * silu(z_ref[at, cols].astype(F32))
            start = spread[p, pl.ds(s * SUB + ROWS // 2, groups, stride=ROWS)]
            start_ref[p, s * groups : (s + 1) * groups] = jnp.exp2(start)
            starts.append(start)
        for h in range(heads):
            lane = h * size % SUB
            start = jnp.broadcast_to(starts[h * size // SUB][:, lane : lane + 1], (groups, SUB))
            row = (s * heads + h) * groups
            factor_ref[row : row + groups] = jnp.exp2(
                jnp.minimum(start - q_ref[h : h + 1, at], 64.0)
            )


def gates(z_rows, columns, q, heads):
    length, width = z_rows.shape
    wide = pl.BlockSpec((TILE, width), lambda i: (i, 0))
    rows = pl.BlockSpec((8, TILE), lambda i: (0, i))
    return pl.pallas_call(
        gates_kernel,
        grid=(length // TILE,),
        in_specs=[wide, pl.BlockSpec((TILE, columns.shape[1]), lambda i: (i, 0)), rows],
        out_specs=[
            wide,
            pl.BlockSpec((TILE // ROWS * heads, SUB), lambda i: (i, 0)),
            pl.BlockSpec((width // SUB, TILE // ROWS, SUB), lambda i: (0, i, 0)),
        ],
        out_shape=[
            jax.ShapeDtypeStruct((length, width), F32),
            jax.ShapeDtypeStruct((length // ROWS * heads, SUB), F32),
            jax.ShapeDtypeStruct((width // SUB, length // ROWS, SUB), F32),
        ],
        scratch_shapes=[pltpu.VMEM((width // SUB, TILE, SUB), F32)],
        compiler_params=params(),
        cost_estimate=BRIEF,
        name="gates",
    )(z_rows, columns, q)


def columns_of(refs, rows, at):
    return jnp.concatenate([ref[first:last, at] for ref, (first, last) in zip(refs, rows)], axis=0)


def columns_from(refs, rows, begins, start):
    parts = [
        ref[first:last, pl.ds(pl.multiple_of(start - begin, SUB), SUB)]
        for ref, (first, last), begin in zip(refs, rows, begins)
    ]
    return jnp.concatenate(parts, axis=0)


def last_state_kernel(rows, wt_ref, decay_ref, *refs):
    pieces, (out_ref, local_ref, before_ref, state, total) = refs[:-5], refs[-5:]
    size = state.shape[0]
    subs = TILE // SUB
    state[...] = jnp.zeros_like(state)
    total[...] = jnp.ones_like(total)

    def tile(t, _):
        held, grown = state[...], total[:1]
        row = pl.multiple_of(t * subs, subs)
        decays = decay_ref[pl.ds(row, subs)]
        products = []
        for s in range(subs):
            at = pl.ds(pl.multiple_of(t * TILE + s * SUB, SUB), SUB)
            b_cols = columns_of(pieces, rows, at)
            added = jnp.dot(b_cols, wt_ref[at], preferred_element_type=F32)
            local_ref[pl.ds(pl.multiple_of((t * subs + s) * size, size), size)] = held
            products.append(grown)
            held = held * decays[s : s + 1] + added
            grown = grown * decays[s : s + 1]
        before_ref[pl.ds(row, subs)] = jnp.concatenate(products, axis=0)
        state[...] = held
        total[...] = jnp.broadcast_to(grown, total.shape)
        return 0

    lax.fori_loop(0, wt_ref.shape[0] // TILE, tile, 0)
    out_ref[:size] = state[...].astype(BF16)
    out_ref[size:] = jnp.broadcast_to(total[:1], (16, total.shape[1])).astype(BF16)


def last_state(weighted, decays, pieces, rows):
    length, width = weighted.shape
    size = sum(last - first for first, last in rows)
    count = length // SUB
    return pl.pallas_call(
        functools.partial(last_state_kernel, rows),
        in_specs=[IN_VMEM] * (2 + len(pieces)),
        out_specs=[IN_VMEM] * 3,
        out_shape=[
            jax.ShapeDtypeStruct((size + 16, width), BF16),
            pltpu.VMEM((count * size, width), F32),
            pltpu.VMEM((count, width), F32),
        ],
        scratch_shapes=[pltpu.VMEM((size, width), F32), pltpu.VMEM((8, width), F32)],
        compiler_params=params(),
        cost_estimate=BRIEF,
        name="last_state",
    )(*in_vmem([weighted, decays, *pieces]))


def join_kernel(bit, mine_ref, other_ref, token_ref, out_ref):
    size = mine_ref.shape[0] - 16
    upper = jnp.bitwise_and(lax.axis_index("seq"), bit) != 0
    mine, other = mine_ref[...].astype(F32), other_ref[...].astype(F32)
    early, late = jnp.where(upper, other, mine), jnp.where(upper, mine, other)
    decay = late[size : size + 1]
    out_ref[:size] = (early[:size] * decay + late[:size]).astype(BF16)
    out_ref[size:] = (early[size:] * decay).astype(BF16)


def join(bit, mine, other, token):
    return pl.pallas_call(
        functools.partial(join_kernel, bit),
        in_specs=[IN_VMEM, IN_VMEM, ANYWHERE],
        out_specs=IN_VMEM,
        out_shape=jax.ShapeDtypeStruct(mine.shape, BF16),
        compiler_params=params(),
        cost_estimate=BRIEF,
        name="join",
    )(*in_vmem([mine, other]), token)


def scan_kernel(
    span, count, b_rows, b_picks, c_rows_of, c_picks, c_begins, gate_ref, factor_ref, start_ref, xs_ref,
    local_ref, before_ref, *refs
):
    others, refs = refs[:count], refs[count:]
    b_refs, c_refs = [refs[i] for i in b_picks], [refs[i] for i in c_picks]
    gated_ref, square_ref, carry, c_rows, scores, carried = refs[-6:]
    length, width = gate_ref.shape
    heads = factor_ref.shape[0] // (length // ROWS)
    groups, subs, pairs = SUB // ROWS, TILE // SUB, width // SUB
    size = carry.shape[0]
    entering = jnp.zeros(carry.shape, F32)
    for k in reversed(range(count)):
        end = others[k][...].astype(F32)
        longer = entering * end[size : size + 1] + end[:size]
        entering = jnp.where(jnp.bitwise_and(lax.axis_index("seq"), 1 << k) != 0, longer, entering)
    carry[...] = entering
    i = lax.broadcasted_iota(jnp.int32, (SUB, SUB), 0)
    j = lax.broadcasted_iota(jnp.int32, (SUB, SUB), 1)
    causal = i >= j
    low = (j < SUB // 2).astype(F32)
    keep_low, keep_high = low.astype(BF16), (1.0 - low).astype(BF16)

    def rows_times(value, load):
        rows = [value[g * ROWS : (g + 1) * ROWS] * load(g) for g in range(groups)]
        return jnp.concatenate(rows, axis=0)

    def repeated(ref, row):
        return jnp.broadcast_to(ref[pl.ds(row, 1)], (ROWS, SUB))

    local = [slice(s * SUB, (s + 1) * SUB) for s in range(subs)]

    def tile(t, _):
        whole = [pl.ds(pl.multiple_of(t * TILE + s * SUB, SUB), SUB) for s in range(subs)]
        row = pl.multiple_of(t * subs, subs)
        factors = pl.multiple_of(t * (subs * heads * groups), subs * heads * groups)
        starts = pl.multiple_of(t * (subs * groups), subs * groups)

        decays = before_ref[pl.ds(row, subs)]

        def turn(s):
            c_rows[local[s]] = columns_from(c_refs, c_rows_of, c_begins, t * TILE + s * SUB).T

        def products(s):
            b_cols = columns_of(b_refs, b_rows, whole[s])
            held = pl.ds(pl.multiple_of((t * subs + s) * size, size), size)
            state = local_ref[held] + carry[...] * decays[s : s + 1]
            both = jnp.dot(
                c_rows[local[s]],
                jnp.concatenate([b_cols, state.astype(BF16)], axis=1),
                preferred_element_type=F32,
            )
            scores[local[s]] = jnp.where(causal, both[:, :SUB], 0.0)
            carried[local[s]] = both[:, SUB:]

        sums = []
        turn(0)
        turn(1)
        products(0)
        for s, at in enumerate(whole):
            if s + 2 < subs:
                turn(s + 2)
            if s + 1 < subs:
                products(s + 1)
            total = None
            score = scores[local[s]]
            for p in range(pairs):
                cols = slice(p * SUB, (p + 1) * SUB)
                mixing = []
                for h in (2 * p, 2 * p + 1):
                    base = factors + (s * heads + h) * groups
                    mixing.append(rows_times(score, lambda g: repeated(factor_ref, base + g)).astype(BF16))
                xs = xs_ref[at, cols]
                mixed = jnp.dot(
                    jnp.concatenate(mixing, axis=1),
                    jnp.concatenate([xs * keep_low, xs * keep_high], axis=0),
                    preferred_element_type=F32,
                )
                base = starts + s * groups
                before = rows_times(carried[local[s], cols], lambda g: repeated(start_ref.at[p], base + g))
                gated = gate_ref[at, cols] * (mixed + before)
                gated_ref[at, cols] = gated.astype(BF16)
                square = gated * gated
                total = square if total is None else total + square
            column = jnp.sum(total, axis=1, keepdims=True)
            sums.append(jnp.sum(jnp.where(i == j, column, 0.0), axis=0, keepdims=True))
        square_ref[pl.ds(row, subs)] = jnp.concatenate(sums, axis=0)
        return 0

    lax.fori_loop(*span, tile, 0)


def scan(span, gate, factor, start, xs, local, before, others, b_pieces, b_rows, c_pieces, c_rows, c_begins, filled=()):
    length, width = xs.shape
    size = sum(last - first for first, last in b_rows)
    pieces = []
    for piece in b_pieces + c_pieces:
        if not any(piece is other for other in pieces):
            pieces.append(piece)
    picks = lambda some: [next(i for i, q in enumerate(pieces) if q is p) for p in some]
    operands = [gate, factor, start, xs, local, before, *others, *pieces, *filled]
    first = len(operands) - len(filled)
    return pl.pallas_call(
        functools.partial(
            scan_kernel, span, len(others), b_rows, picks(b_pieces), c_rows, picks(c_pieces), c_begins
        ),
        in_specs=[IN_VMEM] * len(operands),
        out_specs=[IN_VMEM, IN_VMEM],
        out_shape=[pltpu.VMEM((length, width), BF16), pltpu.VMEM((length // SUB, SUB), F32)],
        scratch_shapes=[
            pltpu.VMEM((size, width), F32),
            pltpu.VMEM((TILE, size), BF16),
            pltpu.VMEM((TILE, SUB), F32),
            pltpu.VMEM((TILE, width), F32),
        ],
        input_output_aliases={first + i: i for i in range(len(filled))},
        compiler_params=params(),
        cost_estimate=BRIEF,
        name="scan",
    )(*in_vmem(operands))


def norm_kernel(channels, gated_ref, gain_ref, *refs):
    squares, (out_ref, rows, sems) = refs[:-3], refs[-3:]
    total = squares[0][...]
    for ref in squares[1:]:
        total = total + ref[...]
    scale = lax.rsqrt(total * (1.0 / channels) + 1e-05).T
    gain = gain_ref[...]
    step = TILE // 2
    copies = []
    for t in range(gated_ref.shape[0] // step):
        for s in range(t * step // SUB, (t + 1) * step // SUB):
            at = slice(s * SUB, (s + 1) * SUB)
            rows[at] = (gated_ref[at].astype(F32) * scale[:, s : s + 1] * gain).astype(BF16)
        at = slice(t * step, (t + 1) * step)
        copies.append(pltpu.make_async_copy(rows.at[at], out_ref.at[at], sems.at[t]))
        copies[-1].start()
    for copy in copies:
        copy.wait()


def norm(channels, gated, gain, squares):
    length, width = gated.shape
    operands = [gated, gain, *squares]
    return pl.pallas_call(
        functools.partial(norm_kernel, channels),
        in_specs=[IN_VMEM] * len(operands),
        out_specs=ANYWHERE,
        out_shape=pltpu.HBM((length, width), BF16),
        scratch_shapes=[
            pltpu.VMEM((length, width), BF16),
            pltpu.SemaphoreType.DMA((2 * length // TILE,)),
        ],
        compiler_params=params(),
        cost_estimate=BRIEF,
        name="norm",
    )(*in_vmem(operands))


def body(x_rows, z_rows, b_rows, c_rows, step_raw, conv_x, conv_b, conv_c, decay_rate, norm_gain):
    length, width = x_rows.shape
    local_heads = decay_rate.shape[0]
    seq, heads = lax.axis_size("seq"), lax.axis_size("head")
    b_cols, c_cols = b_rows.T, c_rows.T
    ends, b_cols, c_cols = tails(x_rows, b_cols, c_cols)
    halo = lax.ppermute(ends, "seq", [(i, i + 1) for i in range(seq - 1)])
    bs, cs, cs_sent = shared_conv(b_cols, c_cols, halo, conv_b.T.astype(F32), conv_c.T.astype(F32))
    cols = bs.shape[0]
    outer, _ = factors(heads)
    tiles = x_rows.shape[0] // TILE
    q, columns, decays = rows_of(step_raw.T, decay_rate[:, None], width)
    conv = functools.partial(head_conv, x_rows, halo, conv_x.astype(F32), columns, local_heads)
    if cols % 16 or factors(heads) != (4, 2):
        b_pieces, c_pieces = [
            [jnp.concatenate(near + along_inner(near), axis=0)]
            for near in ([own] + along_outer(own) for own in (bs, cs))
        ]
        b_rows = c_rows = [(0, b_pieces[0].shape[0])]
        xs, weighted = conv(0, tiles)
        mine, local, before = last_state(weighted, decays, b_pieces, b_rows)
        gate, factor, start = gates(z_rows, columns, q, local_heads)
        token, tail, runs = mine, [], [((0, tiles), None, None)]
    else:
        one = (0, cols)
        b_outer, own, c_own = along_outer(bs), along_inner([bs]), along_inner([cs])
        xs, weighted = conv(0, tiles)
        (b_packed,) = pack(b_outer, [one] * 3, xs, *own, *c_own)
        b_passed = along_inner([b_packed])
        cs_sent, columns = after([cs_sent, columns], b_packed)
        c_outer = along_outer(cs_sent)
        gate, factor, start = gates(z_rows, columns, q, local_heads)
        c_outer[:1] = after(c_outer[:1], start)
        c_passed = c_own + along_inner(c_outer[:1])
        (decays,) = after([decays], c_outer[0])
        b_pieces = [bs, *own, *b_outer, *b_passed]
        b_rows = [one] * 5 + [(0, 3 * cols)]
        mine, local, before = last_state(weighted, decays, b_pieces, b_rows)
        cut = -(-tiles // 2) * TILE
        c_rest = pack(c_outer[:0:-1], [one] * 2, mine, c_passed[1], cuts=[0, cut, length])
        c_ends = along_inner(c_rest)
        c_pieces = [cs, *c_own, *c_outer, c_passed[1]]
        c_rows = [one] * 6
        token, tail = c_rest[0], [(cols, 2 * cols), one]
        runs = [((0, cut // TILE), c_ends[0], 0), ((cut // TILE, tiles), c_ends[1], cut)]
    others, bit = [], 1
    while bit < seq:
        last = 2 * bit == seq
        pairs = [(i, i ^ bit) for i in range(seq) if not (last and i & bit)]
        others.append(lax.ppermute(mine, "seq", pairs))
        if not last:
            mine = join(bit, mine, others[-1], token)
        bit *= 2
    filled = ()
    for span, piece, begin in runs:
        filled = scan(
            span, gate, factor, start, xs, local, before, others, b_pieces, b_rows,
            c_pieces + [piece] * len(tail), c_rows + tail, [0] * len(c_pieces) + [begin] * len(tail), filled,
        )
    gated, square = filled
    square = square + sum(along_outer(square))
    squares = [square] + along_inner([square])
    return norm(heads * width, gated, norm_gain[None, :], squares)


def solution(mesh):
    placed = (
        P("seq", "head"),
        P("seq", "head"),
        P("seq", "head"),
        P("seq", "head"),
        P("seq", "head"),
        P(None, "head"),
        P(None, "head"),
        P(None, "head"),
        P("head"),
        P("head"),
    )
    return jax.shard_map(
        body, mesh=mesh, in_specs=placed, out_specs=P("seq", "head"), check_vma=False
    )
```

```python
import functools
import math

import jax
import jax.numpy as jnp
from jax import lax
from jax.experimental import pallas as pl
from jax.experimental.pallas import tpu as pltpu
from jax.sharding import PartitionSpec as P

SUB = 128
ROWS = 16
TILE = 8 * SUB
LOG2E = math.log2(math.e)
MIB = 1024 * 1024
F32, BF16 = jnp.float32, jnp.bfloat16


def params(mib=16):
    return pltpu.CompilerParams(vmem_limit_bytes=mib * MIB)


def in_hbm(value):
    return pltpu.with_memory_space_constraint(value, pltpu.HBM)


def in_vmem(values):
    return [pltpu.with_memory_space_constraint(value, pltpu.VMEM) for value in values]


IN_VMEM = pl.BlockSpec(memory_space=pltpu.VMEM)
BRIEF = pl.CostEstimate(flops=1000, bytes_accessed=1000, transcendentals=0)
ANYWHERE = pl.BlockSpec(memory_space=pl.ANY)


def silu(value):
    half = 0.5 * value
    return half * jnp.tanh(half) + half


def factors(count):
    inner = max(d for d in range(1, math.isqrt(count) + 1) if count % d == 0)
    return count // inner, inner


def outer_pairs(d):
    outer, inner = factors(lax.axis_size("head"))
    return [(z * inner + y, (z + d) % outer * inner + y) for z in range(outer) for y in range(inner)]


def inner_pairs(e):
    outer, inner = factors(lax.axis_size("head"))
    return [(z * inner + y, z * inner + (y + e) % inner) for z in range(outer) for y in range(inner)]


def along_outer(piece):
    outer, _ = factors(lax.axis_size("head"))
    return [lax.ppermute(piece, "head", outer_pairs(d)) for d in range(1, outer)]


def along_inner(pieces):
    _, inner = factors(lax.axis_size("head"))
    return [lax.ppermute(p, "head", inner_pairs(e)) for e in range(1, inner) for p in pieces]


def tie_kernel(*refs):
    pass


def after(values, *tokens):
    out = pl.pallas_call(
        tie_kernel,
        in_specs=[ANYWHERE] * (len(values) + len(tokens)),
        out_specs=[ANYWHERE] * len(values),
        out_shape=[jax.ShapeDtypeStruct(v.shape, v.dtype) for v in values],
        input_output_aliases={i: i for i in range(len(values))},
        compiler_params=params(1),
        cost_estimate=BRIEF,
        name="tie",
    )(*values, *tokens)
    return list(out)


def pack_kernel(rows, cuts, *refs):
    outs = refs[len(refs) - len(cuts) + 1 :]
    for out_ref, first_token, last_token in zip(outs, cuts[:-1], cuts[1:]):
        row = 0
        for ref, (first, last) in zip(refs, rows):
            out_ref[row : row + last - first] = ref[first:last, first_token:last_token]
            row += last - first


def pack(pieces, rows, *tokens, cuts=None):
    cuts = cuts or [0, pieces[0].shape[1]]
    count = sum(last - first for first, last in rows)
    return pl.pallas_call(
        functools.partial(pack_kernel, rows, cuts),
        in_specs=[IN_VMEM] * len(pieces) + [ANYWHERE] * len(tokens),
        out_specs=[IN_VMEM] * (len(cuts) - 1),
        out_shape=[
            pltpu.VMEM((count, last - first), pieces[0].dtype) for first, last in zip(cuts[:-1], cuts[1:])
        ],
        compiler_params=params(),
        cost_estimate=BRIEF,
        name="pack",
    )(*in_vmem(pieces), *tokens)


def tails_kernel(x_ref, b_ref, c_ref, out_ref, b_out, c_out):
    cols, length = b_ref.shape
    out_ref[...] = jnp.zeros_like(out_ref)
    out_ref[:16] = x_ref[...]
    out_ref[16 : 16 + cols, :SUB] = b_ref[:, length - SUB :]
    out_ref[32 : 32 + cols, :SUB] = c_ref[:, length - SUB :]
    b_out[...] = b_ref[...]
    c_out[...] = c_ref[...]


def tails(x_rows, b_cols, c_cols):
    length, width = x_rows.shape
    cols = b_cols.shape[0]
    whole = pl.BlockSpec((cols, length), lambda i: (0, 0))
    held = pltpu.VMEM((cols, length), BF16)
    return pl.pallas_call(
        tails_kernel,
        grid=(1,),
        in_specs=[pl.BlockSpec((16, width), lambda i: (length // 16 - 1, 0)), whole, whole],
        out_specs=[pl.BlockSpec((48, width), lambda i: (0, 0)), IN_VMEM, IN_VMEM],
        out_shape=[jax.ShapeDtypeStruct((48, width), BF16), held, held],
        compiler_params=params(),
        cost_estimate=BRIEF,
        name="tails",
    )(in_hbm(x_rows), in_hbm(b_cols), in_hbm(c_cols))


def conv_columns(rows, halo, taps):
    wide = jnp.concatenate([halo, rows], axis=1).astype(F32)
    width = taps.shape[1]
    total = None
    for k in range(width):
        lag = width - 1 - k
        moved = pltpu.roll(wide, lag, axis=1) if lag else wide
        term = taps[:, k : k + 1] * moved[:, SUB:]
        total = term if total is None else total + term
    return silu(total).astype(BF16)


def shared_conv_kernel(b_ref, c_ref, halo_ref, tb_ref, tc_ref, bs_ref, cs_ref, again_ref):
    cols = b_ref.shape[0]
    bs_ref[...] = conv_columns(b_ref[...], halo_ref[16 : 16 + cols, :SUB], tb_ref[...])
    cs = conv_columns(c_ref[...], halo_ref[32 : 32 + cols, :SUB], tc_ref[...])
    cs_ref[...], again_ref[...] = cs, cs


def shared_conv(b_cols, c_cols, halo, taps_b, taps_c):
    operands = [b_cols, c_cols, halo, taps_b, taps_c]
    return pl.pallas_call(
        shared_conv_kernel,
        in_specs=[IN_VMEM] * 5,
        out_specs=[IN_VMEM] * 3,
        out_shape=[pltpu.VMEM(b_cols.shape, BF16)] * 3,
        compiler_params=params(),
        cost_estimate=BRIEF,
        name="shared_conv",
    )(*in_vmem(operands))


def parts_of(value, count):
    parts = []
    for _ in range(count):
        part = value.astype(BF16).astype(F32)
        parts.append(part)
        value = value - part
    return jnp.concatenate(parts, axis=0)


def spread_matrix(first, last, count, width, size):
    i = lax.broadcasted_iota(jnp.int32, (count, width), 0)
    j = lax.broadcasted_iota(jnp.int32, (count, width), 1)
    head = jnp.bitwise_and(i, 7) * size
    lanes = jnp.logical_and(j >= head, j < head + size)
    return jnp.logical_and(lanes, jnp.logical_and(i >= first, i < last)).astype(F32).astype(BF16)


def rows_kernel(step_ref, rate_ref, q_ref, column_ref, decay_ref, sp, ld):
    heads, length = step_ref.shape
    width = decay_ref.shape[1]
    subs = length // SUB
    raw = step_ref[...]
    soft = jnp.maximum(raw, 0.0) + jnp.log(1.0 + jnp.exp(-jnp.abs(raw)))
    sp[...] = jnp.ones_like(sp)
    ld[...] = jnp.zeros_like(ld)
    sp[:heads] = soft
    ld[:heads] = soft * (rate_ref[...] * -LOG2E)
    i = lax.broadcasted_iota(jnp.int32, (SUB, SUB), 0)
    j = lax.broadcasted_iota(jnp.int32, (SUB, SUB), 1)
    upper = (i <= j).astype(F32)
    logs = ld[...]
    stacked = jnp.concatenate([logs[:, s * SUB : (s + 1) * SUB] for s in range(subs)], axis=0)
    sums = jnp.dot(stacked, upper, precision=lax.Precision.HIGHEST, preferred_element_type=F32)
    log_step = jnp.log(sp[...]) * LOG2E
    lasts = []
    for s in range(subs):
        at = slice(s * SUB, (s + 1) * SUB)
        cum = sums[s * 8 : (s + 1) * 8]
        q = cum - log_step[:, at]
        q_ref[:, at] = q
        weight = jnp.exp2(cum[:, SUB - 1 :] - q)
        columns = jnp.concatenate([parts_of(weight, 2), parts_of(cum, 3)], axis=0).T
        column_ref[at] = columns.astype(BF16)
        lasts.append(columns[SUB - 1 :])
    whole = jnp.concatenate(lasts, axis=0).astype(BF16)
    to_lanes = spread_matrix(16, 40, 40, width, width // heads)
    decay_ref[...] = jnp.exp2(jnp.dot(whole, to_lanes, preferred_element_type=F32))


def rows_of(steps, rates, width):
    heads, length = steps.shape
    return pl.pallas_call(
        rows_kernel,
        in_specs=[IN_VMEM] * 2,
        out_specs=[IN_VMEM] * 3,
        out_shape=[
            pltpu.VMEM((8, length), F32),
            pltpu.VMEM((length, 40), BF16),
            pltpu.VMEM((length // SUB, width), F32),
        ],
        scratch_shapes=[pltpu.VMEM((8, length), F32), pltpu.VMEM((8, length), F32)],
        compiler_params=params(),
        cost_estimate=BRIEF,
        name="rows",
    )(*in_vmem([steps, rates]))


def head_conv_kernel(first, heads, x_ref, before_ref, halo_ref, taps_ref, column_ref, *refs):
    xs_ref, wt_ref, ext, spread = refs[-4:]
    length, width = x_ref.shape
    taps = taps_ref.shape[0]
    pairs = width // SUB

    @pl.when(pl.program_id(0) == 0)
    def _():
        for p in range(pairs):
            rows = before_ref if first else halo_ref
            ext[p, :8] = rows[8:16, p * SUB : (p + 1) * SUB].astype(F32)

    for p in range(pairs):
        ext[p, 8:] = x_ref[:, p * SUB : (p + 1) * SUB].astype(F32)
    count = column_ref.shape[1]
    spread[...] = jnp.dot(
        column_ref[...],
        spread_matrix(0, 16, count, width, width // heads),
        preferred_element_type=F32,
    )
    for s in range(length // SUB):
        at = slice(s * SUB, (s + 1) * SUB)
        for p in range(pairs):
            cols = slice(p * SUB, (p + 1) * SUB)
            total = None
            for k in range(taps):
                start = 8 - (taps - 1) + k + s * SUB
                term = taps_ref[k : k + 1, cols] * ext[p, start : start + SUB]
                total = term if total is None else total + term
            xs = silu(total).astype(BF16)
            xs_ref[at, cols] = xs
            wt_ref[at, cols] = (spread[at, cols] * xs.astype(F32)).astype(BF16)
    for p in range(pairs):
        ext[p, :8] = ext[p, length : length + 8]


def head_conv(x_rows, halo, taps, columns, heads, first, count, filled=()):
    length, width = x_rows.shape
    wide = pl.BlockSpec((TILE, width), lambda i: (first + i, 0))
    whole = lambda a: pl.BlockSpec(a.shape, lambda i: (0, 0))
    return pl.pallas_call(
        functools.partial(head_conv_kernel, first, heads),
        grid=(count,),
        in_specs=[
            wide,
            pl.BlockSpec((16, width), lambda i: (max(first * TILE // 16 - 1, 0), 0)),
            whole(halo),
            whole(taps),
            pl.BlockSpec((TILE, columns.shape[1]), lambda i: (first + i, 0)),
        ]
        + [ANYWHERE] * len(filled),
        out_specs=[wide, wide],
        out_shape=[jax.ShapeDtypeStruct((length, width), BF16)] * 2,
        scratch_shapes=[
            pltpu.VMEM((width // SUB, TILE + 8, SUB), F32),
            pltpu.VMEM((TILE, width), F32),
        ],
        compiler_params=params(),
        input_output_aliases={5 + i: i for i in range(len(filled))},
        cost_estimate=BRIEF,
        name="head_conv",
    )(in_hbm(x_rows), in_hbm(x_rows), halo, taps, columns, *filled)


def gates_kernel(z_ref, column_ref, q_ref, gate_ref, factor_ref, start_ref, spread):
    length, width = z_ref.shape
    heads = factor_ref.shape[0] // (length // ROWS)
    size = width // heads
    subs, groups = length // SUB, SUB // ROWS
    columns = column_ref[...]
    to_lanes = spread_matrix(16, 40, columns.shape[1], width, size)
    for p in range(width // SUB):
        spread[p] = jnp.dot(
            columns, to_lanes[:, p * SUB : (p + 1) * SUB], preferred_element_type=F32
        )
    for s in range(subs):
        at = slice(s * SUB, (s + 1) * SUB)
        starts = []
        for p in range(width // SUB):
            cols = slice(p * SUB, (p + 1) * SUB)
            cum = spread[p, at].reshape(groups, ROWS // 8, 8, SUB)
            grown = jnp.exp2(cum - cum[:, ROWS // 16 : ROWS // 16 + 1, :1]).reshape(SUB, SUB)
            gate_ref[at, cols] = grown * silu(z_ref[at, cols].astype(F32))
            start = spread[p, pl.ds(s * SUB + ROWS // 2, groups, stride=ROWS)]
            start_ref[p, s * groups : (s + 1) * groups] = jnp.exp2(start)
            starts.append(start)
        for h in range(heads):
            lane = h * size % SUB
            start = jnp.broadcast_to(starts[h * size // SUB][:, lane : lane + 1], (groups, SUB))
            row = (s * heads + h) * groups
            factor_ref[row : row + groups] = jnp.exp2(
                jnp.minimum(start - q_ref[h : h + 1, at], 64.0)
            )


def gates(z_rows, columns, q, heads):
    length, width = z_rows.shape
    wide = pl.BlockSpec((TILE, width), lambda i: (i, 0))
    rows = pl.BlockSpec((8, TILE), lambda i: (0, i))
    return pl.pallas_call(
        gates_kernel,
        grid=(length // TILE,),
        in_specs=[wide, pl.BlockSpec((TILE, columns.shape[1]), lambda i: (i, 0)), rows],
        out_specs=[
            wide,
            pl.BlockSpec((TILE // ROWS * heads, SUB), lambda i: (i, 0)),
            pl.BlockSpec((width // SUB, TILE // ROWS, SUB), lambda i: (0, i, 0)),
        ],
        out_shape=[
            jax.ShapeDtypeStruct((length, width), F32),
            jax.ShapeDtypeStruct((length // ROWS * heads, SUB), F32),
            jax.ShapeDtypeStruct((width // SUB, length // ROWS, SUB), F32),
        ],
        scratch_shapes=[pltpu.VMEM((width // SUB, TILE, SUB), F32)],
        compiler_params=params(),
        cost_estimate=BRIEF,
        name="gates",
    )(z_rows, columns, q)


def columns_of(refs, rows, at):
    return jnp.concatenate([ref[first:last, at] for ref, (first, last) in zip(refs, rows)], axis=0)


def columns_from(refs, rows, begins, start):
    parts = [
        ref[first:last, pl.ds(pl.multiple_of(start - begin, SUB), SUB)]
        for ref, (first, last), begin in zip(refs, rows, begins)
    ]
    return jnp.concatenate(parts, axis=0)


def last_state_kernel(rows, wt_ref, decay_ref, *refs):
    pieces, (out_ref, local_ref, before_ref, state, total) = refs[:-5], refs[-5:]
    size = state.shape[0]
    subs = TILE // SUB
    state[...] = jnp.zeros_like(state)
    total[...] = jnp.ones_like(total)

    def tile(t, _):
        held, grown = state[...], total[:1]
        row = pl.multiple_of(t * subs, subs)
        decays = decay_ref[pl.ds(row, subs)]
        products = []
        for s in range(subs):
            at = pl.ds(pl.multiple_of(t * TILE + s * SUB, SUB), SUB)
            b_cols = columns_of(pieces, rows, at)
            added = jnp.dot(b_cols, wt_ref[at], preferred_element_type=F32)
            local_ref[pl.ds(pl.multiple_of((t * subs + s) * size, size), size)] = held
            products.append(grown)
            held = held * decays[s : s + 1] + added
            grown = grown * decays[s : s + 1]
        before_ref[pl.ds(row, subs)] = jnp.concatenate(products, axis=0)
        state[...] = held
        total[...] = jnp.broadcast_to(grown, total.shape)
        return 0

    lax.fori_loop(0, wt_ref.shape[0] // TILE, tile, 0)
    out_ref[:size] = state[...].astype(BF16)
    out_ref[size:] = jnp.broadcast_to(total[:1], (16, total.shape[1])).astype(BF16)


def last_state(weighted, decays, pieces, rows):
    length, width = weighted.shape
    size = sum(last - first for first, last in rows)
    count = length // SUB
    return pl.pallas_call(
        functools.partial(last_state_kernel, rows),
        in_specs=[IN_VMEM] * (2 + len(pieces)),
        out_specs=[IN_VMEM] * 3,
        out_shape=[
            jax.ShapeDtypeStruct((size + 16, width), BF16),
            pltpu.VMEM((count * size, width), F32),
            pltpu.VMEM((count, width), F32),
        ],
        scratch_shapes=[pltpu.VMEM((size, width), F32), pltpu.VMEM((8, width), F32)],
        compiler_params=params(),
        cost_estimate=BRIEF,
        name="last_state",
    )(*in_vmem([weighted, decays, *pieces]))


def join_kernel(bit, mine_ref, other_ref, token_ref, out_ref):
    size = mine_ref.shape[0] - 16
    upper = jnp.bitwise_and(lax.axis_index("seq"), bit) != 0
    mine, other = mine_ref[...].astype(F32), other_ref[...].astype(F32)
    early, late = jnp.where(upper, other, mine), jnp.where(upper, mine, other)
    decay = late[size : size + 1]
    out_ref[:size] = (early[:size] * decay + late[:size]).astype(BF16)
    out_ref[size:] = (early[size:] * decay).astype(BF16)


def join(bit, mine, other, token):
    return pl.pallas_call(
        functools.partial(join_kernel, bit),
        in_specs=[IN_VMEM, IN_VMEM, ANYWHERE],
        out_specs=IN_VMEM,
        out_shape=jax.ShapeDtypeStruct(mine.shape, BF16),
        compiler_params=params(),
        cost_estimate=BRIEF,
        name="join",
    )(*in_vmem([mine, other]), token)


def scan_kernel(
    span, count, b_rows, b_picks, c_rows_of, c_picks, c_begins, gate_ref, factor_ref, start_ref, xs_ref,
    local_ref, before_ref, *refs
):
    others, refs = refs[:count], refs[count:]
    b_refs, c_refs = [refs[i] for i in b_picks], [refs[i] for i in c_picks]
    gated_ref, square_ref, carry, c_rows, scores, carried, squares = refs[-7:]
    length, width = gate_ref.shape
    heads = factor_ref.shape[0] // (length // ROWS)
    groups, subs, pairs = SUB // ROWS, TILE // SUB, width // SUB
    size = carry.shape[0]
    entering = jnp.zeros(carry.shape, F32)
    for k in reversed(range(count)):
        end = others[k][...].astype(F32)
        longer = entering * end[size : size + 1] + end[:size]
        entering = jnp.where(jnp.bitwise_and(lax.axis_index("seq"), 1 << k) != 0, longer, entering)
    carry[...] = entering
    i = lax.broadcasted_iota(jnp.int32, (SUB, SUB), 0)
    j = lax.broadcasted_iota(jnp.int32, (SUB, SUB), 1)
    causal = i >= j
    low = (j < SUB // 2).astype(F32)
    keep_low, keep_high = low.astype(BF16), (1.0 - low).astype(BF16)

    def rows_times(value, load):
        rows = [value[g * ROWS : (g + 1) * ROWS] * load(g) for g in range(groups)]
        return jnp.concatenate(rows, axis=0)

    def repeated(ref, row):
        return jnp.broadcast_to(ref[pl.ds(row, 1)], (ROWS, SUB))

    local = [slice(s * SUB, (s + 1) * SUB) for s in range(subs)]

    def tile(t, _):
        whole = [pl.ds(pl.multiple_of(t * TILE + s * SUB, SUB), SUB) for s in range(subs)]
        row = pl.multiple_of(t * subs, subs)
        factors = pl.multiple_of(t * (subs * heads * groups), subs * heads * groups)
        starts = pl.multiple_of(t * (subs * groups), subs * groups)

        decays = before_ref[pl.ds(row, subs)]

        def turn(s):
            c_rows[local[s]] = columns_from(c_refs, c_rows_of, c_begins, t * TILE + s * SUB).T

        def products(s):
            b_cols = columns_of(b_refs, b_rows, whole[s])
            held = pl.ds(pl.multiple_of((t * subs + s) * size, size), size)
            state = local_ref[held] + carry[...] * decays[s : s + 1]
            both = jnp.dot(
                c_rows[local[s]],
                jnp.concatenate([b_cols, state.astype(BF16)], axis=1),
                preferred_element_type=F32,
            )
            scores[local[s]] = jnp.where(causal, both[:, :SUB], 0.0)
            carried[local[s]] = both[:, SUB:]

        turn(0)
        turn(1)
        products(0)
        for s, at in enumerate(whole):
            if s + 2 < subs:
                turn(s + 2)
            if s + 1 < subs:
                products(s + 1)
            total = None
            score = scores[local[s]]
            for p in range(pairs):
                cols = slice(p * SUB, (p + 1) * SUB)
                mixing = []
                for h in (2 * p, 2 * p + 1):
                    base = factors + (s * heads + h) * groups
                    mixing.append(rows_times(score, lambda g: repeated(factor_ref, base + g)).astype(BF16))
                xs = xs_ref[at, cols]
                mixed = jnp.dot(
                    jnp.concatenate(mixing, axis=1),
                    jnp.concatenate([xs * keep_low, xs * keep_high], axis=0),
                    preferred_element_type=F32,
                )
                base = starts + s * groups
                before = rows_times(carried[local[s], cols], lambda g: repeated(start_ref.at[p], base + g))
                gated = gate_ref[at, cols] * (mixed + before)
                gated_ref[at, cols] = gated.astype(BF16)
                square = gated * gated
                total = square if total is None else total + square
            squares[local[s]] = total.astype(BF16)
        sums = lax.dot_general(
            jnp.ones((8, SUB), BF16), squares[...], (((1,), (1,)), ((), ())), preferred_element_type=F32
        )
        square_ref[pl.ds(row, subs)] = jnp.concatenate([sums[:1, at] for at in local], axis=0)
        return 0

    lax.fori_loop(*span, tile, 0)


def scan(span, gate, factor, start, xs, local, before, others, b_pieces, b_rows, c_pieces, c_rows, c_begins, filled=()):
    length, width = xs.shape
    size = sum(last - first for first, last in b_rows)
    pieces = []
    for piece in b_pieces + c_pieces:
        if not any(piece is other for other in pieces):
            pieces.append(piece)
    picks = lambda some: [next(i for i, q in enumerate(pieces) if q is p) for p in some]
    operands = [gate, factor, start, xs, local, before, *others, *pieces, *filled]
    first = len(operands) - len(filled)
    return pl.pallas_call(
        functools.partial(
            scan_kernel, span, len(others), b_rows, picks(b_pieces), c_rows, picks(c_pieces), c_begins
        ),
        in_specs=[IN_VMEM] * len(operands),
        out_specs=[IN_VMEM, IN_VMEM],
        out_shape=[pltpu.VMEM((length, width), BF16), pltpu.VMEM((length // SUB, SUB), F32)],
        scratch_shapes=[
            pltpu.VMEM((size, width), F32),
            pltpu.VMEM((TILE, size), BF16),
            pltpu.VMEM((TILE, SUB), F32),
            pltpu.VMEM((TILE, width), F32),
            pltpu.VMEM((TILE, SUB), BF16),
        ],
        input_output_aliases={first + i: i for i in range(len(filled))},
        compiler_params=params(),
        cost_estimate=BRIEF,
        name="scan",
    )(*in_vmem(operands))


def norm_kernel(channels, gated_ref, gain_ref, *refs):
    squares, (out_ref, rows, sems) = refs[:-3], refs[-3:]
    total = squares[0][...]
    for ref in squares[1:]:
        total = total + ref[...]
    scale = lax.rsqrt(total * (1.0 / channels) + 1e-05).T
    gain = gain_ref[...]
    step = 2 * SUB
    copies = []
    for t in range(gated_ref.shape[0] // step):
        for s in range(t * step // SUB, (t + 1) * step // SUB):
            at = slice(s * SUB, (s + 1) * SUB)
            rows[at] = (gated_ref[at].astype(F32) * scale[:, s : s + 1] * gain).astype(BF16)
        at = slice(t * step, (t + 1) * step)
        copies.append(pltpu.make_async_copy(rows.at[at], out_ref.at[at], sems.at[t]))
        copies[-1].start()
    for copy in copies:
        copy.wait()


def norm(channels, gated, gain, squares):
    length, width = gated.shape
    operands = [gated, gain, *squares]
    return pl.pallas_call(
        functools.partial(norm_kernel, channels),
        in_specs=[IN_VMEM] * len(operands),
        out_specs=ANYWHERE,
        out_shape=pltpu.HBM((length, width), BF16),
        scratch_shapes=[
            pltpu.VMEM((length, width), BF16),
            pltpu.SemaphoreType.DMA((length // (2 * SUB),)),
        ],
        compiler_params=params(),
        cost_estimate=BRIEF,
        name="norm",
    )(*in_vmem(operands))


def body(x_rows, z_rows, b_rows, c_rows, step_raw, conv_x, conv_b, conv_c, decay_rate, norm_gain):
    length, width = x_rows.shape
    local_heads = decay_rate.shape[0]
    seq, heads = lax.axis_size("seq"), lax.axis_size("head")
    b_cols, c_cols = b_rows.T, c_rows.T
    ends, b_cols, c_cols = tails(x_rows, b_cols, c_cols)
    halo = lax.ppermute(ends, "seq", [(i, i + 1) for i in range(seq - 1)])
    bs, cs, cs_sent = shared_conv(b_cols, c_cols, halo, conv_b.T.astype(F32), conv_c.T.astype(F32))
    cols = bs.shape[0]
    outer, _ = factors(heads)
    tiles = x_rows.shape[0] // TILE
    q, columns, decays = rows_of(step_raw.T, decay_rate[:, None], width)
    conv = functools.partial(head_conv, x_rows, halo, conv_x.astype(F32), columns, local_heads)
    if cols % 16 or factors(heads) != (4, 2):
        b_pieces, c_pieces = [
            [jnp.concatenate(near + along_inner(near), axis=0)]
            for near in ([own] + along_outer(own) for own in (bs, cs))
        ]
        b_rows = c_rows = [(0, b_pieces[0].shape[0])]
        xs, weighted = conv(0, tiles)
        mine, local, before = last_state(weighted, decays, b_pieces, b_rows)
        gate, factor, start = gates(z_rows, columns, q, local_heads)
        token, tail, runs = mine, [], [((0, tiles), None, None)]
    else:
        one = (0, cols)
        b_outer, own, c_own = along_outer(bs), along_inner([bs]), along_inner([cs])
        xs, weighted = conv(0, tiles)
        (b_packed,) = pack(b_outer, [one] * 3, xs, *own, *c_own)
        b_passed = along_inner([b_packed])
        cs_sent, columns = after([cs_sent, columns], b_packed)
        c_outer = along_outer(cs_sent)
        gate, factor, start = gates(z_rows, columns, q, local_heads)
        c_outer[:1] = after(c_outer[:1], start)
        c_passed = c_own + along_inner(c_outer[:1])
        (decays,) = after([decays], c_outer[0])
        b_pieces = [bs, *own, *b_outer, *b_passed]
        b_rows = [one] * 5 + [(0, 3 * cols)]
        mine, local, before = last_state(weighted, decays, b_pieces, b_rows)
        cut = -(-tiles // 2) * TILE
        c_rest = pack(c_outer[:0:-1], [one] * 2, mine, c_passed[1], cuts=[0, cut, length])
        c_ends = along_inner(c_rest)
        c_pieces = [cs, *c_own, *c_outer, c_passed[1]]
        c_rows = [one] * 6
        token, tail = c_rest[0], [(cols, 2 * cols), one]
        runs = [((0, cut // TILE), c_ends[0], 0), ((cut // TILE, tiles), c_ends[1], cut)]
    others, bit = [], 1
    while bit < seq:
        last = 2 * bit == seq
        pairs = [(i, i ^ bit) for i in range(seq) if not (last and i & bit)]
        others.append(lax.ppermute(mine, "seq", pairs))
        if not last:
            mine = join(bit, mine, others[-1], token)
        bit *= 2
    filled = ()
    for span, piece, begin in runs:
        filled = scan(
            span, gate, factor, start, xs, local, before, others, b_pieces, b_rows,
            c_pieces + [piece] * len(tail), c_rows + tail, [0] * len(c_pieces) + [begin] * len(tail), filled,
        )
    gated, square = filled
    square = square + sum(along_outer(square))
    squares = [square] + along_inner([square])
    return norm(heads * width, gated, norm_gain[None, :], squares)


def solution(mesh):
    placed = (
        P("seq", "head"),
        P("seq", "head"),
        P("seq", "head"),
        P("seq", "head"),
        P("seq", "head"),
        P(None, "head"),
        P(None, "head"),
        P(None, "head"),
        P("head"),
        P("head"),
    )
    return jax.shard_map(
        body, mesh=mesh, in_specs=placed, out_specs=P("seq", "head"), check_vma=False
    )
```

```python
import functools
import math

import jax
import jax.numpy as jnp
from jax import lax
from jax.experimental import pallas as pl
from jax.experimental.pallas import tpu as pltpu
from jax.sharding import PartitionSpec as P

SUB = 128
ROWS = 16
TILE = 8 * SUB
LOG2E = math.log2(math.e)
MIB = 1024 * 1024
F32, BF16 = jnp.float32, jnp.bfloat16


def params(mib=16):
    return pltpu.CompilerParams(vmem_limit_bytes=mib * MIB)


def in_hbm(value):
    return pltpu.with_memory_space_constraint(value, pltpu.HBM)


def in_vmem(values):
    return [pltpu.with_memory_space_constraint(value, pltpu.VMEM) for value in values]


IN_VMEM = pl.BlockSpec(memory_space=pltpu.VMEM)
BRIEF = pl.CostEstimate(flops=1000, bytes_accessed=1000, transcendentals=0)
ANYWHERE = pl.BlockSpec(memory_space=pl.ANY)


def silu(value):
    half = 0.5 * value
    return half * jnp.tanh(half) + half


def factors(count):
    inner = max(d for d in range(1, math.isqrt(count) + 1) if count % d == 0)
    return count // inner, inner


def outer_pairs(d):
    outer, inner = factors(lax.axis_size("head"))
    return [(z * inner + y, (z + d) % outer * inner + y) for z in range(outer) for y in range(inner)]


def inner_pairs(e):
    outer, inner = factors(lax.axis_size("head"))
    return [(z * inner + y, z * inner + (y + e) % inner) for z in range(outer) for y in range(inner)]


def along_outer(piece):
    outer, _ = factors(lax.axis_size("head"))
    return [lax.ppermute(piece, "head", outer_pairs(d)) for d in range(1, outer)]


def along_inner(pieces):
    _, inner = factors(lax.axis_size("head"))
    return [lax.ppermute(p, "head", inner_pairs(e)) for e in range(1, inner) for p in pieces]


def tie_kernel(*refs):
    pass


def after(values, *tokens):
    out = pl.pallas_call(
        tie_kernel,
        in_specs=[ANYWHERE] * (len(values) + len(tokens)),
        out_specs=[ANYWHERE] * len(values),
        out_shape=[jax.ShapeDtypeStruct(v.shape, v.dtype) for v in values],
        input_output_aliases={i: i for i in range(len(values))},
        compiler_params=params(1),
        cost_estimate=BRIEF,
        name="tie",
    )(*values, *tokens)
    return list(out)


def pack_kernel(rows, cuts, *refs):
    outs = refs[len(refs) - len(cuts) + 1 :]
    for out_ref, first_token, last_token in zip(outs, cuts[:-1], cuts[1:]):
        row = 0
        for ref, (first, last) in zip(refs, rows):
            out_ref[row : row + last - first] = ref[first:last, first_token:last_token]
            row += last - first


def pack(pieces, rows, *tokens, cuts=None):
    cuts = cuts or [0, pieces[0].shape[1]]
    count = sum(last - first for first, last in rows)
    return pl.pallas_call(
        functools.partial(pack_kernel, rows, cuts),
        in_specs=[IN_VMEM] * len(pieces) + [ANYWHERE] * len(tokens),
        out_specs=[IN_VMEM] * (len(cuts) - 1),
        out_shape=[
            pltpu.VMEM((count, last - first), pieces[0].dtype) for first, last in zip(cuts[:-1], cuts[1:])
        ],
        compiler_params=params(),
        cost_estimate=BRIEF,
        name="pack",
    )(*in_vmem(pieces), *tokens)


def tails_kernel(x_ref, b_ref, c_ref, out_ref, b_out, c_out):
    cols, length = b_ref.shape
    out_ref[...] = jnp.zeros_like(out_ref)
    out_ref[:16] = x_ref[...]
    out_ref[16 : 16 + cols, :SUB] = b_ref[:, length - SUB :]
    out_ref[32 : 32 + cols, :SUB] = c_ref[:, length - SUB :]
    b_out[...] = b_ref[...]
    c_out[...] = c_ref[...]


def tails(x_rows, b_cols, c_cols):
    length, width = x_rows.shape
    cols = b_cols.shape[0]
    whole = pl.BlockSpec((cols, length), lambda i: (0, 0))
    held = pltpu.VMEM((cols, length), BF16)
    return pl.pallas_call(
        tails_kernel,
        grid=(1,),
        in_specs=[pl.BlockSpec((16, width), lambda i: (length // 16 - 1, 0)), whole, whole],
        out_specs=[pl.BlockSpec((48, width), lambda i: (0, 0)), IN_VMEM, IN_VMEM],
        out_shape=[jax.ShapeDtypeStruct((48, width), BF16), held, held],
        compiler_params=params(),
        cost_estimate=BRIEF,
        name="tails",
    )(in_hbm(x_rows), in_hbm(b_cols), in_hbm(c_cols))


def conv_columns(rows, halo, taps):
    wide = jnp.concatenate([halo, rows], axis=1).astype(F32)
    width = taps.shape[1]
    total = None
    for k in range(width):
        lag = width - 1 - k
        moved = pltpu.roll(wide, lag, axis=1) if lag else wide
        term = taps[:, k : k + 1] * moved[:, SUB:]
        total = term if total is None else total + term
    return silu(total).astype(BF16)


def shared_conv_kernel(b_ref, c_ref, halo_ref, tb_ref, tc_ref, bs_ref, cs_ref, again_ref):
    cols = b_ref.shape[0]
    bs_ref[...] = conv_columns(b_ref[...], halo_ref[16 : 16 + cols, :SUB], tb_ref[...])
    cs = conv_columns(c_ref[...], halo_ref[32 : 32 + cols, :SUB], tc_ref[...])
    cs_ref[...], again_ref[...] = cs, cs


def shared_conv(b_cols, c_cols, halo, taps_b, taps_c):
    operands = [b_cols, c_cols, halo, taps_b, taps_c]
    return pl.pallas_call(
        shared_conv_kernel,
        in_specs=[IN_VMEM] * 5,
        out_specs=[IN_VMEM] * 3,
        out_shape=[pltpu.VMEM(b_cols.shape, BF16)] * 3,
        compiler_params=params(),
        cost_estimate=BRIEF,
        name="shared_conv",
    )(*in_vmem(operands))


def parts_of(value, count):
    parts = []
    for _ in range(count):
        part = value.astype(BF16).astype(F32)
        parts.append(part)
        value = value - part
    return jnp.concatenate(parts, axis=0)


def spread_matrix(first, last, count, width, size):
    i = lax.broadcasted_iota(jnp.int32, (count, width), 0)
    j = lax.broadcasted_iota(jnp.int32, (count, width), 1)
    head = jnp.bitwise_and(i, 7) * size
    lanes = jnp.logical_and(j >= head, j < head + size)
    return jnp.logical_and(lanes, jnp.logical_and(i >= first, i < last)).astype(F32).astype(BF16)


def rows_kernel(step_ref, rate_ref, q_ref, column_ref, decay_ref, sp, ld):
    heads, length = step_ref.shape
    width = decay_ref.shape[1]
    subs = length // SUB
    raw = step_ref[...]
    soft = jnp.maximum(raw, 0.0) + jnp.log(1.0 + jnp.exp(-jnp.abs(raw)))
    sp[...] = jnp.ones_like(sp)
    ld[...] = jnp.zeros_like(ld)
    sp[:heads] = soft
    ld[:heads] = soft * (rate_ref[...] * -LOG2E)
    i = lax.broadcasted_iota(jnp.int32, (SUB, SUB), 0)
    j = lax.broadcasted_iota(jnp.int32, (SUB, SUB), 1)
    upper = (i <= j).astype(F32)
    logs = ld[...]
    stacked = jnp.concatenate([logs[:, s * SUB : (s + 1) * SUB] for s in range(subs)], axis=0)
    sums = jnp.dot(stacked, upper, precision=lax.Precision.HIGHEST, preferred_element_type=F32)
    log_step = jnp.log(sp[...]) * LOG2E
    lasts = []
    for s in range(subs):
        at = slice(s * SUB, (s + 1) * SUB)
        cum = sums[s * 8 : (s + 1) * 8]
        q = cum - log_step[:, at]
        q_ref[:, at] = q
        weight = jnp.exp2(cum[:, SUB - 1 :] - q)
        columns = jnp.concatenate([parts_of(weight, 2), parts_of(cum, 3)], axis=0).T
        column_ref[at] = columns.astype(BF16)
        lasts.append(columns[SUB - 1 :])
    whole = jnp.concatenate(lasts, axis=0).astype(BF16)
    to_lanes = spread_matrix(16, 40, 40, width, width // heads)
    decay_ref[...] = jnp.exp2(jnp.dot(whole, to_lanes, preferred_element_type=F32))


def rows_of(steps, rates, width):
    heads, length = steps.shape
    return pl.pallas_call(
        rows_kernel,
        in_specs=[IN_VMEM] * 2,
        out_specs=[IN_VMEM] * 3,
        out_shape=[
            pltpu.VMEM((8, length), F32),
            pltpu.VMEM((length, 40), BF16),
            pltpu.VMEM((length // SUB, width), F32),
        ],
        scratch_shapes=[pltpu.VMEM((8, length), F32), pltpu.VMEM((8, length), F32)],
        compiler_params=params(),
        cost_estimate=BRIEF,
        name="rows",
    )(*in_vmem([steps, rates]))


def head_conv_kernel(first, heads, x_ref, before_ref, halo_ref, taps_ref, column_ref, *refs):
    xs_ref, wt_ref, ext, spread = refs[-4:]
    length, width = x_ref.shape
    taps = taps_ref.shape[0]
    pairs = width // SUB

    @pl.when(pl.program_id(0) == 0)
    def _():
        for p in range(pairs):
            rows = before_ref if first else halo_ref
            ext[p, :8] = rows[8:16, p * SUB : (p + 1) * SUB].astype(F32)

    for p in range(pairs):
        ext[p, 8:] = x_ref[:, p * SUB : (p + 1) * SUB].astype(F32)
    count = column_ref.shape[1]
    spread[...] = jnp.dot(
        column_ref[...],
        spread_matrix(0, 16, count, width, width // heads),
        preferred_element_type=F32,
    )
    for s in range(length // SUB):
        at = slice(s * SUB, (s + 1) * SUB)
        for p in range(pairs):
            cols = slice(p * SUB, (p + 1) * SUB)
            total = None
            for k in range(taps):
                start = 8 - (taps - 1) + k + s * SUB
                term = taps_ref[k : k + 1, cols] * ext[p, start : start + SUB]
                total = term if total is None else total + term
            xs = silu(total).astype(BF16)
            xs_ref[at, cols] = xs
            wt_ref[at, cols] = (spread[at, cols] * xs.astype(F32)).astype(BF16)
    for p in range(pairs):
        ext[p, :8] = ext[p, length : length + 8]


def head_conv(x_rows, halo, taps, columns, heads, first, count, filled=()):
    length, width = x_rows.shape
    wide = pl.BlockSpec((TILE, width), lambda i: (first + i, 0))
    whole = lambda a: pl.BlockSpec(a.shape, lambda i: (0, 0))
    return pl.pallas_call(
        functools.partial(head_conv_kernel, first, heads),
        grid=(count,),
        in_specs=[
            wide,
            pl.BlockSpec((16, width), lambda i: (max(first * TILE // 16 - 1, 0), 0)),
            whole(halo),
            whole(taps),
            pl.BlockSpec((TILE, columns.shape[1]), lambda i: (first + i, 0)),
        ]
        + [ANYWHERE] * len(filled),
        out_specs=[wide, wide],
        out_shape=[jax.ShapeDtypeStruct((length, width), BF16)] * 2,
        scratch_shapes=[
            pltpu.VMEM((width // SUB, TILE + 8, SUB), F32),
            pltpu.VMEM((TILE, width), F32),
        ],
        compiler_params=params(),
        input_output_aliases={5 + i: i for i in range(len(filled))},
        cost_estimate=BRIEF,
        name="head_conv",
    )(in_hbm(x_rows), in_hbm(x_rows), halo, taps, columns, *filled)


def gates_kernel(z_ref, column_ref, q_ref, gate_ref, factor_ref, start_ref, spread):
    length, width = z_ref.shape
    heads = factor_ref.shape[0] // (length // ROWS)
    size = width // heads
    subs, groups = length // SUB, SUB // ROWS
    columns = column_ref[...]
    to_lanes = spread_matrix(16, 40, columns.shape[1], width, size)
    for p in range(width // SUB):
        spread[p] = jnp.dot(
            columns, to_lanes[:, p * SUB : (p + 1) * SUB], preferred_element_type=F32
        )
    for s in range(subs):
        at = slice(s * SUB, (s + 1) * SUB)
        starts = []
        for p in range(width // SUB):
            cols = slice(p * SUB, (p + 1) * SUB)
            cum = spread[p, at].reshape(groups, ROWS // 8, 8, SUB)
            grown = jnp.exp2(cum - cum[:, ROWS // 16 : ROWS // 16 + 1, :1]).reshape(SUB, SUB)
            gate_ref[at, cols] = grown * silu(z_ref[at, cols].astype(F32))
            start = spread[p, pl.ds(s * SUB + ROWS // 2, groups, stride=ROWS)]
            start_ref[p, s * groups : (s + 1) * groups] = jnp.exp2(start)
            starts.append(start)
        for h in range(heads):
            lane = h * size % SUB
            start = jnp.broadcast_to(starts[h * size // SUB][:, lane : lane + 1], (groups, SUB))
            row = (s * heads + h) * groups
            factor_ref[row : row + groups] = jnp.exp2(
                jnp.minimum(start - q_ref[h : h + 1, at], 64.0)
            )


def gates(z_rows, columns, q, heads):
    length, width = z_rows.shape
    wide = pl.BlockSpec((TILE, width), lambda i: (i, 0))
    rows = pl.BlockSpec((8, TILE), lambda i: (0, i))
    return pl.pallas_call(
        gates_kernel,
        grid=(length // TILE,),
        in_specs=[wide, pl.BlockSpec((TILE, columns.shape[1]), lambda i: (i, 0)), rows],
        out_specs=[
            wide,
            pl.BlockSpec((TILE // ROWS * heads, SUB), lambda i: (i, 0)),
            pl.BlockSpec((width // SUB, TILE // ROWS, SUB), lambda i: (0, i, 0)),
        ],
        out_shape=[
            jax.ShapeDtypeStruct((length, width), F32),
            jax.ShapeDtypeStruct((length // ROWS * heads, SUB), F32),
            jax.ShapeDtypeStruct((width // SUB, length // ROWS, SUB), F32),
        ],
        scratch_shapes=[pltpu.VMEM((width // SUB, TILE, SUB), F32)],
        compiler_params=params(),
        cost_estimate=BRIEF,
        name="gates",
    )(z_rows, columns, q)


def columns_of(refs, rows, at):
    return jnp.concatenate([ref[first:last, at] for ref, (first, last) in zip(refs, rows)], axis=0)


def columns_from(refs, rows, begins, start):
    parts = [
        ref[first:last, pl.ds(pl.multiple_of(start - begin, SUB), SUB)]
        for ref, (first, last), begin in zip(refs, rows, begins)
    ]
    return jnp.concatenate(parts, axis=0)


def last_state_kernel(rows, wt_ref, decay_ref, *refs):
    pieces, (out_ref, local_ref, before_ref, state, total) = refs[:-5], refs[-5:]
    size = state.shape[0]
    subs = TILE // SUB
    state[...] = jnp.zeros_like(state)
    total[...] = jnp.ones_like(total)

    def tile(t, _):
        held, grown = state[...], total[:1]
        row = pl.multiple_of(t * subs, subs)
        decays = decay_ref[pl.ds(row, subs)]
        products = []
        for s in range(subs):
            at = pl.ds(pl.multiple_of(t * TILE + s * SUB, SUB), SUB)
            b_cols = columns_of(pieces, rows, at)
            added = jnp.dot(b_cols, wt_ref[at], preferred_element_type=F32)
            local_ref[pl.ds(pl.multiple_of((t * subs + s) * size, size), size)] = held
            products.append(grown)
            held = held * decays[s : s + 1] + added
            grown = grown * decays[s : s + 1]
        before_ref[pl.ds(row, subs)] = jnp.concatenate(products, axis=0)
        state[...] = held
        total[...] = jnp.broadcast_to(grown, total.shape)
        return 0

    lax.fori_loop(0, wt_ref.shape[0] // TILE, tile, 0)
    out_ref[:size] = state[...].astype(BF16)
    out_ref[size:] = jnp.broadcast_to(total[:1], (16, total.shape[1])).astype(BF16)


def last_state(weighted, decays, pieces, rows):
    length, width = weighted.shape
    size = sum(last - first for first, last in rows)
    count = length // SUB
    return pl.pallas_call(
        functools.partial(last_state_kernel, rows),
        in_specs=[IN_VMEM] * (2 + len(pieces)),
        out_specs=[IN_VMEM] * 3,
        out_shape=[
            jax.ShapeDtypeStruct((size + 16, width), BF16),
            pltpu.VMEM((count * size, width), F32),
            pltpu.VMEM((count, width), F32),
        ],
        scratch_shapes=[pltpu.VMEM((size, width), F32), pltpu.VMEM((8, width), F32)],
        compiler_params=params(),
        cost_estimate=BRIEF,
        name="last_state",
    )(*in_vmem([weighted, decays, *pieces]))


def join_kernel(bit, mine_ref, other_ref, token_ref, out_ref):
    size = mine_ref.shape[0] - 16
    upper = jnp.bitwise_and(lax.axis_index("seq"), bit) != 0
    mine, other = mine_ref[...].astype(F32), other_ref[...].astype(F32)
    early, late = jnp.where(upper, other, mine), jnp.where(upper, mine, other)
    decay = late[size : size + 1]
    out_ref[:size] = (early[:size] * decay + late[:size]).astype(BF16)
    out_ref[size:] = (early[size:] * decay).astype(BF16)


def join(bit, mine, other, token):
    return pl.pallas_call(
        functools.partial(join_kernel, bit),
        in_specs=[IN_VMEM, IN_VMEM, ANYWHERE],
        out_specs=IN_VMEM,
        out_shape=jax.ShapeDtypeStruct(mine.shape, BF16),
        compiler_params=params(),
        cost_estimate=BRIEF,
        name="join",
    )(*in_vmem([mine, other]), token)


def scan_kernel(
    span, count, b_rows, b_picks, c_rows_of, c_picks, c_begins, gate_ref, factor_ref, start_ref, xs_ref,
    local_ref, before_ref, *refs
):
    others, refs = refs[:count], refs[count:]
    b_refs, c_refs = [refs[i] for i in b_picks], [refs[i] for i in c_picks]
    gated_ref, square_ref, carry, c_rows, scores, carried, squares = refs[-7:]
    length, width = gate_ref.shape
    heads = factor_ref.shape[0] // (length // ROWS)
    groups, subs, pairs = SUB // ROWS, TILE // SUB, width // SUB
    size = carry.shape[0]
    entering = jnp.zeros(carry.shape, F32)
    for k in reversed(range(count)):
        end = others[k][...].astype(F32)
        longer = entering * end[size : size + 1] + end[:size]
        entering = jnp.where(jnp.bitwise_and(lax.axis_index("seq"), 1 << k) != 0, longer, entering)
    carry[...] = entering
    i = lax.broadcasted_iota(jnp.int32, (SUB, SUB), 0)
    j = lax.broadcasted_iota(jnp.int32, (SUB, SUB), 1)
    causal = i >= j
    low = (j < SUB // 2).astype(F32)
    keep_low, keep_high = low.astype(BF16), (1.0 - low).astype(BF16)

    def rows_times(value, load):
        rows = [value[g * ROWS : (g + 1) * ROWS] * load(g) for g in range(groups)]
        return jnp.concatenate(rows, axis=0)

    def repeated(ref, row):
        return jnp.broadcast_to(ref[pl.ds(row, 1)], (ROWS, SUB))

    local = [slice(s * SUB, (s + 1) * SUB) for s in range(subs)]

    def tile(t, _):
        whole = [pl.ds(pl.multiple_of(t * TILE + s * SUB, SUB), SUB) for s in range(subs)]
        row = pl.multiple_of(t * subs, subs)
        factors = pl.multiple_of(t * (subs * heads * groups), subs * heads * groups)
        starts = pl.multiple_of(t * (subs * groups), subs * groups)

        decays = before_ref[pl.ds(row, subs)]

        def turn(s):
            c_rows[local[s]] = columns_from(c_refs, c_rows_of, c_begins, t * TILE + s * SUB).T

        def products(s):
            b_cols = columns_of(b_refs, b_rows, whole[s])
            held = pl.ds(pl.multiple_of((t * subs + s) * size, size), size)
            state = local_ref[held] + carry[...] * decays[s : s + 1]
            both = jnp.dot(
                c_rows[local[s]],
                jnp.concatenate([b_cols, state.astype(BF16)], axis=1),
                preferred_element_type=F32,
            )
            scores[local[s]] = jnp.where(causal, both[:, :SUB], 0.0)
            carried[local[s]] = both[:, SUB:]

        turn(0)
        turn(1)
        products(0)
        for s, at in enumerate(whole):
            if s + 2 < subs:
                turn(s + 2)
            if s + 1 < subs:
                products(s + 1)
            total = None
            score = scores[local[s]]
            for p in range(pairs):
                cols = slice(p * SUB, (p + 1) * SUB)
                mixing = []
                for h in (2 * p, 2 * p + 1):
                    base = factors + (s * heads + h) * groups
                    mixing.append(rows_times(score, lambda g: repeated(factor_ref, base + g)).astype(BF16))
                xs = xs_ref[at, cols]
                mixed = jnp.dot(
                    jnp.concatenate(mixing, axis=1),
                    jnp.concatenate([xs * keep_low, xs * keep_high], axis=0),
                    preferred_element_type=F32,
                )
                base = starts + s * groups
                before = rows_times(carried[local[s], cols], lambda g: repeated(start_ref.at[p], base + g))
                gated = gate_ref[at, cols] * (mixed + before)
                gated_ref[at, cols] = gated.astype(BF16)
                square = gated * gated
                total = square if total is None else total + square
            squares[local[s]] = total.astype(BF16)
        sums = lax.dot_general(
            jnp.ones((8, SUB), BF16), squares[...], (((1,), (1,)), ((), ())), preferred_element_type=F32
        )
        square_ref[pl.ds(row, subs)] = jnp.concatenate([sums[:1, at] for at in local], axis=0)
        return 0

    lax.fori_loop(*span, tile, 0)


def scan(span, gate, factor, start, xs, local, before, others, b_pieces, b_rows, c_pieces, c_rows, c_begins, filled=()):
    length, width = xs.shape
    size = sum(last - first for first, last in b_rows)
    pieces = []
    for piece in b_pieces + c_pieces:
        if not any(piece is other for other in pieces):
            pieces.append(piece)
    picks = lambda some: [next(i for i, q in enumerate(pieces) if q is p) for p in some]
    operands = [gate, factor, start, xs, local, before, *others, *pieces, *filled]
    first = len(operands) - len(filled)
    return pl.pallas_call(
        functools.partial(
            scan_kernel, span, len(others), b_rows, picks(b_pieces), c_rows, picks(c_pieces), c_begins
        ),
        in_specs=[IN_VMEM] * len(operands),
        out_specs=[IN_VMEM, IN_VMEM],
        out_shape=[pltpu.VMEM((length, width), BF16), pltpu.VMEM((length // SUB, SUB), F32)],
        scratch_shapes=[
            pltpu.VMEM((size, width), F32),
            pltpu.VMEM((TILE, size), BF16),
            pltpu.VMEM((TILE, SUB), F32),
            pltpu.VMEM((TILE, width), F32),
            pltpu.VMEM((TILE, SUB), BF16),
        ],
        input_output_aliases={first + i: i for i in range(len(filled))},
        compiler_params=params(),
        cost_estimate=BRIEF,
        name="scan",
    )(*in_vmem(operands))


def norm_kernel(channels, gated_ref, gain_ref, *refs):
    squares, (out_ref, rows, sems) = refs[:-3], refs[-3:]
    total = squares[0][...]
    for ref in squares[1:]:
        total = total + ref[...]
    scale = lax.rsqrt(total * (1.0 / channels) + 1e-05).T
    gain = gain_ref[...]
    step = 2 * SUB
    copies = []
    for t in range(gated_ref.shape[0] // step):
        for s in range(t * step // SUB, (t + 1) * step // SUB):
            at = slice(s * SUB, (s + 1) * SUB)
            wide = jnp.broadcast_to(scale[:, s : s + 1], (SUB, SUB))
            for p in range(gated_ref.shape[1] // SUB):
                cols = slice(p * SUB, (p + 1) * SUB)
                rows[at, cols] = (gated_ref[at, cols].astype(F32) * wide * gain[:, cols]).astype(BF16)
        at = slice(t * step, (t + 1) * step)
        copies.append(pltpu.make_async_copy(rows.at[at], out_ref.at[at], sems.at[t]))
        copies[-1].start()
    for copy in copies:
        copy.wait()


def norm(channels, gated, gain, squares):
    length, width = gated.shape
    operands = [gated, gain, *squares]
    return pl.pallas_call(
        functools.partial(norm_kernel, channels),
        in_specs=[IN_VMEM] * len(operands),
        out_specs=ANYWHERE,
        out_shape=pltpu.HBM((length, width), BF16),
        scratch_shapes=[
            pltpu.VMEM((length, width), BF16),
            pltpu.SemaphoreType.DMA((length // (2 * SUB),)),
        ],
        compiler_params=params(),
        cost_estimate=BRIEF,
        name="norm",
    )(*in_vmem(operands))


def body(x_rows, z_rows, b_rows, c_rows, step_raw, conv_x, conv_b, conv_c, decay_rate, norm_gain):
    length, width = x_rows.shape
    local_heads = decay_rate.shape[0]
    seq, heads = lax.axis_size("seq"), lax.axis_size("head")
    b_cols, c_cols = b_rows.T, c_rows.T
    ends, b_cols, c_cols = tails(x_rows, b_cols, c_cols)
    halo = lax.ppermute(ends, "seq", [(i, i + 1) for i in range(seq - 1)])
    bs, cs, cs_sent = shared_conv(b_cols, c_cols, halo, conv_b.T.astype(F32), conv_c.T.astype(F32))
    cols = bs.shape[0]
    outer, _ = factors(heads)
    tiles = x_rows.shape[0] // TILE
    q, columns, decays = rows_of(step_raw.T, decay_rate[:, None], width)
    conv = functools.partial(head_conv, x_rows, halo, conv_x.astype(F32), columns, local_heads)
    if cols % 16 or factors(heads) != (4, 2):
        b_pieces, c_pieces = [
            [jnp.concatenate(near + along_inner(near), axis=0)]
            for near in ([own] + along_outer(own) for own in (bs, cs))
        ]
        b_rows = c_rows = [(0, b_pieces[0].shape[0])]
        xs, weighted = conv(0, tiles)
        mine, local, before = last_state(weighted, decays, b_pieces, b_rows)
        gate, factor, start = gates(z_rows, columns, q, local_heads)
        token, tail, runs = mine, [], [((0, tiles), None, None)]
    else:
        one = (0, cols)
        b_outer, own, c_own = along_outer(bs), along_inner([bs]), along_inner([cs])
        xs, weighted = conv(0, tiles)
        (b_packed,) = pack(b_outer, [one] * 3, xs, *own, *c_own)
        b_passed = along_inner([b_packed])
        cs_sent, columns = after([cs_sent, columns], b_packed)
        c_outer = along_outer(cs_sent)
        gate, factor, start = gates(z_rows, columns, q, local_heads)
        c_outer[:1] = after(c_outer[:1], start)
        c_passed = c_own + along_inner(c_outer[:1])
        (decays,) = after([decays], c_outer[0])
        b_pieces = [bs, *own, *b_outer, *b_passed]
        b_rows = [one] * 5 + [(0, 3 * cols)]
        mine, local, before = last_state(weighted, decays, b_pieces, b_rows)
        cut = -(-tiles // 2) * TILE
        c_rest = pack(c_outer[:0:-1], [one] * 2, mine, c_passed[1], cuts=[0, cut, length])
        c_ends = along_inner(c_rest)
        c_pieces = [cs, *c_own, *c_outer, c_passed[1]]
        c_rows = [one] * 6
        token, tail = c_rest[0], [(cols, 2 * cols), one]
        runs = [((0, cut // TILE), c_ends[0], 0), ((cut // TILE, tiles), c_ends[1], cut)]
    others, bit = [], 1
    while bit < seq:
        last = 2 * bit == seq
        pairs = [(i, i ^ bit) for i in range(seq) if not (last and i & bit)]
        others.append(lax.ppermute(mine, "seq", pairs))
        if not last:
            mine = join(bit, mine, others[-1], token)
        bit *= 2
    filled = ()
    for span, piece, begin in runs:
        filled = scan(
            span, gate, factor, start, xs, local, before, others, b_pieces, b_rows,
            c_pieces + [piece] * len(tail), c_rows + tail, [0] * len(c_pieces) + [begin] * len(tail), filled,
        )
    gated, square = filled
    square = square + sum(along_outer(square))
    squares = [square] + along_inner([square])
    return norm(heads * width, gated, norm_gain[None, :], squares)


def solution(mesh):
    placed = (
        P("seq", "head"),
        P("seq", "head"),
        P("seq", "head"),
        P("seq", "head"),
        P("seq", "head"),
        P(None, "head"),
        P(None, "head"),
        P(None, "head"),
        P("head"),
        P("head"),
    )
    return jax.shard_map(
        body, mesh=mesh, in_specs=placed, out_specs=P("seq", "head"), check_vma=False
    )
```
